32 devices in a mesh: dp: 8 (over y, x, core), mp: 4 (over z).
Axes of the slice: x: 2, y: 2, z: 4, core: 2. Of those that a mesh axis runs over, the one named last changes fastest.
Arguments:
- inputs: bfloat16 [16384, 1024], P(('dp', 'mp')), may hold values from -6 to 6
- lengths: int32 [16], replicated, may hold values from 0 to 4096, as said below
- attention_gain_one: bfloat16 [1024], P('dp'), may hold values from 0.25 to 1.75
- query_weight_one: bfloat16 [1024, 1024], P('dp', 'mp'), may hold values from -0.1875 to 0.1875
- key_weight_one: bfloat16 [1024, 1024], P('dp', 'mp'), may hold values from -0.1875 to 0.1875
- value_weight_one: bfloat16 [1024, 1024], P('dp', 'mp'), may hold values from -0.1875 to 0.1875
- output_weight_one: bfloat16 [1024, 1024], P('mp', 'dp'), may hold values from -1.5 to 1.5
- feedforward_gain_one: bfloat16 [1024], P('dp'), may hold values from 0.25 to 1.75
- gate_weight_one: bfloat16 [1024, 2816], P('dp', 'mp'), may hold values from -0.1875 to 0.1875
- up_weight_one: bfloat16 [1024, 2816], P('dp', 'mp'), may hold values from -0.1875 to 0.1875
- down_weight_one: bfloat16 [2816, 1024], P('mp', 'dp'), may hold values from -0.109375 to 0.109375
- attention_gain_two: bfloat16 [1024], P('dp'), may hold values from 0.25 to 1.75
- query_weight_two: bfloat16 [1024, 1024], P('dp', 'mp'), may hold values from -0.1875 to 0.1875
- key_weight_two: bfloat16 [1024, 1024], P('dp', 'mp'), may hold values from -0.1875 to 0.1875
- value_weight_two: bfloat16 [1024, 1024], P('dp', 'mp'), may hold values from -0.1875 to 0.1875
- output_weight_two: bfloat16 [1024, 1024], P('mp', 'dp'), may hold values from -1.5 to 1.5
- feedforward_gain_two: bfloat16 [1024], P('dp'), may hold values from 0.25 to 1.75
- gate_weight_two: bfloat16 [1024, 2816], P('dp', 'mp'), may hold values from -0.1875 to 0.1875
- up_weight_two: bfloat16 [1024, 2816], P('dp', 'mp'), may hold values from -0.1875 to 0.1875
- down_weight_two: bfloat16 [2816, 1024], P('mp', 'dp'), may hold values from -0.109375 to 0.109375
- cotangent: bfloat16 [16384, 1024], P(('dp', 'mp')), may hold values from -6 to 6
Outputs:
- first_output: bfloat16 [16384, 1024], P(('dp', 'mp'))
- second_output: bfloat16 [16384, 1024], P(('dp', 'mp'))
- input_grad: float32 [16384, 1024], P(('dp', 'mp'))
- grad_attention_gain_one: float32 [1024], P('dp')
- grad_query_one: float32 [1024, 1024], P('dp', 'mp')
- grad_key_one: float32 [1024, 1024], P('dp', 'mp')
- grad_value_one: float32 [1024, 1024], P('dp', 'mp')
- grad_output_one: float32 [1024, 1024], P('mp', 'dp')
- grad_feedforward_gain_one: float32 [1024], P('dp')
- grad_gate_one: float32 [1024, 2816], P('dp', 'mp')
- grad_up_one: float32 [1024, 2816], P('dp', 'mp')
- grad_down_one: float32 [2816, 1024], P('mp', 'dp')
- grad_attention_gain_two: float32 [1024], P('dp')
- grad_query_two: float32 [1024, 1024], P('dp', 'mp')
- grad_key_two: float32 [1024, 1024], P('dp', 'mp')
- grad_value_two: float32 [1024, 1024], P('dp', 'mp')
- grad_output_two: float32 [1024, 1024], P('mp', 'dp')
- grad_feedforward_gain_two: float32 [1024], P('dp')
- grad_gate_two: float32 [1024, 2816], P('dp', 'mp')
- grad_up_two: float32 [1024, 2816], P('dp', 'mp')
- grad_down_two: float32 [2816, 1024], P('mp', 'dp')
- value_norms: float32 [8, 2], P('dp')
The draws below stay inside these ranges and needn't reach their ends.
Inputs may be any that keep to these rules, and one draw needn't show every extreme that they name: `lengths`: each entry is 0, 1024, 2048 or 4096; the entries sum to 16384; every 0 comes after all nonzero entries; some entry equals 4096.
All inputs are finite; a program needn't handle non-finite values.
Results may differ from the reference program's by a relative error of at most 0.035.
Values may be sent and summed in bfloat16 or wider, within the bound.
A program may use at most 384 MiB of HBM per device.

```python
import math
import jax
import jax.numpy as jnp
from jax import lax

D = 1024
HEADS = 16
HEAD_DIM = 64
FF = 2816
TOK_DEV = 2048
TOKENS = 16384
LONGEST = 4096
QB = 512
SLOTS = 16
N_DP = 8


def draw_lengths(key, part):
    key = jax.random.fold_in(key, 7)
    pick_key, force_key = jax.random.split(key)
    pick_values = jax.random.randint(pick_key, (SLOTS,), 0, 3)
    unit_counts = jnp.where(pick_values == 0, 1, jnp.where(pick_values == 1, 2, 4)).astype(jnp.int32)
    forced = jax.random.randint(force_key, (), 0, 4)
    slot_index = jnp.arange(SLOTS)
    unit_counts = jnp.where(slot_index == forced, 4, unit_counts).astype(jnp.int32)

    def take_units(remaining, wanted):
        room_left = jnp.where(remaining >= 4, 4, jnp.where(remaining >= 2, 2, jnp.where(remaining >= 1, 1, 0)))
        taken = jnp.minimum(wanted, room_left).astype(jnp.int32)
        return ((remaining - taken).astype(jnp.int32), taken)
    remaining, taken = lax.scan(take_units, jnp.array(SLOTS, jnp.int32), unit_counts)
    return (taken * (TOK_DEV // 2)).astype(jnp.int32)


def block_scale(own_key, extent, cuts, low, high):
    factor_of = 1.0
    for axis_at, shards_of in cuts:
        heights = jax.random.uniform(jax.random.fold_in(jax.random.fold_in(own_key, 6), axis_at), (shards_of,), jnp.float32, low / len(cuts), high / len(cuts))
        factor_of = factor_of * jnp.repeat(jnp.exp(heights), extent[axis_at] // shards_of).reshape((-1,) + (1,) * (len(extent) - 1 - axis_at))
    return factor_of


def noise(key, dims, spread, bound, cuts=(), kind=jnp.bfloat16):
    level = block_scale(key, dims, cuts, -0.22, 0.18) if cuts else 1.0
    values = jax.random.normal(key, dims, jnp.float32) * spread * level
    return jnp.minimum(jnp.maximum(values, -bound), bound).astype(kind)


def setup_inputs(seed: int = 0) -> dict:
    splits = jax.random.split(jax.random.key(seed), 22)
    inputs = noise(splits[0], (TOKENS, D), 1.0, 6.0, ((0, 32),))
    lengths = draw_lengths(jax.random.fold_in(splits[21], 71), 0)
    attention_gain_one = jnp.clip(1.0 + 0.15 * jax.random.normal(splits[2], (D,), jnp.float32), 0.25, 1.75).astype(jnp.bfloat16)
    query_weight_one = noise(splits[3], (D, D), D ** -0.5, 0.1875, ((0, 8), (1, 4)))
    key_weight_one = noise(splits[4], (D, D), D ** -0.5, 0.1875, ((0, 8), (1, 4)))
    value_weight_one = noise(splits[5], (D, D), D ** -0.5, 0.1875, ((0, 8), (1, 4)))
    output_weight_one = noise(splits[6], (D, D), (D // 64) ** -0.5, 1.5, ((0, 4), (1, 8)))
    feedforward_gain_one = jnp.clip(1.0 + 0.15 * jax.random.normal(splits[7], (D,), jnp.float32), 0.25, 1.75).astype(jnp.bfloat16)
    gate_weight_one = noise(splits[8], (D, FF), D ** -0.5, 0.1875, ((0, 8), (1, 4)))
    up_weight_one = noise(splits[9], (D, FF), D ** -0.5, 0.1875, ((0, 8), (1, 4)))
    down_weight_one = noise(splits[10], (FF, D), FF ** -0.5, 0.109375, ((0, 4), (1, 8)))
    attention_gain_two = jnp.clip(1.0 + 0.15 * jax.random.normal(splits[11], (D,), jnp.float32), 0.25, 1.75).astype(jnp.bfloat16)
    query_weight_two = noise(splits[12], (D, D), D ** -0.5, 0.1875, ((0, 8), (1, 4)))
    key_weight_two = noise(splits[13], (D, D), D ** -0.5, 0.1875, ((0, 8), (1, 4)))
    value_weight_two = noise(splits[14], (D, D), D ** -0.5, 0.1875, ((0, 8), (1, 4)))
    output_weight_two = noise(splits[15], (D, D), (D // 64) ** -0.5, 1.5, ((0, 4), (1, 8)))
    feedforward_gain_two = jnp.clip(1.0 + 0.15 * jax.random.normal(splits[16], (D,), jnp.float32), 0.25, 1.75).astype(jnp.bfloat16)
    gate_weight_two = noise(splits[17], (D, FF), D ** -0.5, 0.1875, ((0, 8), (1, 4)))
    up_weight_two = noise(splits[18], (D, FF), D ** -0.5, 0.1875, ((0, 8), (1, 4)))
    down_weight_two = noise(splits[19], (FF, D), FF ** -0.5, 0.109375, ((0, 4), (1, 8)))
    cotangent = noise(splits[20], (TOKENS, D), 1.0, 6.0, ((0, 32),))
    return dict(inputs=inputs, lengths=lengths, attention_gain_one=attention_gain_one, query_weight_one=query_weight_one, key_weight_one=key_weight_one, value_weight_one=value_weight_one, output_weight_one=output_weight_one, feedforward_gain_one=feedforward_gain_one, gate_weight_one=gate_weight_one, up_weight_one=up_weight_one, down_weight_one=down_weight_one, attention_gain_two=attention_gain_two, query_weight_two=query_weight_two, key_weight_two=key_weight_two, value_weight_two=value_weight_two, output_weight_two=output_weight_two, feedforward_gain_two=feedforward_gain_two, gate_weight_two=gate_weight_two, up_weight_two=up_weight_two, down_weight_two=down_weight_two, cotangent=cotangent)


@jax.custom_vjp
def low(v):
    return lax.optimization_barrier(v.astype(jnp.bfloat16)).astype(jnp.float32)

@jax.custom_vjp
def low_back(v):
    return v

def low_keep(v):
    return (low(v), None)

def low_pass(kept, grad):
    return (grad,)

def back_keep(v):
    return (v, None)

def back_low(kept, grad):
    return (low(grad),)
low.defvjp(low_keep, low_pass)
low_back.defvjp(back_keep, back_low)
EPSILON = 1e-06
MASKED = -1e+30
HIGHEST = lax.Precision.HIGHEST

def matmul(left_side, right_side):
    return jnp.dot(left_side, right_side, precision=HIGHEST, preferred_element_type=jnp.float32)

def norm_rows(values, gain_vector):
    scaling = lax.rsqrt(lax.optimization_barrier(jnp.mean(values * values, axis=-1, keepdims=True)) + EPSILON)
    return values * scaling * gain_vector

def rotary(values, cosine, sine_table):
    half_dim = values.shape[-1] // 2
    leading = values[..., :half_dim]
    trailing = values[..., half_dim:]
    cosine = cosine[:, None, :]
    sine_table = sine_table[:, None, :]
    return jnp.concatenate([leading * cosine - trailing * sine_table, trailing * cosine + leading * sine_table], axis=-1)

def angles(position, head_size):
    half_dim = head_size // 2
    indices = jnp.arange(half_dim).astype(jnp.float32)
    frequency = jnp.exp(indices * (-2.0 * math.log(10000.0) / head_size))
    phases = position.astype(jnp.float32)[:, None] * frequency[None, :]
    return (jnp.cos(phases), jnp.sin(phases))

def locate(places, lengths):
    doc_ends = jnp.cumsum(lengths).astype(jnp.int32)
    passed = doc_ends[None, :] <= places[:, None]
    document = lax.optimization_barrier(jnp.sum(passed.astype(jnp.int32), axis=1)).astype(jnp.int32)
    document = jnp.where(places < 0, -1, document).astype(jnp.int32)
    opening = lax.optimization_barrier(jnp.max(jnp.where(passed, doc_ends[None, :], 0), axis=1)).astype(jnp.int32)
    return (document, (places - opening).astype(jnp.int32))

def attention(queries, key_rows, values, document):
    key_width = LONGEST + QB
    pad_keys = jnp.concatenate([jnp.zeros((LONGEST, HEADS, HEAD_DIM), jnp.float32), key_rows], axis=0)
    pad_values = jnp.concatenate([jnp.zeros((LONGEST, HEADS, HEAD_DIM), jnp.float32), values], axis=0)
    pad_docs = jnp.concatenate([jnp.full((LONGEST,), -1, jnp.int32), document]).astype(jnp.int32)
    scaling = HEAD_DIM ** (-0.5)

    def one_block(block_index):
        first_row = (block_index * QB).astype(jnp.int32)
        query_block = lax.dynamic_slice_in_dim(queries, first_row, QB, 0)
        key_block = lax.dynamic_slice_in_dim(pad_keys, first_row, key_width, 0)
        value_block = lax.dynamic_slice_in_dim(pad_values, first_row, key_width, 0)
        query_docs = lax.dynamic_slice_in_dim(document, first_row, QB, 0)
        key_docs = lax.dynamic_slice_in_dim(pad_docs, first_row, key_width, 0)
        query_place = jnp.arange(QB).astype(jnp.int32) + LONGEST
        key_place = jnp.arange(key_width).astype(jnp.int32)
        allowed = (query_docs[:, None] == key_docs[None, :]) & (key_place[None, :] <= query_place[:, None])
        scores = low_back(jnp.einsum('qhd,khd->hqk', query_block, key_block, precision=HIGHEST) * scaling)
        scores = jnp.where(allowed[None], scores, MASKED)
        weights = jax.nn.softmax(scores, axis=-1)
        return jnp.einsum('hqk,khd->qhd', low(weights), value_block, precision=HIGHEST)
    blocks = lax.map(jax.checkpoint(one_block), jnp.arange(TOKENS // QB).astype(jnp.int32))
    return blocks.reshape(TOKENS, HEADS * HEAD_DIM)

def decoder_layer(stream, weights, cosine, sine_table, document, first_values):
    attention_gain, query_weight, key_weight, value_weight, output_weight, feedforward_gain, gate_weight, up_weight, down_weight = weights
    normed = low(norm_rows(stream, attention_gain))
    queries = low(rotary(low_back(matmul(normed, query_weight)).reshape(TOKENS, HEADS, HEAD_DIM), cosine, sine_table))
    key_rows = low(rotary(low_back(matmul(normed, key_weight)).reshape(TOKENS, HEADS, HEAD_DIM), cosine, sine_table))
    fresh_values = matmul(normed, value_weight)
    if first_values is None:
        values = low(low_back(fresh_values))
    else:
        values = low(low_back(0.5 * fresh_values + 0.5 * first_values))
    mixed_heads = attention(queries, key_rows, values.reshape(TOKENS, HEADS, HEAD_DIM), document)
    mixed_heads = low(low_back(mixed_heads))
    stream = stream + low_back(matmul(mixed_heads, output_weight))
    normed_ff = low(norm_rows(stream, feedforward_gain))
    gate_pre = low_back(matmul(normed_ff, gate_weight))
    upward = low_back(matmul(normed_ff, up_weight))
    hidden = low(jax.nn.silu(gate_pre) * upward)
    stream = stream + low_back(matmul(hidden, down_weight))
    return (stream, values)

def group_rms(values):
    grouped = values.reshape(N_DP, TOK_DEV * D)
    return jnp.sqrt(lax.optimization_barrier(jnp.mean(grouped * grouped, axis=1)))

def reference(inputs, lengths, attention_gain_one, query_weight_one, key_weight_one, value_weight_one, output_weight_one, feedforward_gain_one, gate_weight_one, up_weight_one, down_weight_one, attention_gain_two, query_weight_two, key_weight_two, value_weight_two, output_weight_two, feedforward_gain_two, gate_weight_two, up_weight_two, down_weight_two, cotangent):
    places = jnp.arange(TOKENS).astype(jnp.int32)
    document, position = locate(places, lengths)
    cosine, sine_table = angles(position, HEAD_DIM)
    first_set = tuple((weight_array.astype(jnp.float32) for weight_array in (attention_gain_one, query_weight_one, key_weight_one, value_weight_one, output_weight_one, feedforward_gain_one, gate_weight_one, up_weight_one, down_weight_one)))
    second_set = tuple((weight_array.astype(jnp.float32) for weight_array in (attention_gain_two, query_weight_two, key_weight_two, value_weight_two, output_weight_two, feedforward_gain_two, gate_weight_two, up_weight_two, down_weight_two)))

    def forward(stream, first_weights, second_weights):
        middle_stream, first_values = decoder_layer(stream, first_weights, cosine, sine_table, document, None)
        final_stream, second_values = decoder_layer(middle_stream, second_weights, cosine, sine_table, document, first_values)
        return (final_stream, (middle_stream, first_values, second_values))
    final_stream, pullback, kept = jax.vjp(forward, inputs.astype(jnp.float32), first_set, second_set, has_aux=True)
    middle_stream, first_values, second_values = kept
    input_grad, first_grads, second_grads = pullback(cotangent.astype(jnp.float32))
    value_norms = jnp.stack([group_rms(first_values), group_rms(second_values)], axis=1)
    return (middle_stream.astype(jnp.bfloat16), final_stream.astype(jnp.bfloat16), input_grad, first_grads[0], first_grads[1], first_grads[2], first_grads[3], first_grads[4], first_grads[5], first_grads[6], first_grads[7], first_grads[8], second_grads[0], second_grads[1], second_grads[2], second_grads[3], second_grads[4], second_grads[5], second_grads[6], second_grads[7], second_grads[8], value_norms)
```

```python
import functools
import math

import jax
import jax.numpy as jnp
from jax import lax
from jax.experimental import pallas as pl
from jax.experimental.pallas import tpu as pltpu
from jax.sharding import PartitionSpec as P

D = 1024
HEAD_DIM = 64
TOK_DEV = 2048
LONGEST = 4096

LANES = 128
HEADS_HELD = LANES // HEAD_DIM
CHUNK = 1024
HALO = LONGEST - CHUNK
QUERY_ROWS = 512
EPSILON = 1e-06
MASKED = -1e30
LOG2E = math.log2(math.e)
MESH = pl.DeviceIdType.MESH
ANY = pl.BlockSpec(memory_space=pl.ANY)
VMEM = pl.BlockSpec(memory_space=pltpu.VMEM)
SMEM = pl.BlockSpec(memory_space=pltpu.SMEM)
BIG_VMEM = 56 * 1024 * 1024


def nn(left_side, right_side):
    return jnp.dot(left_side, right_side, preferred_element_type=jnp.float32)


def tn(left_side, right_side):
    return lax.dot_general(
        left_side, right_side, (((0,), (0,)), ((), ())), preferred_element_type=jnp.float32
    )


def nt(left_side, right_side):
    return lax.dot_general(
        left_side, right_side, (((1,), (1,)), ((), ())), preferred_element_type=jnp.float32
    )


def norm_rows(values, gain_vector):
    scaling = lax.rsqrt(jnp.mean(values * values, axis=-1, keepdims=True) + EPSILON)
    return values * scaling * gain_vector


def norm_back(values, gain_vector, grad_output):
    unused, pullback = jax.vjp(norm_rows, values, gain_vector)
    return pullback(grad_output)


class Plan:
    def __init__(self, n, m):
        self.n, self.m = n, m
        self.group = D // LANES
        self.low = self.group // m
        self.segments = n // self.low
        self.rows = TOK_DEV // m
        self.seg_rows = self.rows * self.group
        self.spans = []
        left, distance = HALO, 1
        while left > 0:
            count = min(self.seg_rows, left)
            self.spans.append((distance, left - count, count))
            left -= count
            distance += 1

    def here(self):
        dp, mp = lax.axis_index("dp"), lax.axis_index("mp")
        return dp // self.low, (dp % self.low) * self.m + mp

    def device(self, segment, member):
        return (segment * self.low + member // self.m, member % self.m)


def greet(plan, segment, member):
    barrier = pltpu.get_barrier_semaphore()
    for offset in range(1, plan.group):
        peer = lax.rem(member + offset, plan.group)
        pl.semaphore_signal(
            barrier, inc=1, device_id=plan.device(segment, peer), device_id_type=MESH
        )
    pl.semaphore_wait(barrier, plan.group - 1)


def member_copies(plan, segment, member, source, target, send, recv, own):
    copies = [pltpu.make_async_copy(source(member), target, own)]
    for offset in range(1, plan.group):
        peer = lax.rem(member + offset, plan.group)
        copies.append(
            pltpu.make_async_remote_copy(
                src_ref=source(peer),
                dst_ref=target,
                send_sem=send.at[offset],
                recv_sem=recv.at[offset],
                device_id=plan.device(segment, peer),
                device_id_type=MESH,
            )
        )
    for copy in copies[1:] + copies[:1]:
        copy.start()
    return copies


def columns(index):
    return pl.ds(pl.multiple_of(index * LANES, LANES), LANES)


def spread_kernel(plan, query, key, value, q_seg, k_seg, v_seg, send, recv, own):
    segment, member = plan.here()
    rows = plan.rows
    greet(plan, segment, member)
    copies = []
    place = pl.ds(pl.multiple_of(member * rows, rows), rows)
    for part, (array, out) in enumerate(((key, k_seg), (value, v_seg), (query, q_seg))):

        def source(peer, array=array):
            return array.at[:, columns(peer)]

        copies += member_copies(
            plan, segment, member, source, out.at[place], send.at[part], recv.at[part], own.at[part]
        )
    for copy in copies:
        copy.wait()


def spread(plan, query, key, value):
    segment = jax.ShapeDtypeStruct((plan.seg_rows, LANES), jnp.bfloat16)
    return pl.pallas_call(
        functools.partial(spread_kernel, plan),
        out_shape=(segment,) * 3,
        in_specs=[ANY] * 3,
        out_specs=(ANY, ANY, ANY),
        scratch_shapes=[
            pltpu.SemaphoreType.DMA((3, plan.group)),
            pltpu.SemaphoreType.DMA((3, plan.group)),
            pltpu.SemaphoreType.DMA((3,)),
        ],
        compiler_params=pltpu.CompilerParams(collective_id=1, has_side_effects=True),
        cost_estimate=pl.CostEstimate(flops=0, bytes_accessed=200_000_000, transcendentals=0),
        name="spread",
    )(query, key, value)


def halo_of(plan, seg):
    parts = []
    for distance, first, count in reversed(plan.spans):
        route = [(i, i + distance * plan.low) for i in range(plan.n - distance * plan.low)]
        parts.append(lax.ppermute(seg[plan.seg_rows - count :], "dp", route))
    return parts[0] if len(parts) == 1 else jnp.concatenate(parts, axis=0)


def halo_back(plan, halo):
    parts = []
    for distance, first, count in plan.spans:
        route = [(i, i - distance * plan.low) for i in range(distance * plan.low, plan.n)]
        parts.append(lax.ppermute(halo[first : first + count], "dp", route))
    return parts


def to_rows_kernel(plan, seg, rows_out, send, recv, own):
    segment, member = plan.here()
    rows = plan.rows
    greet(plan, segment, member)

    def source(peer):
        return seg.at[pl.ds(pl.multiple_of(peer * rows, rows), rows)]

    for copy in member_copies(
        plan, segment, member, source, rows_out.at[:, columns(member)], send, recv, own
    ):
        copy.wait()


def to_rows(plan, seg):
    return pl.pallas_call(
        functools.partial(to_rows_kernel, plan),
        out_shape=jax.ShapeDtypeStruct((plan.rows, D), jnp.bfloat16),
        in_specs=[ANY],
        out_specs=ANY,
        scratch_shapes=[
            pltpu.SemaphoreType.DMA((plan.group,)),
            pltpu.SemaphoreType.DMA((plan.group,)),
            pltpu.SemaphoreType.DMA,
        ],
        compiler_params=pltpu.CompilerParams(collective_id=2, has_side_effects=True),
        cost_estimate=pl.CostEstimate(flops=0, bytes_accessed=80_000_000, transcendentals=0),
        name="to_rows",
    )(seg)


def dp_place():
    dp = lax.axis_index("dp")
    return dp, dp % 2, (dp // 2) % 2, dp // 4


def greet_all(plan, dp, mp):
    barrier = pltpu.get_barrier_semaphore()
    others = [(dp, lax.rem(mp + k, plan.m)) for k in range(1, plan.m)]
    others += [(lax.rem(dp + k, plan.n), mp) for k in range(1, plan.n)]
    for other in others:
        pl.semaphore_signal(barrier, inc=1, device_id=other, device_id_type=MESH)
    pl.semaphore_wait(barrier, len(others))


def remote(source, target, send, recv, device):
    copy = pltpu.make_async_remote_copy(
        src_ref=source,
        dst_ref=target,
        send_sem=send,
        recv_sem=recv,
        device_id=device,
        device_id_type=MESH,
    )
    copy.start()
    return copy


def weave_kernel(plan, shard, gain, out, gain_out, own, *sems):
    z_send, z_recv, x_send, x_recv, y_send, y_recv, c_send, c_recv, g_send, g_recv = sems
    (dp, core, x, y), mp = dp_place(), lax.axis_index("mp")
    types, rows = shard.shape[:2]
    half = types // 2
    greet_all(plan, dp, mp)
    beside = dp + 1 - 2 * core
    dp_x, dp_y = dp + 2 - 4 * x, dp + 4 - 8 * y
    dp_xy = dp_x + 4 - 8 * y

    def block(index, column, first=0, count=types):
        z = lax.rem(mp + plan.m - index, plan.m)
        place = pl.ds(pl.multiple_of(z * rows, rows), rows)
        return out.at[pl.ds(first, count), place, columns(column)]

    def pass_on(index, column, sems, slot, device, first=0, count=types):
        region = block(index, column, first, count)
        return remote(
            region, region, sems[0].at[index, slot], sems[1].at[index, slot], (device, mp)
        )

    locals_ = [
        pltpu.make_async_copy(shard, block(0, dp), own.at[0]),
        pltpu.make_async_copy(gain, gain_out.at[:, columns(dp)], own.at[1]),
    ]
    for copy in locals_:
        copy.start()
    z_copies = [None]
    for k in range(1, plan.m):
        z_copies.append(
            remote(shard, block(0, dp), z_send.at[k], z_recv.at[k], (dp, lax.rem(mp + k, plan.m)))
        )
    copies = [
        remote(
            gain,
            gain_out.at[:, columns(dp)],
            g_send.at[k],
            g_recv.at[k],
            (lax.rem(dp + k, plan.n), mp),
        )
        for k in range(1, plan.n)
    ]
    x_sems, y_sems, c_sems = (x_send, x_recv), (y_send, y_recv), (c_send, c_recv)
    x_own, y_own, x_far, y_far, c_all = [], [], [], [], []

    def first_stage(index):
        if index == 0:
            for copy in locals_:
                copy.wait()
        else:
            z_copies[index].wait_recv()
        x_own.append(pass_on(index, dp, x_sems, 0, dp_x))
        y_own.append(pass_on(index, dp, y_sems, 0, dp_y))
        c_all.append(pass_on(index, dp, c_sems, 0, beside))

    def second_stage(index):
        x_own[index].wait_recv()
        y_far.append(pass_on(index, dp_x, y_sems, 1, dp_y, 0, half))
        c_all.append(pass_on(index, dp_x, c_sems, 1, beside))
        y_own[index].wait_recv()
        x_far.append(pass_on(index, dp_y, x_sems, 1, dp_x, half, types - half))
        c_all.append(pass_on(index, dp_y, c_sems, 2, beside))

    def third_stage(index):
        y_far[index].wait_recv()
        c_all.append(pass_on(index, dp_xy, c_sems, 3, beside, 0, half))
        x_far[index].wait_recv()
        c_all.append(pass_on(index, dp_xy, c_sems, 4, beside, half, types - half))

    for step in range(plan.m + 2):
        if step < plan.m:
            first_stage(step)
        if 1 <= step < plan.m + 1:
            second_stage(step - 1)
        if step >= 2:
            third_stage(step - 2)
    for copy in copies + c_all:
        copy.wait()
    for copy in z_copies[1:] + x_own + y_own + x_far + y_far:
        copy.wait_send()


def weave(plan, shard, gain):
    types, rows = shard.shape[:2]
    dma = pltpu.SemaphoreType.DMA
    return pl.pallas_call(
        functools.partial(weave_kernel, plan),
        in_specs=[ANY, ANY],
        out_specs=(ANY, ANY),
        out_shape=(
            jax.ShapeDtypeStruct((types, plan.m * rows, D), jnp.bfloat16),
            jax.ShapeDtypeStruct((gain.shape[0], D), jnp.bfloat16),
        ),
        scratch_shapes=[dma((2,))]
        + [dma((plan.m,))] * 2
        + [dma((plan.m, 2))] * 4
        + [dma((plan.m, 5))] * 2
        + [dma((plan.n,))] * 2,
        compiler_params=pltpu.CompilerParams(collective_id=6, has_side_effects=True),
        cost_estimate=pl.CostEstimate(flops=0, bytes_accessed=150_000_000, transcendentals=0),
        name="weave",
    )(shard, gain)


def shed_kernel(plan, normed, dq, dk, dv, extra, out, left, parts, from_core, sums, *rest):
    from_first, sums_first, from_second, blocks, from_z, c_sems, f_sems, s_sems, z_sems = rest
    (dp, core, x, y), mp = dp_place(), lax.axis_index("mp")
    width = D // plan.n
    wide = D // 2
    greet_all(plan, dp, mp)
    beside, dp_x, dp_y = dp + 1 - 2 * core, dp + 2 - 4 * x, dp + 4 - 8 * y

    def rows_of(index):
        return pl.ds(pl.multiple_of(index * width, width), width)

    def plus(one, other):
        return (one.astype(jnp.float32) + other.astype(jnp.float32)).astype(jnp.bfloat16)

    left[...] = normed[...].T
    c_copies, first, second = [], [], []
    for half in range(2):
        for kind, array in enumerate((dq, dk, dv)):
            place = slice(kind * wide, (kind + 1) * wide)
            source = slice(half * wide, (half + 1) * wide)
            parts[half, :, place] = nn(left[...], array[:, source]).astype(jnp.bfloat16)
        parts[half, :, 3 * wide :] = extra[...].astype(jnp.bfloat16)
        c_copies.append(
            [
                remote(
                    parts.at[half, rows_of(2 * j + 1 - core)],
                    from_core.at[half, j],
                    c_sems.at[0, half, j],
                    c_sems.at[1, half, j],
                    (beside, mp),
                )
                for j in range(4)
            ]
        )
    for half in range(2):
        for j in range(4):
            c_copies[half][j].wait_recv()
            sums[half, j] = plus(parts[half, rows_of(2 * j + core), :], from_core[half, j])
        for k in range(2):
            away = 2 * k + 1 - x if half == 0 else 2 * (1 - y) + k
            first.append(
                remote(
                    sums.at[half, away],
                    from_first.at[half, k],
                    f_sems.at[0, half, k],
                    f_sems.at[1, half, k],
                    (dp_x if half == 0 else dp_y, mp),
                )
            )
    for half in range(2):
        for k in range(2):
            first[2 * half + k].wait_recv()
            kept = 2 * k + x if half == 0 else 2 * y + k
            sums_first[half, k] = plus(sums[half, kept], from_first[half, k])
        second.append(
            remote(
                sums_first.at[half, 1 - y if half == 0 else 1 - x],
                from_second.at[half],
                s_sems.at[0, half],
                s_sems.at[1, half],
                (dp_y if half == 0 else dp_x, mp),
            )
        )
    piece = D // plan.m
    for half in range(2):
        second[half].wait_recv()
        total = plus(sums_first[half, y if half == 0 else x], from_second[half])
        for member in range(2):
            index = 2 * half + member
            for kind in range(3):
                start = kind * wide + member * piece
                blocks[index, :, kind * piece : (kind + 1) * piece] = total[:, start : start + piece]
            blocks[index, :, 3 * piece :] = total[:, 3 * wide :]
    z_copies = []
    for k in range(1, plan.m):
        peer = lax.rem(mp + k, plan.m)
        z_copies.append(
            remote(
                blocks.at[peer], from_z.at[k], z_sems.at[0, k], z_sems.at[1, k], (dp, peer)
            )
        )
    result = blocks[mp].astype(jnp.float32)
    for k in range(1, plan.m):
        z_copies[k - 1].wait_recv()
        result = result + from_z[k].astype(jnp.float32)
    out[...] = result
    for copy in c_copies[0] + c_copies[1] + first + second + z_copies:
        copy.wait_send()


def shed(plan, normed, dqkv, extra):
    dma = pltpu.SemaphoreType.DMA
    width, wide, kept = D // plan.n, 3 * (D // 2) + LANES, 3 * (D // plan.m) + LANES

    def held(*shape):
        return pltpu.VMEM(shape, jnp.bfloat16)

    return pl.pallas_call(
        functools.partial(shed_kernel, plan),
        in_specs=[VMEM] * 5,
        out_specs=VMEM,
        out_shape=jax.ShapeDtypeStruct((width, kept), jnp.float32),
        scratch_shapes=[
            held(D, normed.shape[0]),
            held(2, D, wide),
            held(2, 4, width, wide),
            held(2, 4, width, wide),
            held(2, 2, width, wide),
            held(2, 2, width, wide),
            held(2, width, wide),
            held(plan.m, width, kept),
            held(plan.m, width, kept),
            dma((2, 2, 4)),
            dma((2, 2, 2)),
            dma((2, 2)),
            dma((2, plan.m)),
        ],
        compiler_params=pltpu.CompilerParams(
            collective_id=7, has_side_effects=True, vmem_limit_bytes=BIG_VMEM
        ),
        cost_estimate=pl.CostEstimate(
            flops=4_000_000_000, bytes_accessed=200_000_000, transcendentals=0
        ),
        name="shed",
    )(normed, *dqkv, extra)


def products_kernel(plan, sides, *refs):
    rows_in, refs = refs[0], refs[1:]
    lefts, rights = refs[: len(set(sides))], refs[len(set(sides)) : len(set(sides)) + len(sides)]
    seg, out, left_sides, tiles, send, recv, own, sent = refs[len(lefts) + len(rights) :]
    segment, member = plan.here()
    rows = plan.rows
    greet(plan, segment, member)

    def source(peer):
        return rows_in.at[:, columns(peer)]

    place = seg.at[pl.ds(pl.multiple_of(member * rows, rows), rows)]
    copies = member_copies(plan, segment, member, source, place, send, recv, own)
    for index, array in enumerate(lefts):
        left_sides[index] = array[...].T
    start, pending = 0, [None, None]
    slot = 0
    for array, side in zip(rights, sides):
        size = array.shape[1]
        width = size // 2 if size % (2 * LANES) == 0 and size > D else D
        for first in range(0, size, width):
            if pending[slot] is not None:
                pending[slot].wait()
            tiles[slot, :, :width] = nn(
                left_sides[side], array[:, first : first + width]
            ).astype(jnp.bfloat16)
            pending[slot] = pltpu.make_async_copy(
                tiles.at[slot, :, :width], out.at[:, pl.ds(start, width)], sent.at[slot]
            )
            pending[slot].start()
            start += width
            slot = 1 - slot
    for copy in pending + copies:
        copy.wait()


def products(plan, rows_in, lefts, rights, sides):
    rows, widest = lefts[0].shape[0], max(array.shape[1] for array in rights) // 2
    total = sum(array.shape[1] for array in rights)
    return pl.pallas_call(
        functools.partial(products_kernel, plan, sides),
        in_specs=[ANY] + [VMEM] * (len(lefts) + len(rights)),
        out_specs=(ANY, ANY),
        out_shape=(
            jax.ShapeDtypeStruct((plan.seg_rows, LANES), jnp.bfloat16),
            jax.ShapeDtypeStruct((D, total), jnp.bfloat16),
        ),
        scratch_shapes=[
            pltpu.VMEM((len(lefts), D, rows), jnp.bfloat16),
            pltpu.VMEM((2, D, widest), jnp.bfloat16),
            pltpu.SemaphoreType.DMA((plan.group,)),
            pltpu.SemaphoreType.DMA((plan.group,)),
            pltpu.SemaphoreType.DMA,
            pltpu.SemaphoreType.DMA((2,)),
        ],
        compiler_params=pltpu.CompilerParams(
            collective_id=len(lefts), has_side_effects=True, vmem_limit_bytes=BIG_VMEM
        ),
        cost_estimate=pl.CostEstimate(
            flops=20_000_000_000, bytes_accessed=80_000_000, transcendentals=0
        ),
        name="products",
    )(rows_in, *lefts, *rights)


def collect_kernel(plan, spans, *refs):
    parts = 1 if spans == 0 else 2
    arrays, halos = refs[:parts], refs[parts : parts * (1 + spans)]
    outs, refs = refs[parts * (1 + spans) : parts * (2 + spans)], refs[parts * (2 + spans) :]
    total, send, recv, own = refs
    segment, member = plan.here()
    rows = plan.rows
    greet(plan, segment, member)
    copies = []
    for part, array in enumerate(arrays):
        if spans:
            for piece in range(plan.seg_rows // CHUNK):
                start = piece * CHUNK
                value = array[pl.ds(start, CHUNK), :]
                for index, (distance, first, count) in enumerate(plan.spans):
                    offset = start - (plan.seg_rows - count)
                    if offset >= 0:
                        halo = halos[part * spans + index][pl.ds(offset, CHUNK), :]
                        value = value + halo.astype(jnp.float32)
                total[part, pl.ds(start, CHUNK), :] = value.astype(jnp.bfloat16)
            array = total.at[part]

        def source(peer, array=array):
            return array.at[pl.ds(pl.multiple_of(peer * rows, rows), rows)]

        copies += member_copies(
            plan,
            segment,
            member,
            source,
            outs[part].at[:, columns(member)],
            send.at[part],
            recv.at[part],
            own.at[part],
        )
    for copy in copies:
        copy.wait()


def collect(plan, arrays, halos):
    parts, spans = len(arrays), len(plan.spans) if halos else 0
    return pl.pallas_call(
        functools.partial(collect_kernel, plan, spans),
        out_shape=(jax.ShapeDtypeStruct((plan.rows, D), jnp.bfloat16),) * parts,
        in_specs=[VMEM] * (parts + len(halos)),
        out_specs=(ANY,) * parts,
        scratch_shapes=[
            pltpu.VMEM((parts, plan.seg_rows if halos else 16, LANES), jnp.bfloat16),
            pltpu.SemaphoreType.DMA((parts, plan.group)),
            pltpu.SemaphoreType.DMA((parts, plan.group)),
            pltpu.SemaphoreType.DMA((parts,)),
        ],
        compiler_params=pltpu.CompilerParams(
            collective_id=5 if halos else 8, has_side_effects=True, vmem_limit_bytes=BIG_VMEM
        ),
        cost_estimate=pl.CostEstimate(
            flops=0, bytes_accessed=160_000_000 if halos else 1_000, transcendentals=0
        ),
        name="collect_kv" if halos else "collect_q",
    )(*arrays, *halos)


def swap_halves(values):
    lane = lax.broadcasted_iota(jnp.int32, values.shape, 1)
    half = HEAD_DIM // 2
    ahead = pltpu.roll(values, LANES - half, 1)
    behind = pltpu.roll(values, half, 1)
    return jnp.where(lax.rem(lane, HEAD_DIM) < half, ahead, behind)


def rotate(values, cosine, sine):
    return values * cosine + swap_halves(values) * sine


def of_head(values, head):
    lane = lax.broadcasted_iota(jnp.int32, values.shape, 1)
    return jnp.where(lane // HEAD_DIM == head, values, jnp.zeros_like(values))


def chunk_rows(index, size):
    return pl.ds(pl.multiple_of(index * size, size), size)


HALO_CHUNKS = HALO // CHUNK
PER_CHUNK = CHUNK // QUERY_ROWS


def rotate_keys(prior, first, keys, cosine, sine, k_turned):
    def one(index, unused):
        table = chunk_rows(prior[first + index], CHUNK)
        rows = chunk_rows(index, CHUNK)
        k_turned[rows, :] = rotate(
            keys[rows, :].astype(jnp.float32), cosine[table, :], sine[table, :]
        ).astype(jnp.bfloat16)
        return unused

    lax.fori_loop(0, keys.shape[0] // CHUNK, one, 0)


def query_tables(prior, block, cosine, sine):
    chunk = block // PER_CHUNK
    start = prior[HALO_CHUNKS + chunk] * PER_CHUNK + lax.rem(block, PER_CHUNK)
    rows = chunk_rows(start, QUERY_ROWS)
    return cosine[rows, :], sine[rows, :]


def turned_queries(prior, block, queries, cosine, sine):
    cos_rows, sin_rows = query_tables(prior, block, cosine, sine)
    turned = rotate(queries.astype(jnp.float32), cos_rows, sin_rows)
    return (turned * (LOG2E * HEAD_DIM ** (-0.5))).astype(jnp.bfloat16)


def by_head(parts):
    whole = parts[0]
    lane = lax.broadcasted_iota(jnp.int32, whole.shape, 1)
    for head in range(1, HEADS_HELD):
        whole = jnp.where(lane // HEAD_DIM == head, parts[head], whole)
    return whole


def needs_halo(prior, own_chunks):
    needed = prior[HALO_CHUNKS] > 0
    for chunk in range(1, min(own_chunks, HALO_CHUNKS)):
        needed = needed | (prior[HALO_CHUNKS + chunk] > chunk)
    return needed


ROW_PARTS = 2
UNITS = [(head, part) for part in range(ROW_PARTS) for head in range(HEADS_HELD)]


def add_keys(refs, first, size, diagonal):
    q_head, k_turned, v_wide, top, total = refs
    rows = chunk_rows(first, size)
    key_block, value_block = k_turned[rows, :], v_wide[rows, :]
    part_rows = QUERY_ROWS // ROW_PARTS

    def queries(part):
        return slice(part * part_rows, (part + 1) * part_rows)

    def start(unit):
        head, part = unit
        return nt(q_head[head, queries(part), :], key_block)

    def finish(unit, scores):
        head, part = unit
        held = (head, queries(part))
        if diagonal:
            place = lax.broadcasted_iota(jnp.int32, scores.shape, 0) + part * part_rows
            other = lax.broadcasted_iota(jnp.int32, scores.shape, 1)
            scores = jnp.where(other <= place, scores, MASKED)
        highest = jnp.max(scores, axis=1, keepdims=True)
        if diagonal:
            weights = jnp.exp2((scores - highest).astype(jnp.bfloat16))
            total[held] = nn(weights, value_block)
            top[held] = jnp.broadcast_to(highest, (part_rows, LANES))
        else:
            before = top[held]
            after = jnp.maximum(before, highest)
            weights = jnp.exp2((scores - after[:, :1]).astype(jnp.bfloat16))
            shrink = jnp.exp2(before - after)
            shrink = jnp.concatenate([shrink, shrink], axis=1)
            total[held] = total[held] * shrink + nn(weights, value_block)
            top[held] = after

    scores = start(UNITS[0])
    for index, unit in enumerate(UNITS):
        following = start(UNITS[index + 1]) if index + 1 < len(UNITS) else None
        finish(unit, scores)
        scores = following


def mixed_of(total):
    return by_head([total[head, :, :LANES] / total[head, :, LANES:] for head in range(HEADS_HELD)])


def attend_own_kernel(
    prior, q_ref, keys, values, cosine, sine, out_ref, top_ref, sum_ref, *scratch
):
    k_turned, v_wide, q_head, top, total = scratch
    block = pl.program_id(0)
    chunk = block // PER_CHUNK

    @pl.when(block == 0)
    def _():
        rotate_keys(prior, HALO_CHUNKS, keys, cosine, sine, k_turned)
        v_wide[:, :LANES] = values[...]
        v_wide[:, LANES:] = jnp.ones((values.shape[0], LANES), jnp.bfloat16)

    turned = turned_queries(prior, block, q_ref[...], cosine, sine)
    for head in range(HEADS_HELD):
        q_head[head] = of_head(turned, head)
    held = (q_head, k_turned, v_wide, top, total)
    add_keys(held, block, QUERY_ROWS, True)

    def same_chunk(index, unused):
        add_keys(held, chunk * PER_CHUNK + index, QUERY_ROWS, False)
        return unused

    def earlier_chunk(index, unused):
        add_keys(held, chunk - 1 - index, CHUNK, False)
        return unused

    lax.fori_loop(0, lax.rem(block, PER_CHUNK), same_chunk, 0)
    lax.fori_loop(0, jnp.minimum(prior[HALO_CHUNKS + chunk], chunk), earlier_chunk, 0)
    out_ref[...] = mixed_of(total).astype(jnp.bfloat16)
    top_ref[...] = by_head([top[head] for head in range(HEADS_HELD)])
    sum_ref[...] = by_head([total[head, :, LANES:] for head in range(HEADS_HELD)])


def attend_own(prior, q_seg, keys, values, cosine, sine):
    seg_rows = q_seg.shape[0]
    query_spec = pl.BlockSpec((QUERY_ROWS, LANES), lambda i, prior: (i, 0))
    wide = jax.ShapeDtypeStruct((seg_rows, LANES), jnp.float32)
    return pl.pallas_call(
        attend_own_kernel,
        grid_spec=pltpu.PrefetchScalarGridSpec(
            num_scalar_prefetch=1,
            grid=(seg_rows // QUERY_ROWS,),
            in_specs=[query_spec, VMEM, VMEM, VMEM, VMEM],
            out_specs=(query_spec,) * 3,
            scratch_shapes=[
                pltpu.VMEM((seg_rows, LANES), jnp.bfloat16),
                pltpu.VMEM((seg_rows, 2 * LANES), jnp.bfloat16),
                pltpu.VMEM((HEADS_HELD, QUERY_ROWS, LANES), jnp.bfloat16),
                pltpu.VMEM((HEADS_HELD, QUERY_ROWS, LANES), jnp.float32),
                pltpu.VMEM((HEADS_HELD, QUERY_ROWS, 2 * LANES), jnp.float32),
            ],
        ),
        out_shape=(jax.ShapeDtypeStruct((seg_rows, LANES), jnp.bfloat16), wide, wide),
        compiler_params=pltpu.CompilerParams(vmem_limit_bytes=BIG_VMEM),
        cost_estimate=pl.CostEstimate(
            flops=20_000_000_000, bytes_accessed=100_000_000, transcendentals=16_000_000
        ),
        name="attend_own",
    )(prior, q_seg, keys, values, cosine, sine)


def copy_in(pairs, sems):
    copies = [
        pltpu.make_async_copy(source, target, sems.at[index])
        for index, (source, target) in enumerate(pairs)
    ]
    for copy in copies:
        copy.start()
    for copy in copies:
        copy.wait()


def attend_halo_kernel(
    own_chunks, prior, q_seg, keys, values, cos_hbm, sin_hbm, out_in, top_in, sum_in,
    out, top_out, sum_out, *scratch
):
    k_turned, v_wide, q_head, top, total, key_rows, value_rows, cosine, sine = scratch[:9]
    q_rows, out_rows, top_rows, sum_rows, sems = scratch[9:]

    def one_block(block, unused):
        chunk = block // PER_CHUNK
        count = prior[HALO_CHUNKS + chunk] - chunk
        rows = chunk_rows(block, QUERY_ROWS)

        @pl.when(count > 0)
        def _():
            turned = turned_queries(prior, block, q_rows[rows, :], cosine, sine)
            mixed, tops, sums = out_rows[rows, :], top_rows[rows, :], sum_rows[rows, :]
            for head in range(HEADS_HELD):
                lane = head * HEAD_DIM
                q_head[head] = of_head(turned, head)
                top[head] = jnp.broadcast_to(tops[:, lane : lane + 1], top.shape[1:])
                weight = jnp.broadcast_to(sums[:, lane : lane + 1], top.shape[1:])
                total[head, :, :LANES] = mixed.astype(jnp.float32) * weight
                total[head, :, LANES:] = weight

            def earlier_chunk(index, unused):
                held = (q_head, k_turned, v_wide, top, total)
                add_keys(held, HALO_CHUNKS - 1 - index, CHUNK, False)
                return unused

            lax.fori_loop(0, count, earlier_chunk, 0)
            out_rows[rows, :] = mixed_of(total).astype(jnp.bfloat16)
            top_rows[rows, :] = by_head([top[head] for head in range(HEADS_HELD)])
            sum_rows[rows, :] = by_head([total[head, :, LANES:] for head in range(HEADS_HELD)])

        return unused

    @pl.when(needs_halo(prior, own_chunks))
    def _():
        part = pl.ds(0, q_rows.shape[0])
        held = ((out, out_rows), (top_out, top_rows), (sum_out, sum_rows))
        copy_in(
            (
                (keys, key_rows), (values, value_rows), (cos_hbm, cosine), (sin_hbm, sine),
                (q_seg.at[part], q_rows), *((hbm.at[part], rows) for hbm, rows in held),
            ),
            sems,
        )
        rotate_keys(prior, 0, key_rows, cosine, sine, k_turned)
        v_wide[:, :LANES] = value_rows[...]
        v_wide[:, LANES:] = jnp.ones((value_rows.shape[0], LANES), jnp.bfloat16)
        lax.fori_loop(0, q_rows.shape[0] // QUERY_ROWS, one_block, 0)
        copy_in([(rows, hbm.at[part]) for hbm, rows in held], sems)


def attend_halo(prior, q_seg, keys, values, cosine, sine, earlier):
    part = (min(q_seg.shape[0], HALO), LANES)
    per_head = (HEADS_HELD, QUERY_ROWS, LANES)
    return pl.pallas_call(
        functools.partial(attend_halo_kernel, q_seg.shape[0] // CHUNK),
        in_specs=[SMEM] + [ANY] * 8,
        out_specs=(ANY,) * 3,
        out_shape=tuple(jax.ShapeDtypeStruct(one.shape, one.dtype) for one in earlier),
        scratch_shapes=[
            pltpu.VMEM((HALO, LANES), jnp.bfloat16),
            pltpu.VMEM((HALO, 2 * LANES), jnp.bfloat16),
            pltpu.VMEM(per_head, jnp.bfloat16),
            pltpu.VMEM(per_head, jnp.float32),
            pltpu.VMEM((HEADS_HELD, QUERY_ROWS, 2 * LANES), jnp.float32),
            pltpu.VMEM((HALO, LANES), jnp.bfloat16),
            pltpu.VMEM((HALO, LANES), jnp.bfloat16),
            pltpu.VMEM((LONGEST, LANES), jnp.float32),
            pltpu.VMEM((LONGEST, LANES), jnp.float32),
            pltpu.VMEM(part, jnp.bfloat16),
            pltpu.VMEM(part, jnp.bfloat16),
            pltpu.VMEM(part, jnp.float32),
            pltpu.VMEM(part, jnp.float32),
            pltpu.SemaphoreType.DMA((8,)),
        ],
        input_output_aliases={6: 0, 7: 1, 8: 2},
        compiler_params=pltpu.CompilerParams(vmem_limit_bytes=BIG_VMEM),
        cost_estimate=pl.CostEstimate(
            flops=10_000_000_000, bytes_accessed=20_000_000, transcendentals=8_000_000
        ),
        name="attend_halo",
    )(prior, q_seg, keys, values, cosine, sine, *earlier)


def prepare_back(refs, block, prior, queries, grads, mixed, tops, sums, cosine, sine):
    q_head, grad_head, row_stats = refs
    turned = turned_queries(prior, block, queries, cosine, sine)
    grads = grads.astype(jnp.float32) / sums
    dots = (grads * mixed.astype(jnp.float32)).T
    tops = tops.T
    grads = grads.astype(jnp.bfloat16)
    for head in range(HEADS_HELD):
        q_head[head] = of_head(turned, head)
        grad_head[head] = of_head(grads, head)
        lanes = slice(head * HEAD_DIM, (head + 1) * HEAD_DIM)
        row_stats[head, 0:1, :] = tops[head * HEAD_DIM : head * HEAD_DIM + 1, :]
        row_stats[head, 1:2, :] = jnp.sum(dots[lanes, :], axis=0, keepdims=True)


def add_keys_back(refs, first, diagonal):
    q_head, grad_head, row_stats, k_turned, values, dq_total, dk_total, dv_total = refs
    part_rows = QUERY_ROWS // ROW_PARTS

    def keys(part):
        start = pl.multiple_of(first * QUERY_ROWS + part * part_rows, part_rows)
        return pl.ds(start, part_rows)

    def start(unit):
        head, part = unit
        rows = keys(part)
        return nt(k_turned[rows, :], q_head[head]), nt(values[rows, :], grad_head[head])

    def finish(unit, products_):
        head, part = unit
        rows = keys(part)
        scores, grad_weights = products_
        weights = jnp.exp2((scores - row_stats[head, 0:1, :]).astype(jnp.bfloat16))
        if diagonal:
            other = lax.broadcasted_iota(jnp.int32, scores.shape, 0) + part * part_rows
            place = lax.broadcasted_iota(jnp.int32, scores.shape, 1)
            weights = jnp.where(other <= place, weights, jnp.zeros_like(weights))
        grad_scores = weights * (grad_weights - row_stats[head, 1:2, :]).astype(jnp.bfloat16)
        dv_total[rows, :] += nn(weights, grad_head[head])
        dk_total[rows, :] += nn(grad_scores, q_head[head])
        dq_total[head] += tn(grad_scores, k_turned[rows, :])

    held = start(UNITS[0])
    for index, unit in enumerate(UNITS):
        following = start(UNITS[index + 1]) if index + 1 < len(UNITS) else None
        finish(unit, held)
        held = following


def turn_keys_back(prior, first_chunk, dk_total, dv_total, cosine, sine, dk_ref, dv_ref):
    def one(index, unused):
        table = chunk_rows(prior[first_chunk + index], CHUNK)
        rows = chunk_rows(index, CHUNK)
        turned = rotate(dk_total[rows, :], cosine[table, :], -sine[table, :]) * (1.0 / LOG2E)
        dk_ref[rows, :] = turned.astype(dk_ref.dtype)
        dv_ref[rows, :] = dv_total[rows, :].astype(dv_ref.dtype)
        return unused

    lax.fori_loop(0, dk_ref.shape[0] // CHUNK, one, 0)


def attend_back_own_kernel(
    prior, q_ref, grad_ref, out_ref, top_ref, sum_ref, keys, values, cosine, sine, dq_part,
    dq_ref, dk_ref, dv_ref, k_turned, q_head, grad_head, dq_total, dk_total, dv_total, row_stats
):
    block = pl.program_id(0)
    chunk = block // PER_CHUNK
    chunks_back = prior[HALO_CHUNKS + chunk]

    @pl.when(block == 0)
    def _():
        rotate_keys(prior, HALO_CHUNKS, keys, cosine, sine, k_turned)
        dk_total[...] = jnp.zeros_like(dk_total)
        dv_total[...] = jnp.zeros_like(dv_total)

    prepare_back(
        (q_head, grad_head, row_stats), block, prior, q_ref[...], grad_ref[...], out_ref[...],
        top_ref[...], sum_ref[...], cosine, sine,
    )
    from_halo = jnp.where(chunks_back > chunk, dq_part[...], jnp.zeros_like(dq_part))
    for head in range(HEADS_HELD):
        dq_total[head] = from_halo
    held = (q_head, grad_head, row_stats, k_turned, values, dq_total, dk_total, dv_total)
    add_keys_back(held, block, True)

    def whole(index, unused):
        add_keys_back(held, index, False)
        return unused

    lax.fori_loop(jnp.maximum(chunk - chunks_back, 0) * PER_CHUNK, block, whole, 0)
    cos_rows, sin_rows = query_tables(prior, block, cosine, sine)
    turned = rotate(by_head([dq_total[head] for head in range(HEADS_HELD)]), cos_rows, -sin_rows)
    dq_ref[...] = (turned * HEAD_DIM ** (-0.5)).astype(jnp.bfloat16)

    @pl.when(block == pl.num_programs(0) - 1)
    def _():
        turn_keys_back(prior, HALO_CHUNKS, dk_total, dv_total, cosine, sine, dk_ref, dv_ref)


def back_scratch(key_rows):
    per_head = (HEADS_HELD, QUERY_ROWS, LANES)
    return [
        pltpu.VMEM((key_rows, LANES), jnp.bfloat16),
        pltpu.VMEM(per_head, jnp.bfloat16),
        pltpu.VMEM(per_head, jnp.bfloat16),
        pltpu.VMEM(per_head, jnp.float32),
        pltpu.VMEM((key_rows, LANES), jnp.float32),
        pltpu.VMEM((key_rows, LANES), jnp.float32),
        pltpu.VMEM((HEADS_HELD, 8, QUERY_ROWS), jnp.float32),
    ]


def attend_back_own(prior, q_seg, grad_seg, seen, keys, values, cosine, sine, dq_part):
    seg_rows = q_seg.shape[0]
    query_spec = pl.BlockSpec((QUERY_ROWS, LANES), lambda i, prior: (i, 0))
    wide = jax.ShapeDtypeStruct((seg_rows, LANES), jnp.float32)
    return pl.pallas_call(
        attend_back_own_kernel,
        grid_spec=pltpu.PrefetchScalarGridSpec(
            num_scalar_prefetch=1,
            grid=(seg_rows // QUERY_ROWS,),
            in_specs=[query_spec] * 5 + [VMEM] * 4 + [query_spec],
            out_specs=(query_spec, VMEM, VMEM),
            scratch_shapes=back_scratch(seg_rows),
        ),
        out_shape=(jax.ShapeDtypeStruct((seg_rows, LANES), jnp.bfloat16), wide, wide),
        compiler_params=pltpu.CompilerParams(vmem_limit_bytes=BIG_VMEM),
        cost_estimate=pl.CostEstimate(
            flops=40_000_000_000, bytes_accessed=150_000_000, transcendentals=16_000_000
        ),
        name="attend_back_own",
    )(prior, q_seg, grad_seg, *seen, keys, values, cosine, sine, dq_part)


def attend_back_halo_kernel(
    own_chunks, prior, q_seg, grad_seg, mixed, tops, sums, keys, values, cos_hbm, sin_hbm,
    dq_out, dk_out, dv_out, *scratch
):
    k_turned, q_head, grad_head, dq_total, dk_total, dv_total, row_stats = scratch[:7]
    key_rows, value_rows, cosine, sine, dk_half, dv_half = scratch[7:13]
    q_rows, grad_rows, out_rows, top_rows, sum_rows, dq_rows, sems = scratch[13:]
    needed = needs_halo(prior, own_chunks)
    part = pl.ds(0, q_rows.shape[0])

    def one_block(block, unused):
        chunk = block // PER_CHUNK
        chunks_back = prior[HALO_CHUNKS + chunk]
        rows = chunk_rows(block, QUERY_ROWS)

        @pl.when(chunks_back > chunk)
        def _():
            prepare_back(
                (q_head, grad_head, row_stats), block, prior, q_rows[rows, :], grad_rows[rows, :],
                out_rows[rows, :], top_rows[rows, :], sum_rows[rows, :], cosine, sine,
            )
            dq_total[...] = jnp.zeros_like(dq_total)

            def whole(index, unused):
                add_keys_back(
                    (
                        q_head, grad_head, row_stats, k_turned, value_rows, dq_total, dk_total,
                        dv_total,
                    ),
                    index,
                    False,
                )
                return unused

            start = (HALO_CHUNKS + chunk - chunks_back) * PER_CHUNK
            lax.fori_loop(start, HALO_CHUNKS * PER_CHUNK, whole, 0)
            dq_rows[rows, :] = by_head([dq_total[head] for head in range(HEADS_HELD)])

        return unused

    @pl.when(needed)
    def _():
        copy_in(
            (
                (keys, key_rows), (values, value_rows), (cos_hbm, cosine), (sin_hbm, sine),
                (q_seg.at[part], q_rows), (grad_seg.at[part], grad_rows),
                (mixed.at[part], out_rows), (tops.at[part], top_rows), (sums.at[part], sum_rows),
            ),
            sems,
        )
        rotate_keys(prior, 0, key_rows, cosine, sine, k_turned)
        dk_total[...] = jnp.zeros_like(dk_total)
        dv_total[...] = jnp.zeros_like(dv_total)
        lax.fori_loop(0, q_rows.shape[0] // QUERY_ROWS, one_block, 0)
        turn_keys_back(prior, 0, dk_total, dv_total, cosine, sine, dk_half, dv_half)
        copy_in(((dq_rows, dq_out.at[part]),), sems)

    @pl.when(jnp.logical_not(needed))
    def _():
        dk_half[...] = jnp.zeros_like(dk_half)
        dv_half[...] = jnp.zeros_like(dv_half)

    copy_in(((dk_half, dk_out), (dv_half, dv_out)), sems)


def attend_back_halo(prior, q_seg, grad_seg, seen, keys, values, cosine, sine):
    seg_rows = q_seg.shape[0]
    part = (min(seg_rows, HALO), LANES)
    half = jax.ShapeDtypeStruct((HALO, LANES), jnp.bfloat16)
    return pl.pallas_call(
        functools.partial(attend_back_halo_kernel, seg_rows // CHUNK),
        in_specs=[SMEM] + [ANY] * 9,
        out_specs=(ANY,) * 3,
        out_shape=(jax.ShapeDtypeStruct((seg_rows, LANES), jnp.float32), half, half),
        scratch_shapes=back_scratch(HALO)
        + [
            pltpu.VMEM((HALO, LANES), jnp.bfloat16),
            pltpu.VMEM((HALO, LANES), jnp.bfloat16),
            pltpu.VMEM((LONGEST, LANES), jnp.float32),
            pltpu.VMEM((LONGEST, LANES), jnp.float32),
            pltpu.VMEM((HALO, LANES), jnp.bfloat16),
            pltpu.VMEM((HALO, LANES), jnp.bfloat16),
            pltpu.VMEM(part, jnp.bfloat16),
            pltpu.VMEM(part, jnp.bfloat16),
            pltpu.VMEM(part, jnp.bfloat16),
            pltpu.VMEM(part, jnp.float32),
            pltpu.VMEM(part, jnp.float32),
            pltpu.VMEM(part, jnp.float32),
            pltpu.SemaphoreType.DMA((9,)),
        ],
        compiler_params=pltpu.CompilerParams(vmem_limit_bytes=BIG_VMEM),
        cost_estimate=pl.CostEstimate(
            flops=20_000_000_000, bytes_accessed=20_000_000, transcendentals=8_000_000
        ),
        name="attend_back_halo",
    )(prior, q_seg, grad_seg, *seen, keys, values, cosine, sine)


def attention(plan, tables, q_seg, k_seg, v_seg):
    k_halo, v_halo = halo_of(plan, k_seg), halo_of(plan, v_seg)
    earlier = attend_own(tables[0], q_seg, k_seg, v_seg, *tables[1:])
    seen = attend_halo(tables[0], q_seg, k_halo, v_halo, *tables[1:], earlier)
    return seen[0], (q_seg, k_seg, v_seg, k_halo, v_halo, seen)


def attention_back(plan, tables, kept, grad_seg, waiting):
    q_seg, k_seg, v_seg, k_halo, v_halo, seen = kept
    queries = (tables[0], q_seg, grad_seg, seen)
    dq_part, dk_halo, dv_halo = attend_back_halo(*queries, k_halo, v_halo, *tables[1:])
    halos = halo_back(plan, dk_halo) + halo_back(plan, dv_halo)
    dq, dk_own, dv_own = attend_back_own(*queries, k_seg, v_seg, *tables[1:], dq_part)
    dq = collect(plan, (dq,), ())[0]
    dq, waiting, *halos = lax.optimization_barrier((dq, waiting, *halos))
    return (dq, *collect(plan, (dk_own, dv_own), halos)), waiting


def rotary_tables():
    half = HEAD_DIM // 2
    lane = jnp.arange(LANES)
    frequency = jnp.exp(
        (lane % half).astype(jnp.float32) * (-2.0 * math.log(10000.0) / HEAD_DIM)
    )
    sign = jnp.where(lane % HEAD_DIM < half, -1.0, 1.0).astype(jnp.float32)
    step = 64
    fine = jnp.arange(step).astype(jnp.float32)[:, None] * frequency[None, :]
    coarse = jnp.arange(0, LONGEST, step).astype(jnp.float32)[:, None] * frequency[None, :]
    cos_fine, sin_fine, cos_coarse, sin_coarse = lax.optimization_barrier(
        (jnp.cos(fine), jnp.sin(fine), jnp.cos(coarse), jnp.sin(coarse))
    )
    cosine = cos_coarse[:, None] * cos_fine[None] - sin_coarse[:, None] * sin_fine[None]
    sine = sin_coarse[:, None] * cos_fine[None] + cos_coarse[:, None] * sin_fine[None]
    return (
        cosine.reshape(LONGEST, LANES),
        (sine * sign).reshape(LONGEST, LANES),
    )


def chunks_before(plan, lengths):
    segment, unused = plan.here()
    count = (HALO + plan.seg_rows) // CHUNK
    places = segment * plan.seg_rows - HALO + CHUNK * jnp.arange(count)
    ends = jnp.cumsum(lengths)
    passed = ends[None, :] <= places[:, None]
    opening = jnp.max(jnp.where(passed, ends[None, :], 0), axis=1)
    return jnp.clip((places - opening) // CHUNK, 0, HALO_CHUNKS).astype(jnp.int32)


def tied(array, *others):
    return lax.optimization_barrier((array, *others))[0]


def attention_pack(weights):
    return jnp.stack([weights[1].T, weights[2].T, weights[3].T, weights[4]])


def feedforward_pack(weights):
    return jnp.stack([weights[6].T, weights[7].T, weights[8]])


def fetch_mp(packs):
    rows = [pack.reshape(-1, pack.shape[-1]) for pack in packs]
    whole = rows[0] if len(rows) == 1 else jnp.concatenate(rows, axis=0)
    return lax.all_gather(whole, "mp", axis=0, tiled=False)


def fetch_dp(whole, first, pack):
    count, rows, width = pack.shape
    members = whole.shape[0]
    part = whole[:, first : first + count * rows].reshape(members, count, rows, width)
    part = part.transpose(1, 0, 2, 3).reshape(count, members * rows, width)
    return lax.all_gather(part, "dp", axis=2, tiled=True)


def turn_kernel(members, sizes, part, out):
    start, row = 0, 0
    for size in sizes:
        turned = part[:, start : start + size].T
        count = size // members
        for member in range(members):
            out[member, row : row + count, :] = turned[member * count : (member + 1) * count, :]
        start += size
        row += count


def mp_blocks(plan, part, sizes):
    rows = sum(sizes) // plan.m
    if part.shape[0] == LANES:
        return pl.pallas_call(
            functools.partial(turn_kernel, plan.m, sizes),
            in_specs=[VMEM],
            out_specs=VMEM,
            out_shape=jax.ShapeDtypeStruct((plan.m, rows, LANES), part.dtype),
            compiler_params=pltpu.CompilerParams(vmem_limit_bytes=BIG_VMEM),
            cost_estimate=pl.CostEstimate(
                flops=0, bytes_accessed=10_000_000, transcendentals=0
            ),
            name="turn",
        )(part)
    turned, start, pieces = part.T, 0, []
    for size in sizes:
        piece = turned[start : start + size]
        pieces.append(piece.reshape(plan.m, size // plan.m, turned.shape[1]))
        start += size
    return jnp.concatenate(pieces, axis=1)


def reduce_mp(plan, blocks, sizes):
    part = lax.psum_scatter(blocks, "mp", scatter_dimension=0, tiled=False).astype(jnp.float32)
    start, pieces = 0, []
    for size in sizes:
        pieces.append(part[start : start + size // plan.m])
        start += size // plan.m
    return pieces


def reduce_qkv(plan, gradient, extra):
    gradient = jnp.concatenate([gradient, extra.astype(jnp.bfloat16)], axis=1)
    part = lax.psum_scatter(gradient, "dp", scatter_dimension=0, tiled=True)
    width = D // plan.m
    blocks = part[:, : 3 * D].reshape(-1, 3, plan.m, width).transpose(2, 0, 1, 3)
    blocks = blocks.reshape(plan.m, -1, 3 * width)
    shared = jnp.broadcast_to(part[None, :, 3 * D :], (plan.m, part.shape[0], LANES))
    blocks = jnp.concatenate([blocks, shared], axis=2)
    return lax.psum_scatter(blocks, "mp", scatter_dimension=0, tiled=False).astype(jnp.float32)


def project(normed, attention, first_values):
    query, key, fresh = (nt(normed, attention[part]) for part in range(3))
    if first_values is not None:
        fresh = 0.5 * fresh + 0.5 * first_values.astype(jnp.float32)
    return tuple(array.astype(jnp.bfloat16) for array in (query, key, fresh))


def feed_forward(middle, gain, feedforward):
    normed_ff = norm_rows(middle, gain).astype(jnp.bfloat16)
    gate = nt(normed_ff, feedforward[0])
    upward = nt(normed_ff, feedforward[1])
    hidden = (jax.nn.silu(gate) * upward).astype(jnp.bfloat16)
    final = middle + nn(hidden, feedforward[2])
    return final, (normed_ff, gate, upward, hidden)


def feed_forward_back(grad_final, middle, gain, weights, stored):
    attention, feedforward = weights
    normed_ff, gate, upward, hidden = stored
    grad_bar = grad_final.astype(jnp.bfloat16)
    grad_hidden = nt(grad_bar, feedforward[2])
    gate_sigmoid = jax.nn.sigmoid(gate)
    grad_gate = (
        grad_hidden * upward * gate_sigmoid * (1.0 + gate * (1.0 - gate_sigmoid))
    ).astype(jnp.bfloat16)
    grad_up = (grad_hidden * gate * gate_sigmoid).astype(jnp.bfloat16)
    grad_normed_ff = nn(grad_gate, feedforward[0]) + nn(grad_up, feedforward[1])
    grad_norm, grad_gain = norm_back(middle, gain, grad_normed_ff)
    grad_middle = grad_final + grad_norm
    middle_bar = grad_middle.astype(jnp.bfloat16)
    grad_mixed = nt(middle_bar, attention[3]).astype(jnp.bfloat16)
    return grad_middle, grad_gain, grad_mixed, (grad_bar, grad_gate, grad_up, middle_bar)


def project_back(grad_middle, stream, gain, attention, dqkv):
    grad_normed = sum(nn(array, attention[part]) for part, array in enumerate(dqkv))
    grad_norm, grad_gain = norm_back(stream, gain, grad_normed)
    return grad_middle + grad_norm, grad_gain


def square_sum(values):
    widened = values.astype(jnp.float32)
    return jnp.sum(widened * widened)


def shards(n, m, inputs, lengths, *rest):
    plan = Plan(n, m)
    first, second, cotangent = rest[:9], rest[9:18], rest[18]
    cosine, sine = rotary_tables()
    tables = (chunks_before(plan, lengths), cosine, sine)
    by_hand = (n, m) == (8, 4)
    gain_shard = jnp.stack([first[0], first[5], second[0], second[5]])
    packs_one = (attention_pack(first), feedforward_pack(first))
    packs_two = (attention_pack(second), feedforward_pack(second))
    if by_hand:
        attention_one, gains = weave(plan, packs_one[0], jnp.pad(gain_shard, ((0, 12), (0, 0))))
        whole = tied(fetch_mp(packs_one[1:]), gains)
        feedforward_one = fetch_dp(whole, 0, packs_one[1])
    else:
        gains = lax.all_gather(gain_shard, "dp", axis=1, tiled=True)
        whole = fetch_mp(packs_one)
        attention_one = fetch_dp(whole, 0, packs_one[0])
        feedforward_one = fetch_dp(whole, 4 * packs_one[0].shape[1], packs_one[1])
    gains = gains[:4].astype(jnp.float32)
    heads, hidden_rows = first[4].shape[0] * m, first[8].shape[0] * m
    rest_sizes = (hidden_rows, hidden_rows, hidden_rows, heads)

    stream = inputs.astype(jnp.float32)
    normed_one = norm_rows(stream, gains[0]).astype(jnp.bfloat16)
    qkv = project(normed_one, attention_one, None)
    values_one = qkv[2]
    q_seg, k_seg, v_seg = spread(plan, *qkv)
    feedforward_one, q_seg, packs_two = lax.optimization_barrier(
        (feedforward_one, q_seg, packs_two)
    )
    whole_two = fetch_mp(packs_two)
    out_seg, seen_one = attention(plan, tables, q_seg, k_seg, v_seg)
    out_seg, whole_two = lax.optimization_barrier((out_seg, whole_two))
    mixed_one = to_rows(plan, out_seg)
    attention_two = fetch_dp(whole_two, 0, packs_two[0])
    feedforward_two = fetch_dp(whole_two, 4 * packs_two[0].shape[1], packs_two[1])
    middle_one = stream + nn(mixed_one, attention_one[3])
    between, ff_one = feed_forward(middle_one, gains[1], feedforward_one)

    normed_two = norm_rows(between, gains[2]).astype(jnp.bfloat16)
    qkv = project(normed_two, attention_two, values_one)
    values_two = qkv[2]
    q_seg, k_seg, v_seg = spread(plan, *qkv)
    out_seg, seen_two = attention(plan, tables, q_seg, k_seg, v_seg)
    mixed_two = to_rows(plan, out_seg)
    middle_two = between + nn(mixed_two, attention_two[3])
    final, ff_two = feed_forward(middle_two, gains[3], feedforward_two)

    grad_middle, gain_ff_two, grad_mixed, (bar, grad_gate, grad_up, middle_bar) = feed_forward_back(
        cotangent.astype(jnp.float32), middle_two, gains[3], (attention_two, feedforward_two), ff_two
    )
    grad_seg, rest = products(
        plan,
        grad_mixed,
        (bar, ff_two[0], middle_bar),
        (ff_two[3], grad_gate, grad_up, mixed_two),
        (0, 1, 1, 2),
    )
    dqkv, rest = attention_back(plan, tables, seen_two, grad_seg, rest)
    rest_two = lax.psum_scatter(rest, "dp", scatter_dimension=0, tiled=True)
    value_extra = 0.5 * dqkv[2].astype(jnp.float32)
    dqkv_two = (dqkv[0], dqkv[1], value_extra.astype(jnp.bfloat16))
    grad_between, gain_two = project_back(
        grad_middle, between, gains[2], attention_two, dqkv_two
    )

    grad_middle, gain_ff_one, grad_mixed, (bar, grad_gate, grad_up, middle_bar) = feed_forward_back(
        grad_between, middle_one, gains[1], (attention_one, feedforward_one), ff_one
    )
    grad_seg, rest = products(
        plan,
        grad_mixed,
        (bar, ff_one[0], middle_bar, normed_two),
        (ff_one[3], grad_gate, grad_up, mixed_one, *dqkv_two),
        (0, 1, 1, 2, 3, 3, 3),
    )
    blocks_two = mp_blocks(plan, tied(rest_two, grad_seg), rest_sizes)
    grad_seg, blocks_two, rest = lax.optimization_barrier((grad_seg, blocks_two, rest))
    reduced_two = reduce_mp(plan, blocks_two, rest_sizes)
    rest_one = lax.psum_scatter(rest, "dp", scatter_dimension=0, tiled=True)
    dqkv, reduced_two = attention_back(plan, tables, seen_one, grad_seg, reduced_two)
    grad_values = dqkv[2].astype(jnp.float32) + value_extra
    dqkv_one = (dqkv[0], dqkv[1], grad_values.astype(jnp.bfloat16))
    input_grad, gain_one = project_back(grad_middle, stream, gains[0], attention_one, dqkv_one)
    input_grad, rest_one = lax.optimization_barrier((input_grad, rest_one))
    both_sizes = rest_sizes + (heads,) * 3
    blocks_one, dqkv_one = lax.optimization_barrier(
        (mp_blocks(plan, rest_one, both_sizes), dqkv_one)
    )
    down_one, gate_one, up_one, output_one, query_two, key_two, value_two = reduce_mp(
        plan, blocks_one, both_sizes
    )
    down_two, gate_two, up_two, output_two = reduced_two
    squares = [square_sum(values_one), square_sum(values_two)]
    width = D // n
    own_row = jnp.arange(D) == lax.axis_index("dp") * width
    squares = [jnp.where(own_row, square, 0.0) for square in squares]
    extra = jnp.stack([gain_one, gain_ff_one, gain_two, gain_ff_two, *squares], axis=1)
    extra = jnp.pad(extra, ((0, 0), (0, LANES - extra.shape[1])))
    if by_hand:
        part = shed(plan, normed_one, dqkv_one, extra)
    else:
        whole = [tn(normed_one, array).astype(jnp.bfloat16) for array in dqkv_one]
        part = reduce_qkv(plan, jnp.concatenate(whole, axis=1), extra)
    piece = D // m
    query_one, key_one, value_one = (part[:, i * piece : (i + 1) * piece] for i in range(3))
    shared = part[:, 3 * piece :]
    value_norms = jnp.sqrt(shared[:1, 4:6] / (TOK_DEV * D))
    return (
        between.astype(jnp.bfloat16),
        final.astype(jnp.bfloat16),
        input_grad,
        shared[:, 0], query_one, key_one, value_one, output_one,
        shared[:, 1], gate_one.T, up_one.T, down_one,
        shared[:, 2], query_two.T, key_two.T, value_two.T, output_two,
        shared[:, 3], gate_two.T, up_two.T, down_two,
        value_norms,
    )


def solution(mesh):
    tokens, row_split, column_split = P(("dp", "mp"), None), P("dp", "mp"), P("mp", "dp")
    layer = (
        P("dp"), row_split, row_split, row_split, column_split, P("dp"), row_split, row_split,
        column_split,
    )
    return jax.shard_map(
        functools.partial(shards, mesh.shape["dp"], mesh.shape["mp"]),
        mesh=mesh,
        in_specs=(tokens, P(), *layer, *layer, tokens),
        out_specs=(tokens, tokens, tokens, *layer, *layer, P("dp", None)),
        check_vma=False,
    )
```

```python
import functools
import math

import jax
import jax.numpy as jnp
from jax import lax
from jax.experimental import pallas as pl
from jax.experimental.pallas import tpu as pltpu
from jax.sharding import PartitionSpec as P

D = 1024
HEAD_DIM = 64
TOK_DEV = 2048
LONGEST = 4096

LANES = 128
HEADS_HELD = LANES // HEAD_DIM
CHUNK = 1024
HALO = LONGEST - CHUNK
QUERY_ROWS = 1024
TILE = 256
EPSILON = 1e-06
MASKED = -1e30
LOG2E = math.log2(math.e)
MESH = pl.DeviceIdType.MESH
ANY = pl.BlockSpec(memory_space=pl.ANY)
VMEM = pl.BlockSpec(memory_space=pltpu.VMEM)
SMEM = pl.BlockSpec(memory_space=pltpu.SMEM)
BIG_VMEM = 56 * 1024 * 1024
BRIEF = pl.CostEstimate(flops=0, bytes_accessed=1_000, transcendentals=0)


def nn(left_side, right_side):
    return jnp.dot(left_side, right_side, preferred_element_type=jnp.float32)


def tn(left_side, right_side):
    return lax.dot_general(
        left_side, right_side, (((0,), (0,)), ((), ())), preferred_element_type=jnp.float32
    )


def nt(left_side, right_side):
    return lax.dot_general(
        left_side, right_side, (((1,), (1,)), ((), ())), preferred_element_type=jnp.float32
    )


def norm_rows(values, gain_vector):
    scaling = lax.rsqrt(jnp.mean(values * values, axis=-1, keepdims=True) + EPSILON)
    return values * scaling * gain_vector


def norm_back(values, gain_vector, grad_output):
    unused, pullback = jax.vjp(norm_rows, values, gain_vector)
    return pullback(grad_output)


class Plan:
    def __init__(self, n, m):
        self.n, self.m = n, m
        self.group = D // LANES
        self.low = self.group // m
        self.segments = n // self.low
        self.rows = TOK_DEV // m
        self.seg_rows = self.rows * self.group
        self.spans = []
        left, distance = HALO, 1
        while left > 0:
            count = min(self.seg_rows, left)
            self.spans.append((distance, left - count, count))
            left -= count
            distance += 1

    def here(self):
        dp, mp = lax.axis_index("dp"), lax.axis_index("mp")
        return dp // self.low, (dp % self.low) * self.m + mp

    def device(self, segment, member):
        return (segment * self.low + member // self.m, member % self.m)


def greet(plan, segment, member):
    barrier = pltpu.get_barrier_semaphore()
    for offset in range(1, plan.group):
        peer = lax.rem(member + offset, plan.group)
        pl.semaphore_signal(
            barrier, inc=1, device_id=plan.device(segment, peer), device_id_type=MESH
        )
    pl.semaphore_wait(barrier, plan.group - 1)


def member_copies(plan, segment, member, source, target, send, recv, own):
    copies = [pltpu.make_async_copy(source(member), target, own)]
    for offset in range(1, plan.group):
        peer = lax.rem(member + offset, plan.group)
        copies.append(
            pltpu.make_async_remote_copy(
                src_ref=source(peer),
                dst_ref=target,
                send_sem=send.at[offset],
                recv_sem=recv.at[offset],
                device_id=plan.device(segment, peer),
                device_id_type=MESH,
            )
        )
    for copy in copies[1:] + copies[:1]:
        copy.start()
    return copies


def columns(index):
    return pl.ds(pl.multiple_of(index * LANES, LANES), LANES)


def spread_kernel(plan, query, key, value, q_seg, k_seg, v_seg, send, recv, own):
    segment, member = plan.here()
    rows = plan.rows
    greet(plan, segment, member)
    copies = []
    place = pl.ds(pl.multiple_of(member * rows, rows), rows)
    for part, (array, out) in enumerate(((key, k_seg), (value, v_seg), (query, q_seg))):

        def source(peer, array=array):
            return array.at[:, columns(peer)]

        copies += member_copies(
            plan, segment, member, source, out.at[place], send.at[part], recv.at[part], own.at[part]
        )
    for copy in copies:
        copy.wait()


def spread(plan, query, key, value):
    segment = jax.ShapeDtypeStruct((plan.seg_rows, LANES), jnp.bfloat16)
    return pl.pallas_call(
        functools.partial(spread_kernel, plan),
        out_shape=(segment,) * 3,
        in_specs=[ANY] * 3,
        out_specs=(ANY, ANY, ANY),
        scratch_shapes=[
            pltpu.SemaphoreType.DMA((3, plan.group)),
            pltpu.SemaphoreType.DMA((3, plan.group)),
            pltpu.SemaphoreType.DMA((3,)),
        ],
        compiler_params=pltpu.CompilerParams(collective_id=1, has_side_effects=True),
        cost_estimate=BRIEF,
        name="spread",
    )(query, key, value)


def halo_of(plan, seg):
    parts = []
    for distance, first, count in reversed(plan.spans):
        route = [(i, i + distance * plan.low) for i in range(plan.n - distance * plan.low)]
        parts.append(lax.ppermute(seg[plan.seg_rows - count :], "dp", route))
    return parts[0] if len(parts) == 1 else jnp.concatenate(parts, axis=0)


def halo_back(plan, halo):
    parts = []
    for distance, first, count in plan.spans:
        route = [(i, i - distance * plan.low) for i in range(distance * plan.low, plan.n)]
        parts.append(lax.ppermute(halo[first : first + count], "dp", route))
    return parts


def to_rows_kernel(plan, seg, rows_out, send, recv, own):
    segment, member = plan.here()
    rows = plan.rows
    greet(plan, segment, member)

    def source(peer):
        return seg.at[pl.ds(pl.multiple_of(peer * rows, rows), rows)]

    for copy in member_copies(
        plan, segment, member, source, rows_out.at[:, columns(member)], send, recv, own
    ):
        copy.wait()


def to_rows(plan, seg):
    return pl.pallas_call(
        functools.partial(to_rows_kernel, plan),
        out_shape=jax.ShapeDtypeStruct((plan.rows, D), jnp.bfloat16),
        in_specs=[ANY],
        out_specs=ANY,
        scratch_shapes=[
            pltpu.SemaphoreType.DMA((plan.group,)),
            pltpu.SemaphoreType.DMA((plan.group,)),
            pltpu.SemaphoreType.DMA,
        ],
        compiler_params=pltpu.CompilerParams(collective_id=2, has_side_effects=True),
        cost_estimate=BRIEF,
        name="to_rows",
    )(seg)


def dp_place():
    dp = lax.axis_index("dp")
    return dp, dp % 2, (dp // 2) % 2, dp // 4


def greet_all(plan, dp, mp):
    barrier = pltpu.get_barrier_semaphore()
    others = [(dp, lax.rem(mp + k, plan.m)) for k in range(1, plan.m)]
    others += [(lax.rem(dp + k, plan.n), mp) for k in range(1, plan.n)]
    for other in others:
        pl.semaphore_signal(barrier, inc=1, device_id=other, device_id_type=MESH)
    pl.semaphore_wait(barrier, len(others))


def remote(source, target, send, recv, device):
    copy = pltpu.make_async_remote_copy(
        src_ref=source,
        dst_ref=target,
        send_sem=send,
        recv_sem=recv,
        device_id=device,
        device_id_type=MESH,
    )
    copy.start()
    return copy


def weave_kernel(plan, shard, gain, out, gain_out, own, *sems):
    z_send, z_recv, x_send, x_recv, y_send, y_recv, c_send, c_recv, g_send, g_recv = sems
    (dp, core, x, y), mp = dp_place(), lax.axis_index("mp")
    types, rows = shard.shape[:2]
    half = types // 2
    greet_all(plan, dp, mp)
    beside = dp + 1 - 2 * core
    dp_x, dp_y = dp + 2 - 4 * x, dp + 4 - 8 * y
    dp_xy = dp_x + 4 - 8 * y

    def block(index, column, first=0, count=types):
        z = lax.rem(mp + plan.m - index, plan.m)
        place = pl.ds(pl.multiple_of(z * rows, rows), rows)
        return out.at[pl.ds(first, count), place, columns(column)]

    def pass_on(index, column, sems, slot, device, first=0, count=types):
        region = block(index, column, first, count)
        return remote(
            region, region, sems[0].at[index, slot], sems[1].at[index, slot], (device, mp)
        )

    locals_ = [
        pltpu.make_async_copy(shard, block(0, dp), own.at[0]),
        pltpu.make_async_copy(gain, gain_out.at[:, columns(dp)], own.at[1]),
    ]
    for copy in locals_:
        copy.start()
    z_copies = [None]
    for k in range(1, plan.m):
        z_copies.append(
            remote(shard, block(0, dp), z_send.at[k], z_recv.at[k], (dp, lax.rem(mp + k, plan.m)))
        )
    copies = [
        remote(
            gain,
            gain_out.at[:, columns(dp)],
            g_send.at[k],
            g_recv.at[k],
            (lax.rem(dp + k, plan.n), mp),
        )
        for k in range(1, plan.n)
    ]
    x_sems, y_sems, c_sems = (x_send, x_recv), (y_send, y_recv), (c_send, c_recv)
    x_own, y_own, x_far, y_far, c_all = [], [], [], [], []

    def first_stage(index):
        if index == 0:
            for copy in locals_:
                copy.wait()
        else:
            z_copies[index].wait_recv()
        x_own.append(pass_on(index, dp, x_sems, 0, dp_x))
        y_own.append(pass_on(index, dp, y_sems, 0, dp_y))
        c_all.append(pass_on(index, dp, c_sems, 0, beside))

    def second_stage(index):
        x_own[index].wait_recv()
        y_far.append(pass_on(index, dp_x, y_sems, 1, dp_y, 0, half))
        c_all.append(pass_on(index, dp_x, c_sems, 1, beside))
        y_own[index].wait_recv()
        x_far.append(pass_on(index, dp_y, x_sems, 1, dp_x, half, types - half))
        c_all.append(pass_on(index, dp_y, c_sems, 2, beside))

    def third_stage(index):
        y_far[index].wait_recv()
        c_all.append(pass_on(index, dp_xy, c_sems, 3, beside, 0, half))
        x_far[index].wait_recv()
        c_all.append(pass_on(index, dp_xy, c_sems, 4, beside, half, types - half))

    for step in range(plan.m + 2):
        if step < plan.m:
            first_stage(step)
        if 1 <= step < plan.m + 1:
            second_stage(step - 1)
        if step >= 2:
            third_stage(step - 2)
    for copy in copies + c_all:
        copy.wait()
    for copy in z_copies[1:] + x_own + y_own + x_far + y_far:
        copy.wait_send()


def weave(plan, shard, gain):
    types, rows = shard.shape[:2]
    dma = pltpu.SemaphoreType.DMA
    return pl.pallas_call(
        functools.partial(weave_kernel, plan),
        in_specs=[ANY, ANY],
        out_specs=(ANY, ANY),
        out_shape=(
            jax.ShapeDtypeStruct((types, plan.m * rows, D), jnp.bfloat16),
            jax.ShapeDtypeStruct((gain.shape[0], D), jnp.bfloat16),
        ),
        scratch_shapes=[dma((2,))]
        + [dma((plan.m,))] * 2
        + [dma((plan.m, 2))] * 4
        + [dma((plan.m, 5))] * 2
        + [dma((plan.n,))] * 2,
        compiler_params=pltpu.CompilerParams(collective_id=6, has_side_effects=True),
        cost_estimate=BRIEF,
        name="weave",
    )(shard, gain)


def shed_kernel(plan, normed, dq, dk, dv, extra, out, left, parts, from_core, sums, *rest):
    from_first, sums_first, from_second, blocks, from_z, c_sems, f_sems, s_sems, z_sems = rest
    (dp, core, x, y), mp = dp_place(), lax.axis_index("mp")
    width = D // plan.n
    wide = D // 2
    greet_all(plan, dp, mp)
    beside, dp_x, dp_y = dp + 1 - 2 * core, dp + 2 - 4 * x, dp + 4 - 8 * y

    def rows_of(index):
        return pl.ds(pl.multiple_of(index * width, width), width)

    def plus(one, other):
        return (one.astype(jnp.float32) + other.astype(jnp.float32)).astype(jnp.bfloat16)

    left[...] = normed[...].T
    c_copies, first, second = [], [], []
    for half in range(2):
        for kind, array in enumerate((dq, dk, dv)):
            place = slice(kind * wide, (kind + 1) * wide)
            source = slice(half * wide, (half + 1) * wide)
            parts[half, :, place] = nn(left[...], array[:, source]).astype(jnp.bfloat16)
        parts[half, :, 3 * wide :] = extra[...].astype(jnp.bfloat16)
        c_copies.append(
            [
                remote(
                    parts.at[half, rows_of(2 * j + 1 - core)],
                    from_core.at[half, j],
                    c_sems.at[0, half, j],
                    c_sems.at[1, half, j],
                    (beside, mp),
                )
                for j in range(4)
            ]
        )
    for half in range(2):
        for j in range(4):
            c_copies[half][j].wait_recv()
            sums[half, j] = plus(parts[half, rows_of(2 * j + core), :], from_core[half, j])
        for k in range(2):
            away = 2 * k + 1 - x if half == 0 else 2 * (1 - y) + k
            first.append(
                remote(
                    sums.at[half, away],
                    from_first.at[half, k],
                    f_sems.at[0, half, k],
                    f_sems.at[1, half, k],
                    (dp_x if half == 0 else dp_y, mp),
                )
            )
    for half in range(2):
        for k in range(2):
            first[2 * half + k].wait_recv()
            kept = 2 * k + x if half == 0 else 2 * y + k
            sums_first[half, k] = plus(sums[half, kept], from_first[half, k])
        second.append(
            remote(
                sums_first.at[half, 1 - y if half == 0 else 1 - x],
                from_second.at[half],
                s_sems.at[0, half],
                s_sems.at[1, half],
                (dp_y if half == 0 else dp_x, mp),
            )
        )
    piece = D // plan.m
    for half in range(2):
        second[half].wait_recv()
        total = plus(sums_first[half, y if half == 0 else x], from_second[half])
        for member in range(2):
            index = 2 * half + member
            for kind in range(3):
                start = kind * wide + member * piece
                blocks[index, :, kind * piece : (kind + 1) * piece] = total[:, start : start + piece]
            blocks[index, :, 3 * piece :] = total[:, 3 * wide :]
    z_copies = []
    for k in range(1, plan.m):
        peer = lax.rem(mp + k, plan.m)
        z_copies.append(
            remote(
                blocks.at[peer], from_z.at[k], z_sems.at[0, k], z_sems.at[1, k], (dp, peer)
            )
        )
    result = blocks[mp].astype(jnp.float32)
    for k in range(1, plan.m):
        z_copies[k - 1].wait_recv()
        result = result + from_z[k].astype(jnp.float32)
    out[...] = result
    for copy in c_copies[0] + c_copies[1] + first + second + z_copies:
        copy.wait_send()


def shed(plan, normed, dqkv, extra):
    dma = pltpu.SemaphoreType.DMA
    width, wide, kept = D // plan.n, 3 * (D // 2) + LANES, 3 * (D // plan.m) + LANES

    def held(*shape):
        return pltpu.VMEM(shape, jnp.bfloat16)

    return pl.pallas_call(
        functools.partial(shed_kernel, plan),
        in_specs=[VMEM] * 5,
        out_specs=VMEM,
        out_shape=jax.ShapeDtypeStruct((width, kept), jnp.float32),
        scratch_shapes=[
            held(D, normed.shape[0]),
            held(2, D, wide),
            held(2, 4, width, wide),
            held(2, 4, width, wide),
            held(2, 2, width, wide),
            held(2, 2, width, wide),
            held(2, width, wide),
            held(plan.m, width, kept),
            held(plan.m, width, kept),
            dma((2, 2, 4)),
            dma((2, 2, 2)),
            dma((2, 2)),
            dma((2, plan.m)),
        ],
        compiler_params=pltpu.CompilerParams(
            collective_id=7, has_side_effects=True, vmem_limit_bytes=BIG_VMEM
        ),
        cost_estimate=BRIEF,
        name="shed",
    )(normed, *dqkv, extra)


def products_kernel(plan, sides, *refs):
    rows_in, refs = refs[0], refs[1:]
    lefts, rights = refs[: len(set(sides))], refs[len(set(sides)) : len(set(sides)) + len(sides)]
    seg, out, left_sides, tiles, send, recv, own, sent = refs[len(lefts) + len(rights) :]
    segment, member = plan.here()
    rows = plan.rows
    greet(plan, segment, member)

    def source(peer):
        return rows_in.at[:, columns(peer)]

    place = seg.at[pl.ds(pl.multiple_of(member * rows, rows), rows)]
    copies = member_copies(plan, segment, member, source, place, send, recv, own)
    for index, array in enumerate(lefts):
        left_sides[index] = array[...].T
    start, pending = 0, [None, None]
    slot = 0
    for array, side in zip(rights, sides):
        size = array.shape[1]
        width = size // 2 if size % (2 * LANES) == 0 and size > D else D
        for first in range(0, size, width):
            if pending[slot] is not None:
                pending[slot].wait()
            tiles[slot, :, :width] = nn(
                left_sides[side], array[:, first : first + width]
            ).astype(jnp.bfloat16)
            pending[slot] = pltpu.make_async_copy(
                tiles.at[slot, :, :width], out.at[:, pl.ds(start, width)], sent.at[slot]
            )
            pending[slot].start()
            start += width
            slot = 1 - slot
    for copy in pending + copies:
        copy.wait()


def products(plan, rows_in, lefts, rights, sides):
    rows, widest = lefts[0].shape[0], max(array.shape[1] for array in rights) // 2
    total = sum(array.shape[1] for array in rights)
    return pl.pallas_call(
        functools.partial(products_kernel, plan, sides),
        in_specs=[ANY] + [VMEM] * (len(lefts) + len(rights)),
        out_specs=(ANY, ANY),
        out_shape=(
            jax.ShapeDtypeStruct((plan.seg_rows, LANES), jnp.bfloat16),
            jax.ShapeDtypeStruct((D, total), jnp.bfloat16),
        ),
        scratch_shapes=[
            pltpu.VMEM((len(lefts), D, rows), jnp.bfloat16),
            pltpu.VMEM((2, D, widest), jnp.bfloat16),
            pltpu.SemaphoreType.DMA((plan.group,)),
            pltpu.SemaphoreType.DMA((plan.group,)),
            pltpu.SemaphoreType.DMA,
            pltpu.SemaphoreType.DMA((2,)),
        ],
        compiler_params=pltpu.CompilerParams(
            collective_id=len(lefts), has_side_effects=True, vmem_limit_bytes=BIG_VMEM
        ),
        cost_estimate=BRIEF,
        name="products",
    )(rows_in, *lefts, *rights)


def collect_kernel(plan, spans, more, *refs):
    parts = 1 if spans == 0 else 2
    arrays, halos, refs = refs[:parts], refs[parts : parts * (1 + spans)], refs[parts * (1 + spans) :]
    beside, refs = refs[:more], refs[more:]
    outs, refs = refs[:parts], refs[parts:]
    total, send, recv, own = refs[-4:]
    segment, member = plan.here()
    rows = plan.rows
    greet(plan, segment, member)
    copies = []
    for part, array in enumerate(arrays):
        if spans:
            for piece in range(plan.seg_rows // CHUNK):
                start = piece * CHUNK
                value = array[pl.ds(start, CHUNK), :]
                for index, (distance, first, count) in enumerate(plan.spans):
                    offset = start - (plan.seg_rows - count)
                    if offset >= 0:
                        halo = halos[part * spans + index][pl.ds(offset, CHUNK), :]
                        value = value + halo.astype(jnp.float32)
                total[part, pl.ds(start, CHUNK), :] = value.astype(jnp.bfloat16)
            array = total.at[part]

        def source(peer, array=array):
            return array.at[pl.ds(pl.multiple_of(peer * rows, rows), rows)]

        copies += member_copies(
            plan,
            segment,
            member,
            source,
            outs[part].at[:, columns(member)],
            send.at[part],
            recv.at[part],
            own.at[part],
        )
    if beside:
        (hidden, weights, middle), (final, down, loaded) = beside, refs[:3]
        load = pltpu.make_async_copy(weights.at[2], down, loaded)
        load.start()
        load.wait()
        for first in range(0, D, TILE):
            place = slice(first, first + TILE)
            final[:, place] = (middle[:, place] + nn(hidden[...], down[:, place])).astype(
                jnp.bfloat16
            )
    for copy in copies:
        copy.wait()


def collect(plan, arrays, halos, beside=()):
    parts, spans = len(arrays), len(plan.spans) if halos else 0
    return pl.pallas_call(
        functools.partial(collect_kernel, plan, spans, len(beside)),
        out_shape=(jax.ShapeDtypeStruct((plan.rows, D), jnp.bfloat16),) * (parts + bool(beside)),
        in_specs=[VMEM] * (parts + len(halos)) + [VMEM, ANY, VMEM][: len(beside)],
        out_specs=(ANY,) * parts + (VMEM,) * bool(beside),
        scratch_shapes=[pltpu.VMEM(one.shape[1:], one.dtype) for one in beside[1:2]]
        + [pltpu.SemaphoreType.DMA] * bool(beside)
        + [
            pltpu.VMEM((parts, plan.seg_rows if halos else 16, LANES), jnp.bfloat16),
            pltpu.SemaphoreType.DMA((parts, plan.group)),
            pltpu.SemaphoreType.DMA((parts, plan.group)),
            pltpu.SemaphoreType.DMA((parts,)),
        ],
        compiler_params=pltpu.CompilerParams(
            collective_id=5 if halos else 9 if beside else 8, has_side_effects=True, vmem_limit_bytes=BIG_VMEM
        ),
        cost_estimate=BRIEF,
        name="collect_kv" if halos else "collect_q",
    )(*arrays, *halos, *beside)


def swap_halves(values):
    lane = lax.broadcasted_iota(jnp.int32, values.shape, 1)
    half = HEAD_DIM // 2
    ahead = pltpu.roll(values, LANES - half, 1)
    behind = pltpu.roll(values, half, 1)
    return jnp.where(lax.rem(lane, HEAD_DIM) < half, ahead, behind)


def rotate(values, cosine, sine):
    return values * cosine + swap_halves(values) * sine


def of_head(values, head):
    lane = lax.broadcasted_iota(jnp.int32, values.shape, 1)
    return jnp.where(lane // HEAD_DIM == head, values, jnp.zeros_like(values))


def chunk_rows(index, size):
    return pl.ds(pl.multiple_of(index * size, size), size)


HALO_CHUNKS = HALO // CHUNK


def rotate_keys(prior, first, keys, cosine, sine, k_turned):
    def one(index, unused):
        table = chunk_rows(prior[first + index], CHUNK)
        rows = chunk_rows(index, CHUNK)
        k_turned[rows, :] = rotate(
            keys[rows, :].astype(jnp.float32), cosine[table, :], sine[table, :]
        ).astype(jnp.bfloat16)
        return unused

    lax.fori_loop(0, keys.shape[0] // CHUNK, one, 0)


def query_tables(prior, block, cosine, sine):
    rows = chunk_rows(prior[HALO_CHUNKS + block], QUERY_ROWS)
    return cosine[rows, :], sine[rows, :]


def turned_queries(prior, block, queries, cosine, sine):
    cos_rows, sin_rows = query_tables(prior, block, cosine, sine)
    turned = rotate(queries.astype(jnp.float32), cos_rows, sin_rows)
    return (turned * (LOG2E * HEAD_DIM ** (-0.5))).astype(jnp.bfloat16)


def by_head(parts):
    whole = parts[0]
    lane = lax.broadcasted_iota(jnp.int32, whole.shape, 1)
    for head in range(1, HEADS_HELD):
        whole = jnp.where(lane // HEAD_DIM == head, parts[head], whole)
    return whole


def needs_halo(prior, own_chunks):
    needed = prior[HALO_CHUNKS] > 0
    for chunk in range(1, min(own_chunks, HALO_CHUNKS)):
        needed = needed | (prior[HALO_CHUNKS + chunk] > chunk)
    return needed


ROW_PARTS = 4
UNITS = [(head, part) for part in range(ROW_PARTS) for head in range(HEADS_HELD)]


def add_keys(refs, first, diagonal):
    q_head, k_turned, v_wide, top, total = refs
    start_row = pl.multiple_of(first * CHUNK, CHUNK)
    part_rows = QUERY_ROWS // ROW_PARTS

    def queries(part):
        return slice(part * part_rows, (part + 1) * part_rows)

    def keys(part):
        return pl.ds(start_row, (part + 1) * part_rows if diagonal else CHUNK)

    def start(unit):
        head, part = unit
        return nt(q_head[head, queries(part), :], k_turned[keys(part), :])

    def finish(unit, scores):
        head, part = unit
        held = (head, queries(part))
        value_block = v_wide[keys(part), :]
        if diagonal:
            place = lax.broadcasted_iota(jnp.int32, scores.shape, 0) + part * part_rows
            other = lax.broadcasted_iota(jnp.int32, scores.shape, 1)
            scores = jnp.where(other <= place, scores, MASKED)
        highest = jnp.max(scores, axis=1, keepdims=True)
        if diagonal:
            weights = jnp.exp2((scores - highest).astype(jnp.bfloat16))
            total[held] = nn(weights, value_block)
            top[held] = jnp.broadcast_to(highest, (part_rows, LANES))
        else:
            before = top[held]
            after = jnp.maximum(before, highest)
            weights = jnp.exp2((scores - after[:, :1]).astype(jnp.bfloat16))
            shrink = jnp.exp2(before - after)
            shrink = jnp.concatenate([shrink, shrink], axis=1)
            total[held] = total[held] * shrink + nn(weights, value_block)
            top[held] = after

    scores = start(UNITS[0])
    for index, unit in enumerate(UNITS):
        following = start(UNITS[index + 1]) if index + 1 < len(UNITS) else None
        finish(unit, scores)
        scores = following


def mixed_of(total):
    return by_head([total[head, :, :LANES] / total[head, :, LANES:] for head in range(HEADS_HELD)])


def attend_own_kernel(
    prior, q_ref, keys, values, cosine, sine, out_ref, top_ref, sum_ref, *scratch
):
    k_turned, v_wide, q_head, top, total = scratch
    block = pl.program_id(0)

    @pl.when(block == 0)
    def _():
        rotate_keys(prior, HALO_CHUNKS, keys, cosine, sine, k_turned)
        v_wide[:, :LANES] = values[...]
        v_wide[:, LANES:] = jnp.ones((values.shape[0], LANES), jnp.bfloat16)

    turned = turned_queries(prior, block, q_ref[...], cosine, sine)
    for head in range(HEADS_HELD):
        q_head[head] = of_head(turned, head)
    held = (q_head, k_turned, v_wide, top, total)
    add_keys(held, block, True)

    def earlier_chunk(index, unused):
        add_keys(held, block - 1 - index, False)
        return unused

    lax.fori_loop(0, jnp.minimum(prior[HALO_CHUNKS + block], block), earlier_chunk, 0)
    out_ref[...] = mixed_of(total).astype(jnp.bfloat16)
    top_ref[...] = by_head([top[head] for head in range(HEADS_HELD)])
    sum_ref[...] = by_head([total[head, :, LANES:] for head in range(HEADS_HELD)])


def attend_own(prior, q_seg, keys, values, cosine, sine):
    seg_rows = q_seg.shape[0]
    query_spec = pl.BlockSpec((QUERY_ROWS, LANES), lambda i, prior: (i, 0))
    wide = jax.ShapeDtypeStruct((seg_rows, LANES), jnp.float32)
    return pl.pallas_call(
        attend_own_kernel,
        grid_spec=pltpu.PrefetchScalarGridSpec(
            num_scalar_prefetch=1,
            grid=(seg_rows // QUERY_ROWS,),
            in_specs=[query_spec, VMEM, VMEM, VMEM, VMEM],
            out_specs=(query_spec,) * 3,
            scratch_shapes=[
                pltpu.VMEM((seg_rows, LANES), jnp.bfloat16),
                pltpu.VMEM((seg_rows, 2 * LANES), jnp.bfloat16),
                pltpu.VMEM((HEADS_HELD, QUERY_ROWS, LANES), jnp.bfloat16),
                pltpu.VMEM((HEADS_HELD, QUERY_ROWS, LANES), jnp.float32),
                pltpu.VMEM((HEADS_HELD, QUERY_ROWS, 2 * LANES), jnp.float32),
            ],
        ),
        out_shape=(jax.ShapeDtypeStruct((seg_rows, LANES), jnp.bfloat16), wide, wide),
        compiler_params=pltpu.CompilerParams(vmem_limit_bytes=BIG_VMEM),
        cost_estimate=BRIEF,
        name="attend_own",
    )(prior, q_seg, keys, values, cosine, sine)


def copy_in(pairs, sems):
    copies = [
        pltpu.make_async_copy(source, target, sems.at[index])
        for index, (source, target) in enumerate(pairs)
    ]
    for copy in copies:
        copy.start()
    for copy in copies:
        copy.wait()


def attend_halo_kernel(
    own_chunks, prior, q_seg, keys, values, cos_hbm, sin_hbm, out_in, top_in, sum_in,
    out, top_out, sum_out, *scratch
):
    k_turned, v_wide, q_head, top, total, key_rows, value_rows, cosine, sine = scratch[:9]
    q_rows, out_rows, top_rows, sum_rows, sems = scratch[9:]

    def one_block(block, unused):
        count = prior[HALO_CHUNKS + block] - block
        rows = chunk_rows(block, QUERY_ROWS)

        @pl.when(count > 0)
        def _():
            turned = turned_queries(prior, block, q_rows[rows, :], cosine, sine)
            mixed, tops, sums = out_rows[rows, :], top_rows[rows, :], sum_rows[rows, :]
            for head in range(HEADS_HELD):
                lane = head * HEAD_DIM
                q_head[head] = of_head(turned, head)
                top[head] = jnp.broadcast_to(tops[:, lane : lane + 1], top.shape[1:])
                weight = jnp.broadcast_to(sums[:, lane : lane + 1], top.shape[1:])
                total[head, :, :LANES] = mixed.astype(jnp.float32) * weight
                total[head, :, LANES:] = weight

            def earlier_chunk(index, unused):
                held = (q_head, k_turned, v_wide, top, total)
                add_keys(held, HALO_CHUNKS - 1 - index, False)
                return unused

            lax.fori_loop(0, count, earlier_chunk, 0)
            out_rows[rows, :] = mixed_of(total).astype(jnp.bfloat16)
            top_rows[rows, :] = by_head([top[head] for head in range(HEADS_HELD)])
            sum_rows[rows, :] = by_head([total[head, :, LANES:] for head in range(HEADS_HELD)])

        return unused

    @pl.when(needs_halo(prior, own_chunks))
    def _():
        part = pl.ds(0, q_rows.shape[0])
        held = ((out, out_rows), (top_out, top_rows), (sum_out, sum_rows))
        copy_in(
            (
                (keys, key_rows), (values, value_rows), (cos_hbm, cosine), (sin_hbm, sine),
                (q_seg.at[part], q_rows), *((hbm.at[part], rows) for hbm, rows in held),
            ),
            sems,
        )
        rotate_keys(prior, 0, key_rows, cosine, sine, k_turned)
        v_wide[:, :LANES] = value_rows[...]
        v_wide[:, LANES:] = jnp.ones((value_rows.shape[0], LANES), jnp.bfloat16)
        lax.fori_loop(0, q_rows.shape[0] // QUERY_ROWS, one_block, 0)
        copy_in([(rows, hbm.at[part]) for hbm, rows in held], sems)


def attend_halo(prior, q_seg, keys, values, cosine, sine, earlier):
    part = (min(q_seg.shape[0], HALO), LANES)
    per_head = (HEADS_HELD, QUERY_ROWS, LANES)
    return pl.pallas_call(
        functools.partial(attend_halo_kernel, q_seg.shape[0] // CHUNK),
        in_specs=[SMEM] + [ANY] * 8,
        out_specs=(ANY,) * 3,
        out_shape=tuple(jax.ShapeDtypeStruct(one.shape, one.dtype) for one in earlier),
        scratch_shapes=[
            pltpu.VMEM((HALO, LANES), jnp.bfloat16),
            pltpu.VMEM((HALO, 2 * LANES), jnp.bfloat16),
            pltpu.VMEM(per_head, jnp.bfloat16),
            pltpu.VMEM(per_head, jnp.float32),
            pltpu.VMEM((HEADS_HELD, QUERY_ROWS, 2 * LANES), jnp.float32),
            pltpu.VMEM((HALO, LANES), jnp.bfloat16),
            pltpu.VMEM((HALO, LANES), jnp.bfloat16),
            pltpu.VMEM((LONGEST, LANES), jnp.float32),
            pltpu.VMEM((LONGEST, LANES), jnp.float32),
            pltpu.VMEM(part, jnp.bfloat16),
            pltpu.VMEM(part, jnp.bfloat16),
            pltpu.VMEM(part, jnp.float32),
            pltpu.VMEM(part, jnp.float32),
            pltpu.SemaphoreType.DMA((8,)),
        ],
        input_output_aliases={6: 0, 7: 1, 8: 2},
        compiler_params=pltpu.CompilerParams(vmem_limit_bytes=BIG_VMEM),
        cost_estimate=BRIEF,
        name="attend_halo",
    )(prior, q_seg, keys, values, cosine, sine, *earlier)


def prepare_back(refs, block, prior, queries, grads, mixed, tops, sums, cosine, sine):
    q_head, grad_head, row_stats = refs
    turned = turned_queries(prior, block, queries, cosine, sine)
    grads = grads.astype(jnp.float32) / sums
    dots = (grads * mixed.astype(jnp.float32)).T
    tops = tops.T
    grads = grads.astype(jnp.bfloat16)
    for head in range(HEADS_HELD):
        q_head[head] = of_head(turned, head)
        grad_head[head] = of_head(grads, head)
        lanes = slice(head * HEAD_DIM, (head + 1) * HEAD_DIM)
        row_stats[head, 0:1, :] = tops[head * HEAD_DIM : head * HEAD_DIM + 1, :]
        row_stats[head, 1:2, :] = jnp.sum(dots[lanes, :], axis=0, keepdims=True)


def add_keys_back(refs, first, diagonal):
    q_head, grad_head, row_stats, k_turned, values, dq_total, dk_total, dv_total = refs
    part_rows = QUERY_ROWS // ROW_PARTS

    def keys(part):
        start = pl.multiple_of(first * CHUNK + part * part_rows, part_rows)
        return pl.ds(start, part_rows)

    def queries(part):
        return slice(part * part_rows if diagonal else 0, QUERY_ROWS)

    def start(unit):
        head, part = unit
        rows, wanted = keys(part), queries(part)
        return (
            nt(k_turned[rows, :], q_head[head, wanted, :]),
            nt(values[rows, :], grad_head[head, wanted, :]),
        )

    def finish(unit, products_):
        head, part = unit
        rows, wanted = keys(part), queries(part)
        scores, grad_weights = products_
        weights = jnp.exp2((scores - row_stats[head, 0:1, wanted]).astype(jnp.bfloat16))
        if diagonal:
            other = lax.broadcasted_iota(jnp.int32, scores.shape, 0)
            place = lax.broadcasted_iota(jnp.int32, scores.shape, 1)
            weights = jnp.where(other <= place, weights, jnp.zeros_like(weights))
        grad_scores = weights * (grad_weights - row_stats[head, 1:2, wanted]).astype(jnp.bfloat16)
        dv_total[rows, :] += nn(weights, grad_head[head, wanted, :])
        dk_total[rows, :] += nn(grad_scores, q_head[head, wanted, :])
        dq_total[head, wanted, :] += tn(grad_scores, k_turned[rows, :])

    held = start(UNITS[0])
    for index, unit in enumerate(UNITS):
        following = start(UNITS[index + 1]) if index + 1 < len(UNITS) else None
        finish(unit, held)
        held = following


def turn_keys_back(prior, first_chunk, dk_total, dv_total, cosine, sine, dk_ref, dv_ref):
    def one(index, unused):
        table = chunk_rows(prior[first_chunk + index], CHUNK)
        rows = chunk_rows(index, CHUNK)
        turned = rotate(dk_total[rows, :], cosine[table, :], -sine[table, :]) * (1.0 / LOG2E)
        dk_ref[rows, :] = turned.astype(dk_ref.dtype)
        dv_ref[rows, :] = dv_total[rows, :].astype(dv_ref.dtype)
        return unused

    lax.fori_loop(0, dk_ref.shape[0] // CHUNK, one, 0)


def attend_back_own_kernel(
    prior, q_ref, grad_ref, out_ref, top_ref, sum_ref, keys, values, cosine, sine, dq_part,
    dq_ref, dk_ref, dv_ref, k_turned, q_head, grad_head, dq_total, dk_total, dv_total, row_stats
):
    block = pl.program_id(0)
    chunks_back = prior[HALO_CHUNKS + block]

    @pl.when(block == 0)
    def _():
        rotate_keys(prior, HALO_CHUNKS, keys, cosine, sine, k_turned)
        dk_total[...] = jnp.zeros_like(dk_total)
        dv_total[...] = jnp.zeros_like(dv_total)

    prepare_back(
        (q_head, grad_head, row_stats), block, prior, q_ref[...], grad_ref[...], out_ref[...],
        top_ref[...], sum_ref[...], cosine, sine,
    )
    from_halo = jnp.where(chunks_back > block, dq_part[...], jnp.zeros_like(dq_part))
    for head in range(HEADS_HELD):
        dq_total[head] = from_halo
    held = (q_head, grad_head, row_stats, k_turned, values, dq_total, dk_total, dv_total)
    add_keys_back(held, block, True)

    def whole(index, unused):
        add_keys_back(held, index, False)
        return unused

    lax.fori_loop(jnp.maximum(block - chunks_back, 0), block, whole, 0)
    cos_rows, sin_rows = query_tables(prior, block, cosine, sine)
    turned = rotate(by_head([dq_total[head] for head in range(HEADS_HELD)]), cos_rows, -sin_rows)
    dq_ref[...] = (turned * HEAD_DIM ** (-0.5)).astype(jnp.bfloat16)

    @pl.when(block == pl.num_programs(0) - 1)
    def _():
        turn_keys_back(prior, HALO_CHUNKS, dk_total, dv_total, cosine, sine, dk_ref, dv_ref)


def back_scratch(key_rows):
    per_head = (HEADS_HELD, QUERY_ROWS, LANES)
    return [
        pltpu.VMEM((key_rows, LANES), jnp.bfloat16),
        pltpu.VMEM(per_head, jnp.bfloat16),
        pltpu.VMEM(per_head, jnp.bfloat16),
        pltpu.VMEM(per_head, jnp.float32),
        pltpu.VMEM((key_rows, LANES), jnp.float32),
        pltpu.VMEM((key_rows, LANES), jnp.float32),
        pltpu.VMEM((HEADS_HELD, 8, QUERY_ROWS), jnp.float32),
    ]


def attend_back_own(prior, q_seg, grad_seg, seen, keys, values, cosine, sine, dq_part):
    seg_rows = q_seg.shape[0]
    query_spec = pl.BlockSpec((QUERY_ROWS, LANES), lambda i, prior: (i, 0))
    wide = jax.ShapeDtypeStruct((seg_rows, LANES), jnp.float32)
    return pl.pallas_call(
        attend_back_own_kernel,
        grid_spec=pltpu.PrefetchScalarGridSpec(
            num_scalar_prefetch=1,
            grid=(seg_rows // QUERY_ROWS,),
            in_specs=[query_spec] * 5 + [VMEM] * 4 + [query_spec],
            out_specs=(query_spec, VMEM, VMEM),
            scratch_shapes=back_scratch(seg_rows),
        ),
        out_shape=(jax.ShapeDtypeStruct((seg_rows, LANES), jnp.bfloat16), wide, wide),
        compiler_params=pltpu.CompilerParams(vmem_limit_bytes=BIG_VMEM),
        cost_estimate=BRIEF,
        name="attend_back_own",
    )(prior, q_seg, grad_seg, *seen, keys, values, cosine, sine, dq_part)


def attend_back_halo_kernel(
    own_chunks, prior, q_seg, grad_seg, mixed, tops, sums, keys, values, cos_hbm, sin_hbm,
    dq_out, dk_out, dv_out, *scratch
):
    k_turned, q_head, grad_head, dq_total, dk_total, dv_total, row_stats = scratch[:7]
    key_rows, value_rows, cosine, sine, dk_half, dv_half = scratch[7:13]
    q_rows, grad_rows, out_rows, top_rows, sum_rows, dq_rows, sems = scratch[13:]
    needed = needs_halo(prior, own_chunks)
    part = pl.ds(0, q_rows.shape[0])

    def one_block(block, unused):
        chunks_back = prior[HALO_CHUNKS + block]
        rows = chunk_rows(block, QUERY_ROWS)

        @pl.when(chunks_back > block)
        def _():
            prepare_back(
                (q_head, grad_head, row_stats), block, prior, q_rows[rows, :], grad_rows[rows, :],
                out_rows[rows, :], top_rows[rows, :], sum_rows[rows, :], cosine, sine,
            )
            dq_total[...] = jnp.zeros_like(dq_total)

            def whole(index, unused):
                add_keys_back(
                    (
                        q_head, grad_head, row_stats, k_turned, value_rows, dq_total, dk_total,
                        dv_total,
                    ),
                    index,
                    False,
                )
                return unused

            lax.fori_loop(HALO_CHUNKS + block - chunks_back, HALO_CHUNKS, whole, 0)
            dq_rows[rows, :] = by_head([dq_total[head] for head in range(HEADS_HELD)])

        return unused

    @pl.when(needed)
    def _():
        copy_in(
            (
                (keys, key_rows), (values, value_rows), (cos_hbm, cosine), (sin_hbm, sine),
                (q_seg.at[part], q_rows), (grad_seg.at[part], grad_rows),
                (mixed.at[part], out_rows), (tops.at[part], top_rows), (sums.at[part], sum_rows),
            ),
            sems,
        )
        rotate_keys(prior, 0, key_rows, cosine, sine, k_turned)
        dk_total[...] = jnp.zeros_like(dk_total)
        dv_total[...] = jnp.zeros_like(dv_total)
        lax.fori_loop(0, q_rows.shape[0] // QUERY_ROWS, one_block, 0)
        turn_keys_back(prior, 0, dk_total, dv_total, cosine, sine, dk_half, dv_half)
        copy_in(((dq_rows, dq_out.at[part]),), sems)

    @pl.when(jnp.logical_not(needed))
    def _():
        dk_half[...] = jnp.zeros_like(dk_half)
        dv_half[...] = jnp.zeros_like(dv_half)

    copy_in(((dk_half, dk_out), (dv_half, dv_out)), sems)


def attend_back_halo(prior, q_seg, grad_seg, seen, keys, values, cosine, sine):
    seg_rows = q_seg.shape[0]
    part = (min(seg_rows, HALO), LANES)
    half = jax.ShapeDtypeStruct((HALO, LANES), jnp.bfloat16)
    return pl.pallas_call(
        functools.partial(attend_back_halo_kernel, seg_rows // CHUNK),
        in_specs=[SMEM] + [ANY] * 9,
        out_specs=(ANY,) * 3,
        out_shape=(jax.ShapeDtypeStruct((seg_rows, LANES), jnp.float32), half, half),
        scratch_shapes=back_scratch(HALO)
        + [
            pltpu.VMEM((HALO, LANES), jnp.bfloat16),
            pltpu.VMEM((HALO, LANES), jnp.bfloat16),
            pltpu.VMEM((LONGEST, LANES), jnp.float32),
            pltpu.VMEM((LONGEST, LANES), jnp.float32),
            pltpu.VMEM((HALO, LANES), jnp.bfloat16),
            pltpu.VMEM((HALO, LANES), jnp.bfloat16),
            pltpu.VMEM(part, jnp.bfloat16),
            pltpu.VMEM(part, jnp.bfloat16),
            pltpu.VMEM(part, jnp.bfloat16),
            pltpu.VMEM(part, jnp.float32),
            pltpu.VMEM(part, jnp.float32),
            pltpu.VMEM(part, jnp.float32),
            pltpu.SemaphoreType.DMA((9,)),
        ],
        compiler_params=pltpu.CompilerParams(vmem_limit_bytes=BIG_VMEM),
        cost_estimate=BRIEF,
        name="attend_back_halo",
    )(prior, q_seg, grad_seg, *seen, keys, values, cosine, sine)


def attention(plan, tables, q_seg, k_seg, v_seg):
    k_halo, v_halo = halo_of(plan, k_seg), halo_of(plan, v_seg)
    earlier = attend_own(tables[0], q_seg, k_seg, v_seg, *tables[1:])
    seen = attend_halo(tables[0], q_seg, k_halo, v_halo, *tables[1:], earlier)
    return seen[0], (q_seg, k_seg, v_seg, k_halo, v_halo, seen)


def attention_back(plan, tables, kept, grad_seg, waiting, beside=()):
    q_seg, k_seg, v_seg, k_halo, v_halo, seen = kept
    queries = (tables[0], q_seg, grad_seg, seen)
    dq_part, dk_halo, dv_halo = attend_back_halo(*queries, k_halo, v_halo, *tables[1:])
    halos = halo_back(plan, dk_halo) + halo_back(plan, dv_halo)
    dq_part, waiting = lax.optimization_barrier((dq_part, waiting))
    dq, dk_own, dv_own = attend_back_own(*queries, k_seg, v_seg, *tables[1:], dq_part)
    dq, *final = collect(plan, (dq,), (), beside)
    dq, *halos = lax.optimization_barrier((dq, *halos))
    return (dq, *collect(plan, (dk_own, dv_own), halos)), waiting, *final


def rotary_tables():
    half = HEAD_DIM // 2
    lane = jnp.arange(LANES)
    frequency = jnp.exp(
        (lane % half).astype(jnp.float32) * (-2.0 * math.log(10000.0) / HEAD_DIM)
    )
    sign = jnp.where(lane % HEAD_DIM < half, -1.0, 1.0).astype(jnp.float32)
    step = 64
    fine = jnp.arange(step).astype(jnp.float32)[:, None] * frequency[None, :]
    coarse = jnp.arange(0, LONGEST, step).astype(jnp.float32)[:, None] * frequency[None, :]
    cos_fine, sin_fine, cos_coarse, sin_coarse = lax.optimization_barrier(
        (jnp.cos(fine), jnp.sin(fine), jnp.cos(coarse), jnp.sin(coarse))
    )
    cosine = cos_coarse[:, None] * cos_fine[None] - sin_coarse[:, None] * sin_fine[None]
    sine = sin_coarse[:, None] * cos_fine[None] + cos_coarse[:, None] * sin_fine[None]
    return (
        cosine.reshape(LONGEST, LANES),
        (sine * sign).reshape(LONGEST, LANES),
    )


def chunks_before(plan, lengths):
    segment, unused = plan.here()
    count = (HALO + plan.seg_rows) // CHUNK
    places = segment * plan.seg_rows - HALO + CHUNK * jnp.arange(count)
    ends = jnp.cumsum(lengths)
    passed = ends[None, :] <= places[:, None]
    opening = jnp.max(jnp.where(passed, ends[None, :], 0), axis=1)
    return jnp.clip((places - opening) // CHUNK, 0, HALO_CHUNKS).astype(jnp.int32)


def tied(array, *others):
    return lax.optimization_barrier((array, *others))[0]


def attention_pack(weights):
    return jnp.stack([weights[1].T, weights[2].T, weights[3].T, weights[4]])


def feedforward_pack(weights):
    return jnp.stack([weights[6].T, weights[7].T, weights[8]])


def fetch_mp(packs):
    rows = [pack.reshape(-1, pack.shape[-1]) for pack in packs]
    whole = rows[0] if len(rows) == 1 else jnp.concatenate(rows, axis=0)
    return lax.all_gather(whole, "mp", axis=0, tiled=False)


def fetch_dp(whole, first, pack):
    count, rows, width = pack.shape
    members = whole.shape[0]
    part = whole[:, first : first + count * rows].reshape(members, count, rows, width)
    part = part.transpose(1, 0, 2, 3).reshape(count, members * rows, width)
    return lax.all_gather(part, "dp", axis=2, tiled=True)


def turn_kernel(members, sizes, *refs):
    parts, out = refs[:-1], refs[-1]
    index, start, row = 0, 0, 0
    for size in sizes:
        if start == parts[index].shape[1]:
            index, start = index + 1, 0
        turned = parts[index][:, start : start + size].T
        count = size // members
        for member in range(members):
            out[member, row : row + count, :] = turned[member * count : (member + 1) * count, :]
        start += size
        row += count


def mp_blocks(plan, parts, sizes):
    rows = sum(sizes) // plan.m
    if parts[0].shape[0] == LANES:
        return pl.pallas_call(
            functools.partial(turn_kernel, plan.m, sizes),
            in_specs=[VMEM] * len(parts),
            out_specs=VMEM,
            out_shape=jax.ShapeDtypeStruct((plan.m, rows, LANES), jnp.bfloat16),
            compiler_params=pltpu.CompilerParams(vmem_limit_bytes=BIG_VMEM),
            cost_estimate=BRIEF,
            name="turn",
        )(*parts)
    turned, start, pieces = jnp.concatenate(parts, axis=1).T, 0, []
    for size in sizes:
        piece = turned[start : start + size]
        pieces.append(piece.reshape(plan.m, size // plan.m, turned.shape[1]))
        start += size
    return jnp.concatenate(pieces, axis=1)


def reduce_mp(plan, blocks, sizes):
    part = lax.psum_scatter(blocks, "mp", scatter_dimension=0, tiled=False).astype(jnp.float32)
    start, pieces = 0, []
    for size in sizes:
        pieces.append(part[start : start + size // plan.m])
        start += size // plan.m
    return pieces


def reduce_qkv(plan, gradient, extra):
    gradient = jnp.concatenate([gradient, extra.astype(jnp.bfloat16)], axis=1)
    part = lax.psum_scatter(gradient, "dp", scatter_dimension=0, tiled=True)
    width = D // plan.m
    blocks = part[:, : 3 * D].reshape(-1, 3, plan.m, width).transpose(2, 0, 1, 3)
    blocks = blocks.reshape(plan.m, -1, 3 * width)
    shared = jnp.broadcast_to(part[None, :, 3 * D :], (plan.m, part.shape[0], LANES))
    blocks = jnp.concatenate([blocks, shared], axis=2)
    return lax.psum_scatter(blocks, "mp", scatter_dimension=0, tiled=False).astype(jnp.float32)


def project(normed, attention, first_values):
    query, key, fresh = (nt(normed, attention[part]) for part in range(3))
    if first_values is not None:
        fresh = 0.5 * fresh + 0.5 * first_values.astype(jnp.float32)
    return tuple(array.astype(jnp.bfloat16) for array in (query, key, fresh))


def feed_forward(middle, gain, feedforward):
    normed_ff = norm_rows(middle, gain).astype(jnp.bfloat16)
    gate = nt(normed_ff, feedforward[0])
    upward = nt(normed_ff, feedforward[1])
    hidden = (jax.nn.silu(gate) * upward).astype(jnp.bfloat16)
    return normed_ff, gate, upward, hidden


def feed_forward_back(grad_final, middle, gain, weights, stored):
    attention, feedforward = weights
    normed_ff, gate, upward, hidden = stored
    grad_bar = grad_final.astype(jnp.bfloat16)
    grad_hidden = nt(grad_bar, feedforward[2])
    gate_sigmoid = jax.nn.sigmoid(gate)
    grad_gate = (
        grad_hidden * upward * gate_sigmoid * (1.0 + gate * (1.0 - gate_sigmoid))
    ).astype(jnp.bfloat16)
    grad_up = (grad_hidden * gate * gate_sigmoid).astype(jnp.bfloat16)
    grad_normed_ff = nn(grad_gate, feedforward[0]) + nn(grad_up, feedforward[1])
    grad_norm, grad_gain = norm_back(middle, gain, grad_normed_ff)
    grad_middle = grad_final + grad_norm
    middle_bar = grad_middle.astype(jnp.bfloat16)
    grad_mixed = nt(middle_bar, attention[3]).astype(jnp.bfloat16)
    return grad_middle, grad_gain, grad_mixed, (grad_bar, grad_gate, grad_up, middle_bar)


def project_back(grad_middle, stream, gain, attention, dqkv):
    grad_normed = sum(nn(array, attention[part]) for part, array in enumerate(dqkv))
    grad_norm, grad_gain = norm_back(stream, gain, grad_normed)
    return grad_middle + grad_norm, grad_gain


def square_sum(values):
    widened = values.astype(jnp.float32)
    return jnp.sum(widened * widened)


def shards(n, m, inputs, lengths, *rest):
    plan = Plan(n, m)
    first, second, cotangent = rest[:9], rest[9:18], rest[18]
    cosine, sine = rotary_tables()
    tables = (chunks_before(plan, lengths), cosine, sine)
    by_hand = (n, m) == (8, 4)
    gain_shard = jnp.stack([first[0], first[5], second[0], second[5]])
    attention_packs = attention_pack(first), attention_pack(second)
    feedforward_packs = feedforward_pack(first), feedforward_pack(second)
    feedforward_rows = feedforward_packs[0].shape[0] * feedforward_packs[0].shape[1]
    whole = fetch_mp(feedforward_packs)
    if by_hand:
        gain_shard = jnp.pad(gain_shard, ((0, 12), (0, 0)))
        attention_one, gains = weave(plan, attention_packs[0], gain_shard)
        whole = tied(whole, gains)
    else:
        gains = lax.all_gather(gain_shard, "dp", axis=1, tiled=True)
        attention_one = fetch_dp(fetch_mp(attention_packs[:1]), 0, attention_packs[0])
    feedforward_one = fetch_dp(whole, 0, feedforward_packs[0])
    gains = gains[:4].astype(jnp.float32)
    heads, hidden_rows = first[4].shape[0] * m, first[8].shape[0] * m
    rest_sizes = (hidden_rows, hidden_rows, hidden_rows, heads)

    stream = inputs.astype(jnp.float32)
    normed_one = norm_rows(stream, gains[0]).astype(jnp.bfloat16)
    qkv = project(normed_one, attention_one, None)
    values_one = qkv[2]
    q_seg, k_seg, v_seg = spread(plan, *qkv)
    feedforward_one, q_seg, pack_two = lax.optimization_barrier(
        (feedforward_one, q_seg, attention_packs[1])
    )
    whole_two = fetch_mp((pack_two,))
    out_seg, seen_one = attention(plan, tables, q_seg, k_seg, v_seg)
    out_seg, whole_two, whole = lax.optimization_barrier((out_seg, whole_two, whole))
    mixed_one = to_rows(plan, out_seg)
    attention_two = fetch_dp(whole_two, 0, pack_two)
    feedforward_two = fetch_dp(whole, feedforward_rows, feedforward_packs[1])
    middle_one = stream + nn(mixed_one, attention_one[3])
    ff_one = feed_forward(middle_one, gains[1], feedforward_one)
    between = middle_one + nn(ff_one[3], feedforward_one[2])

    normed_two = norm_rows(between, gains[2]).astype(jnp.bfloat16)
    qkv = project(normed_two, attention_two, values_one)
    values_two = qkv[2]
    q_seg, k_seg, v_seg = spread(plan, *qkv)
    out_seg, seen_two = attention(plan, tables, q_seg, k_seg, v_seg)
    mixed_two = to_rows(plan, out_seg)
    middle_two = between + nn(mixed_two, attention_two[3])
    ff_two = feed_forward(middle_two, gains[3], feedforward_two)

    grad_middle, gain_ff_two, grad_mixed, (bar, grad_gate, grad_up, middle_bar) = feed_forward_back(
        cotangent.astype(jnp.float32), middle_two, gains[3], (attention_two, feedforward_two), ff_two
    )
    grad_seg, rest = products(
        plan,
        grad_mixed,
        (bar, ff_two[0], middle_bar),
        (ff_two[3], grad_gate, grad_up, mixed_two),
        (0, 1, 1, 2),
    )
    rest_two = lax.psum_scatter(rest, "dp", scatter_dimension=0, tiled=True)
    dqkv, unused, final = attention_back(
        plan, tables, seen_two, grad_seg, (), (ff_two[3], feedforward_two, middle_two)
    )
    value_extra = 0.5 * dqkv[2].astype(jnp.float32)
    dqkv_two = (dqkv[0], dqkv[1], value_extra.astype(jnp.bfloat16))
    grad_between, gain_two = project_back(
        grad_middle, between, gains[2], attention_two, dqkv_two
    )

    qkv_two = jnp.concatenate(
        [tn(normed_two, array).astype(jnp.bfloat16) for array in dqkv_two], axis=1
    )
    grad_between, qkv_two = lax.optimization_barrier((grad_between, qkv_two))
    qkv_two = lax.psum_scatter(qkv_two, "dp", scatter_dimension=0, tiled=True)
    grad_middle, gain_ff_one, grad_mixed, (bar, grad_gate, grad_up, middle_bar) = feed_forward_back(
        grad_between, middle_one, gains[1], (attention_one, feedforward_one), ff_one
    )
    grad_mixed, rest_two = lax.optimization_barrier((grad_mixed, rest_two))
    grad_seg, rest = products(
        plan,
        grad_mixed,
        (bar, ff_one[0], middle_bar),
        (ff_one[3], grad_gate, grad_up, mixed_one),
        (0, 1, 1, 2),
    )
    rest_one = lax.psum_scatter(rest, "dp", scatter_dimension=0, tiled=True)
    dqkv, qkv_two = attention_back(plan, tables, seen_one, grad_seg, qkv_two)
    grad_values = dqkv[2].astype(jnp.float32) + value_extra
    dqkv_one = (dqkv[0], dqkv[1], grad_values.astype(jnp.bfloat16))
    input_grad, gain_one = project_back(grad_middle, stream, gains[0], attention_one, dqkv_one)
    input_grad, rest_one = lax.optimization_barrier((input_grad, rest_one))
    sizes = rest_sizes + (heads,) * 3 + rest_sizes
    blocks, dqkv_one = lax.optimization_barrier(
        (mp_blocks(plan, (rest_two, qkv_two, rest_one), sizes), dqkv_one)
    )
    reduced = reduce_mp(plan, blocks, sizes)
    down_two, gate_two, up_two, output_two, query_two, key_two, value_two = reduced[:7]
    down_one, gate_one, up_one, output_one = reduced[7:]
    squares = [square_sum(values_one), square_sum(values_two)]
    width = D // n
    own_row = jnp.arange(D) == lax.axis_index("dp") * width
    squares = [jnp.where(own_row, square, 0.0) for square in squares]
    extra = jnp.stack([gain_one, gain_ff_one, gain_two, gain_ff_two, *squares], axis=1)
    extra = jnp.pad(extra, ((0, 0), (0, LANES - extra.shape[1])))
    if by_hand:
        part = shed(plan, normed_one, dqkv_one, extra)
    else:
        whole = [tn(normed_one, array).astype(jnp.bfloat16) for array in dqkv_one]
        part = reduce_qkv(plan, jnp.concatenate(whole, axis=1), extra)
    piece = D // m
    query_one, key_one, value_one = (part[:, i * piece : (i + 1) * piece] for i in range(3))
    shared = part[:, 3 * piece :]
    value_norms = jnp.sqrt(shared[:1, 4:6] / (TOK_DEV * D))
    return (
        between.astype(jnp.bfloat16),
        final,
        input_grad,
        shared[:, 0], query_one, key_one, value_one, output_one,
        shared[:, 1], gate_one.T, up_one.T, down_one,
        shared[:, 2], query_two.T, key_two.T, value_two.T, output_two,
        shared[:, 3], gate_two.T, up_two.T, down_two,
        value_norms,
    )


def solution(mesh):
    tokens, row_split, column_split = P(("dp", "mp"), None), P("dp", "mp"), P("mp", "dp")
    layer = (
        P("dp"), row_split, row_split, row_split, column_split, P("dp"), row_split, row_split,
        column_split,
    )
    return jax.shard_map(
        functools.partial(shards, mesh.shape["dp"], mesh.shape["mp"]),
        mesh=mesh,
        in_specs=(tokens, P(), *layer, *layer, tokens),
        out_specs=(tokens, tokens, tokens, *layer, *layer, P("dp", None)),
        check_vma=False,
    )
```

```python
import functools
import math

import jax
import jax.numpy as jnp
from jax import lax
from jax.experimental import pallas as pl
from jax.experimental.pallas import tpu as pltpu
from jax.sharding import PartitionSpec as P

D = 1024
HEAD_DIM = 64
TOK_DEV = 2048
LONGEST = 4096

LANES = 128
HEADS_HELD = LANES // HEAD_DIM
CHUNK = 1024
HALO = LONGEST - CHUNK
QUERY_ROWS = 1024
TILE = 256
EPSILON = 1e-06
MASKED = -1e30
LOG2E = math.log2(math.e)
MESH = pl.DeviceIdType.MESH
ANY = pl.BlockSpec(memory_space=pl.ANY)
VMEM = pl.BlockSpec(memory_space=pltpu.VMEM)
SMEM = pl.BlockSpec(memory_space=pltpu.SMEM)
BIG_VMEM = 56 * 1024 * 1024
BRIEF = pl.CostEstimate(flops=0, bytes_accessed=1_000, transcendentals=0)


def nn(left_side, right_side):
    return jnp.dot(left_side, right_side, preferred_element_type=jnp.float32)


def tn(left_side, right_side):
    return lax.dot_general(
        left_side, right_side, (((0,), (0,)), ((), ())), preferred_element_type=jnp.float32
    )


def nt(left_side, right_side):
    return lax.dot_general(
        left_side, right_side, (((1,), (1,)), ((), ())), preferred_element_type=jnp.float32
    )


def norm_rows(values, gain_vector):
    scaling = lax.rsqrt(jnp.mean(values * values, axis=-1, keepdims=True) + EPSILON)
    return values * scaling * gain_vector


def norm_back(values, gain_vector, grad_output):
    unused, pullback = jax.vjp(norm_rows, values, gain_vector)
    return pullback(grad_output)


class Plan:
    def __init__(self, n, m):
        self.n, self.m = n, m
        self.group = D // LANES
        self.low = self.group // m
        self.segments = n // self.low
        self.rows = TOK_DEV // m
        self.seg_rows = self.rows * self.group
        self.spans = []
        left, distance = HALO, 1
        while left > 0:
            count = min(self.seg_rows, left)
            self.spans.append((distance, left - count, count))
            left -= count
            distance += 1

    def here(self):
        dp, mp = lax.axis_index("dp"), lax.axis_index("mp")
        return dp // self.low, (dp % self.low) * self.m + mp

    def device(self, segment, member):
        return (segment * self.low + member // self.m, member % self.m)


def greet(plan, segment, member):
    barrier = pltpu.get_barrier_semaphore()
    for offset in range(1, plan.group):
        peer = lax.rem(member + offset, plan.group)
        pl.semaphore_signal(
            barrier, inc=1, device_id=plan.device(segment, peer), device_id_type=MESH
        )
    pl.semaphore_wait(barrier, plan.group - 1)


def member_copies(plan, segment, member, source, target, send, recv, own):
    copies = [pltpu.make_async_copy(source(member), target, own)]
    for offset in range(1, plan.group):
        peer = lax.rem(member + offset, plan.group)
        copies.append(
            pltpu.make_async_remote_copy(
                src_ref=source(peer),
                dst_ref=target,
                send_sem=send.at[offset],
                recv_sem=recv.at[offset],
                device_id=plan.device(segment, peer),
                device_id_type=MESH,
            )
        )
    for copy in copies[1:] + copies[:1]:
        copy.start()
    return copies


def columns(index):
    return pl.ds(pl.multiple_of(index * LANES, LANES), LANES)


def spread_kernel(plan, query, key, value, q_seg, k_seg, v_seg, send, recv, own):
    segment, member = plan.here()
    rows = plan.rows
    greet(plan, segment, member)
    copies = []
    place = pl.ds(pl.multiple_of(member * rows, rows), rows)
    for part, (array, out) in enumerate(((key, k_seg), (value, v_seg), (query, q_seg))):

        def source(peer, array=array):
            return array.at[:, columns(peer)]

        copies += member_copies(
            plan, segment, member, source, out.at[place], send.at[part], recv.at[part], own.at[part]
        )
    for copy in copies:
        copy.wait()


def spread(plan, query, key, value):
    segment = jax.ShapeDtypeStruct((plan.seg_rows, LANES), jnp.bfloat16)
    return pl.pallas_call(
        functools.partial(spread_kernel, plan),
        out_shape=(segment,) * 3,
        in_specs=[ANY] * 3,
        out_specs=(ANY, ANY, ANY),
        scratch_shapes=[
            pltpu.SemaphoreType.DMA((3, plan.group)),
            pltpu.SemaphoreType.DMA((3, plan.group)),
            pltpu.SemaphoreType.DMA((3,)),
        ],
        compiler_params=pltpu.CompilerParams(collective_id=1, has_side_effects=True),
        cost_estimate=BRIEF,
        name="spread",
    )(query, key, value)


def halo_of(plan, seg):
    parts = []
    for distance, first, count in reversed(plan.spans):
        route = [(i, i + distance * plan.low) for i in range(plan.n - distance * plan.low)]
        parts.append(lax.ppermute(seg[plan.seg_rows - count :], "dp", route))
    return parts[0] if len(parts) == 1 else jnp.concatenate(parts, axis=0)


def halo_back(plan, halo):
    parts = []
    for distance, first, count in plan.spans:
        route = [(i, i - distance * plan.low) for i in range(distance * plan.low, plan.n)]
        parts.append(lax.ppermute(halo[:, first : first + count], "dp", route))
    return parts


def to_rows_kernel(plan, seg, rows_out, send, recv, own):
    segment, member = plan.here()
    rows = plan.rows
    greet(plan, segment, member)

    def source(peer):
        return seg.at[pl.ds(pl.multiple_of(peer * rows, rows), rows)]

    for copy in member_copies(
        plan, segment, member, source, rows_out.at[:, columns(member)], send, recv, own
    ):
        copy.wait()


def to_rows(plan, seg):
    return pl.pallas_call(
        functools.partial(to_rows_kernel, plan),
        out_shape=jax.ShapeDtypeStruct((plan.rows, D), jnp.bfloat16),
        in_specs=[ANY],
        out_specs=ANY,
        scratch_shapes=[
            pltpu.SemaphoreType.DMA((plan.group,)),
            pltpu.SemaphoreType.DMA((plan.group,)),
            pltpu.SemaphoreType.DMA,
        ],
        compiler_params=pltpu.CompilerParams(collective_id=2, has_side_effects=True),
        cost_estimate=BRIEF,
        name="to_rows",
    )(seg)


def dp_place():
    dp = lax.axis_index("dp")
    return dp, dp % 2, (dp // 2) % 2, dp // 4


def greet_all(plan, dp, mp):
    barrier = pltpu.get_barrier_semaphore()
    others = [(dp, lax.rem(mp + k, plan.m)) for k in range(1, plan.m)]
    others += [(lax.rem(dp + k, plan.n), mp) for k in range(1, plan.n)]
    for other in others:
        pl.semaphore_signal(barrier, inc=1, device_id=other, device_id_type=MESH)
    pl.semaphore_wait(barrier, len(others))


def remote(source, target, send, recv, device):
    copy = pltpu.make_async_remote_copy(
        src_ref=source,
        dst_ref=target,
        send_sem=send,
        recv_sem=recv,
        device_id=device,
        device_id_type=MESH,
    )
    copy.start()
    return copy


def weave_kernel(plan, shard, gain, out, gain_out, own, *sems):
    z_send, z_recv, x_send, x_recv, y_send, y_recv, c_send, c_recv, g_send, g_recv = sems
    (dp, core, x, y), mp = dp_place(), lax.axis_index("mp")
    types, rows = shard.shape[:2]
    half = types // 2
    greet_all(plan, dp, mp)
    beside = dp + 1 - 2 * core
    dp_x, dp_y = dp + 2 - 4 * x, dp + 4 - 8 * y
    dp_xy = dp_x + 4 - 8 * y

    def block(index, column, first=0, count=types):
        z = lax.rem(mp + plan.m - index, plan.m)
        place = pl.ds(pl.multiple_of(z * rows, rows), rows)
        return out.at[pl.ds(first, count), place, columns(column)]

    def pass_on(index, column, sems, slot, device, first=0, count=types):
        region = block(index, column, first, count)
        return remote(
            region, region, sems[0].at[index, slot], sems[1].at[index, slot], (device, mp)
        )

    locals_ = [
        pltpu.make_async_copy(shard, block(0, dp), own.at[0]),
        pltpu.make_async_copy(gain, gain_out.at[:, columns(dp)], own.at[1]),
    ]
    for copy in locals_:
        copy.start()
    z_copies = [None]
    for k in range(1, plan.m):
        z_copies.append(
            remote(shard, block(0, dp), z_send.at[k], z_recv.at[k], (dp, lax.rem(mp + k, plan.m)))
        )
    copies = [
        remote(
            gain,
            gain_out.at[:, columns(dp)],
            g_send.at[k],
            g_recv.at[k],
            (lax.rem(dp + k, plan.n), mp),
        )
        for k in range(1, plan.n)
    ]
    x_sems, y_sems, c_sems = (x_send, x_recv), (y_send, y_recv), (c_send, c_recv)
    x_own, y_own, x_far, y_far, c_all = [], [], [], [], []

    def first_stage(index):
        if index == 0:
            for copy in locals_:
                copy.wait()
        else:
            z_copies[index].wait_recv()
        x_own.append(pass_on(index, dp, x_sems, 0, dp_x))
        y_own.append(pass_on(index, dp, y_sems, 0, dp_y))
        c_all.append(pass_on(index, dp, c_sems, 0, beside))

    def second_stage(index):
        x_own[index].wait_recv()
        y_far.append(pass_on(index, dp_x, y_sems, 1, dp_y, 0, half))
        c_all.append(pass_on(index, dp_x, c_sems, 1, beside))
        y_own[index].wait_recv()
        x_far.append(pass_on(index, dp_y, x_sems, 1, dp_x, half, types - half))
        c_all.append(pass_on(index, dp_y, c_sems, 2, beside))

    def third_stage(index):
        y_far[index].wait_recv()
        c_all.append(pass_on(index, dp_xy, c_sems, 3, beside, 0, half))
        x_far[index].wait_recv()
        c_all.append(pass_on(index, dp_xy, c_sems, 4, beside, half, types - half))

    for step in range(plan.m + 2):
        if step < plan.m:
            first_stage(step)
        if 1 <= step < plan.m + 1:
            second_stage(step - 1)
        if step >= 2:
            third_stage(step - 2)
    for copy in copies + c_all:
        copy.wait()
    for copy in z_copies[1:] + x_own + y_own + x_far + y_far:
        copy.wait_send()


def weave(plan, shard, gain):
    types, rows = shard.shape[:2]
    dma = pltpu.SemaphoreType.DMA
    return pl.pallas_call(
        functools.partial(weave_kernel, plan),
        in_specs=[ANY, ANY],
        out_specs=(ANY, ANY),
        out_shape=(
            jax.ShapeDtypeStruct((types, plan.m * rows, D), jnp.bfloat16),
            jax.ShapeDtypeStruct((gain.shape[0], D), jnp.bfloat16),
        ),
        scratch_shapes=[dma((2,))]
        + [dma((plan.m,))] * 2
        + [dma((plan.m, 2))] * 4
        + [dma((plan.m, 5))] * 2
        + [dma((plan.n,))] * 2,
        compiler_params=pltpu.CompilerParams(collective_id=6, has_side_effects=True),
        cost_estimate=BRIEF,
        name="weave",
    )(shard, gain)


def shed_kernel(plan, normed, dq, dk, dv, extra, out, left, parts, from_core, sums, *rest):
    from_first, sums_first, from_second, blocks, from_z, c_sems, f_sems, s_sems, z_sems = rest
    (dp, core, x, y), mp = dp_place(), lax.axis_index("mp")
    width = D // plan.n
    wide = D // 2
    greet_all(plan, dp, mp)
    beside, dp_x, dp_y = dp + 1 - 2 * core, dp + 2 - 4 * x, dp + 4 - 8 * y

    def rows_of(index):
        return pl.ds(pl.multiple_of(index * width, width), width)

    def plus(one, other):
        return (one.astype(jnp.float32) + other.astype(jnp.float32)).astype(jnp.bfloat16)

    left[...] = normed[...].T
    c_copies, first, second = [], [], []
    for half in range(2):
        for kind, array in enumerate((dq, dk, dv)):
            place = slice(kind * wide, (kind + 1) * wide)
            source = slice(half * wide, (half + 1) * wide)
            parts[half, :, place] = nn(left[...], array[:, source]).astype(jnp.bfloat16)
        parts[half, :, 3 * wide :] = extra[...].astype(jnp.bfloat16)
        c_copies.append(
            [
                remote(
                    parts.at[half, rows_of(2 * j + 1 - core)],
                    from_core.at[half, j],
                    c_sems.at[0, half, j],
                    c_sems.at[1, half, j],
                    (beside, mp),
                )
                for j in range(4)
            ]
        )
    for half in range(2):
        for j in range(4):
            c_copies[half][j].wait_recv()
            sums[half, j] = plus(parts[half, rows_of(2 * j + core), :], from_core[half, j])
        for k in range(2):
            away = 2 * k + 1 - x if half == 0 else 2 * (1 - y) + k
            first.append(
                remote(
                    sums.at[half, away],
                    from_first.at[half, k],
                    f_sems.at[0, half, k],
                    f_sems.at[1, half, k],
                    (dp_x if half == 0 else dp_y, mp),
                )
            )
    for half in range(2):
        for k in range(2):
            first[2 * half + k].wait_recv()
            kept = 2 * k + x if half == 0 else 2 * y + k
            sums_first[half, k] = plus(sums[half, kept], from_first[half, k])
        second.append(
            remote(
                sums_first.at[half, 1 - y if half == 0 else 1 - x],
                from_second.at[half],
                s_sems.at[0, half],
                s_sems.at[1, half],
                (dp_y if half == 0 else dp_x, mp),
            )
        )
    piece = D // plan.m
    for half in range(2):
        second[half].wait_recv()
        total = plus(sums_first[half, y if half == 0 else x], from_second[half])
        for member in range(2):
            index = 2 * half + member
            for kind in range(3):
                start = kind * wide + member * piece
                blocks[index, :, kind * piece : (kind + 1) * piece] = total[:, start : start + piece]
            blocks[index, :, 3 * piece :] = total[:, 3 * wide :]
    z_copies = []
    for k in range(1, plan.m):
        peer = lax.rem(mp + k, plan.m)
        z_copies.append(
            remote(
                blocks.at[peer], from_z.at[k], z_sems.at[0, k], z_sems.at[1, k], (dp, peer)
            )
        )
    result = blocks[mp].astype(jnp.float32)
    for k in range(1, plan.m):
        z_copies[k - 1].wait_recv()
        result = result + from_z[k].astype(jnp.float32)
    out[...] = result
    for copy in c_copies[0] + c_copies[1] + first + second + z_copies:
        copy.wait_send()


def shed(plan, normed, dqkv, extra):
    dma = pltpu.SemaphoreType.DMA
    width, wide, kept = D // plan.n, 3 * (D // 2) + LANES, 3 * (D // plan.m) + LANES

    def held(*shape):
        return pltpu.VMEM(shape, jnp.bfloat16)

    return pl.pallas_call(
        functools.partial(shed_kernel, plan),
        in_specs=[VMEM] * 5,
        out_specs=VMEM,
        out_shape=jax.ShapeDtypeStruct((width, kept), jnp.float32),
        scratch_shapes=[
            held(D, normed.shape[0]),
            held(2, D, wide),
            held(2, 4, width, wide),
            held(2, 4, width, wide),
            held(2, 2, width, wide),
            held(2, 2, width, wide),
            held(2, width, wide),
            held(plan.m, width, kept),
            held(plan.m, width, kept),
            dma((2, 2, 4)),
            dma((2, 2, 2)),
            dma((2, 2)),
            dma((2, plan.m)),
        ],
        compiler_params=pltpu.CompilerParams(
            collective_id=7, has_side_effects=True, vmem_limit_bytes=BIG_VMEM
        ),
        cost_estimate=BRIEF,
        name="shed",
    )(normed, *dqkv, extra)


def products_kernel(plan, sides, *refs):
    rows_in, refs = refs[0], refs[1:]
    lefts, rights = refs[: len(set(sides))], refs[len(set(sides)) : len(set(sides)) + len(sides)]
    seg, out, left_sides, tiles, send, recv, own, sent = refs[len(lefts) + len(rights) :]
    segment, member = plan.here()
    rows = plan.rows
    greet(plan, segment, member)

    def source(peer):
        return rows_in.at[:, columns(peer)]

    place = seg.at[pl.ds(pl.multiple_of(member * rows, rows), rows)]
    copies = member_copies(plan, segment, member, source, place, send, recv, own)
    for index, array in enumerate(lefts):
        left_sides[index] = array[...].T
    start, pending = 0, [None, None]
    slot = 0
    for array, side in zip(rights, sides):
        size = array.shape[1]
        width = size // 2 if size % (2 * LANES) == 0 and size > D else D
        for first in range(0, size, width):
            if pending[slot] is not None:
                pending[slot].wait()
            tiles[slot, :, :width] = nn(
                left_sides[side], array[:, first : first + width]
            ).astype(jnp.bfloat16)
            pending[slot] = pltpu.make_async_copy(
                tiles.at[slot, :, :width], out.at[:, pl.ds(start, width)], sent.at[slot]
            )
            pending[slot].start()
            start += width
            slot = 1 - slot
    for copy in pending + copies:
        copy.wait()


def products(plan, rows_in, lefts, rights, sides):
    rows, widest = lefts[0].shape[0], max(array.shape[1] for array in rights) // 2
    total = sum(array.shape[1] for array in rights)
    return pl.pallas_call(
        functools.partial(products_kernel, plan, sides),
        in_specs=[ANY] + [VMEM] * (len(lefts) + len(rights)),
        out_specs=(ANY, ANY),
        out_shape=(
            jax.ShapeDtypeStruct((plan.seg_rows, LANES), jnp.bfloat16),
            jax.ShapeDtypeStruct((D, total), jnp.bfloat16),
        ),
        scratch_shapes=[
            pltpu.VMEM((len(lefts), D, rows), jnp.bfloat16),
            pltpu.VMEM((2, D, widest), jnp.bfloat16),
            pltpu.SemaphoreType.DMA((plan.group,)),
            pltpu.SemaphoreType.DMA((plan.group,)),
            pltpu.SemaphoreType.DMA,
            pltpu.SemaphoreType.DMA((2,)),
        ],
        compiler_params=pltpu.CompilerParams(
            collective_id=len(lefts), has_side_effects=True, vmem_limit_bytes=BIG_VMEM
        ),
        cost_estimate=BRIEF,
        name="products",
    )(rows_in, *lefts, *rights)


def collect_kernel(plan, spans, more, *refs):
    parts = 1 if spans == 0 else 2
    arrays, halos, refs = refs[:parts], refs[parts : parts + spans], refs[parts + spans :]
    beside, refs = refs[:more], refs[more:]
    outs, refs = refs[:parts], refs[parts:]
    total, send, recv, own = refs[-4:]
    segment, member = plan.here()
    rows = plan.rows
    greet(plan, segment, member)
    copies = []
    for part, array in enumerate(arrays):
        if spans:
            for piece in range(plan.seg_rows // CHUNK):
                start = piece * CHUNK
                value = array[pl.ds(start, CHUNK), :]
                for index, (distance, first, count) in enumerate(plan.spans):
                    offset = start - (plan.seg_rows - count)
                    if offset >= 0:
                        halo = halos[index][part, pl.ds(offset, CHUNK), :]
                        value = value + halo.astype(jnp.float32)
                total[part, pl.ds(start, CHUNK), :] = value.astype(jnp.bfloat16)
            array = total.at[part]

        def source(peer, array=array):
            return array.at[pl.ds(pl.multiple_of(peer * rows, rows), rows)]

        copies += member_copies(
            plan,
            segment,
            member,
            source,
            outs[part].at[:, columns(member)],
            send.at[part],
            recv.at[part],
            own.at[part],
        )
    if beside:
        (hidden, weights, middle), (final, down, loaded) = beside, refs[:3]
        load = pltpu.make_async_copy(weights.at[2], down, loaded)
        load.start()
        load.wait()
        for first in range(0, D, TILE):
            place = slice(first, first + TILE)
            final[:, place] = (middle[:, place] + nn(hidden[...], down[:, place])).astype(
                jnp.bfloat16
            )
    for copy in copies:
        copy.wait()


def collect(plan, arrays, halos, beside=()):
    parts, spans = len(arrays), len(plan.spans) if halos else 0
    return pl.pallas_call(
        functools.partial(collect_kernel, plan, spans, len(beside)),
        out_shape=(jax.ShapeDtypeStruct((plan.rows, D), jnp.bfloat16),) * (parts + bool(beside)),
        in_specs=[VMEM] * (parts + len(halos)) + [VMEM, ANY, VMEM][: len(beside)],
        out_specs=(ANY,) * parts + (VMEM,) * bool(beside),
        scratch_shapes=[pltpu.VMEM(one.shape[1:], one.dtype) for one in beside[1:2]]
        + [pltpu.SemaphoreType.DMA] * bool(beside)
        + [
            pltpu.VMEM((parts, plan.seg_rows if halos else 16, LANES), jnp.bfloat16),
            pltpu.SemaphoreType.DMA((parts, plan.group)),
            pltpu.SemaphoreType.DMA((parts, plan.group)),
            pltpu.SemaphoreType.DMA((parts,)),
        ],
        compiler_params=pltpu.CompilerParams(
            collective_id=5 if halos else 9 if beside else 8, has_side_effects=True, vmem_limit_bytes=BIG_VMEM
        ),
        cost_estimate=BRIEF,
        name="collect_kv" if halos else "collect_q",
    )(*arrays, *halos, *beside)


def swap_halves(values):
    lane = lax.broadcasted_iota(jnp.int32, values.shape, 1)
    half = HEAD_DIM // 2
    ahead = pltpu.roll(values, LANES - half, 1)
    behind = pltpu.roll(values, half, 1)
    return jnp.where(lax.rem(lane, HEAD_DIM) < half, ahead, behind)


def rotate(values, cosine, sine):
    return values * cosine + swap_halves(values) * sine


def of_head(values, head):
    lane = lax.broadcasted_iota(jnp.int32, values.shape, 1)
    return jnp.where(lane // HEAD_DIM == head, values, jnp.zeros_like(values))


def chunk_rows(index, size):
    return pl.ds(pl.multiple_of(index * size, size), size)


HALO_CHUNKS = HALO // CHUNK


def rotate_keys(prior, first, keys, cosine, sine, k_turned):
    def one(index, unused):
        table = chunk_rows(prior[first + index], CHUNK)
        rows = chunk_rows(index, CHUNK)
        k_turned[rows, :] = rotate(
            keys[rows, :].astype(jnp.float32), cosine[table, :], sine[table, :]
        ).astype(jnp.bfloat16)
        return unused

    lax.fori_loop(0, keys.shape[0] // CHUNK, one, 0)


def query_tables(prior, block, cosine, sine):
    rows = chunk_rows(prior[HALO_CHUNKS + block], QUERY_ROWS)
    return cosine[rows, :], sine[rows, :]


def turned_queries(prior, block, queries, cosine, sine):
    cos_rows, sin_rows = query_tables(prior, block, cosine, sine)
    turned = rotate(queries.astype(jnp.float32), cos_rows, sin_rows)
    return (turned * (LOG2E * HEAD_DIM ** (-0.5))).astype(jnp.bfloat16)


def by_head(parts):
    whole = parts[0]
    lane = lax.broadcasted_iota(jnp.int32, whole.shape, 1)
    for head in range(1, HEADS_HELD):
        whole = jnp.where(lane // HEAD_DIM == head, parts[head], whole)
    return whole


def needs_halo(prior, own_chunks):
    needed = prior[HALO_CHUNKS] > 0
    for chunk in range(1, min(own_chunks, HALO_CHUNKS)):
        needed = needed | (prior[HALO_CHUNKS + chunk] > chunk)
    return needed


ROW_PARTS = 4
UNITS = [(head, part) for part in range(ROW_PARTS) for head in range(HEADS_HELD)]


def add_keys(refs, first, diagonal):
    q_head, k_turned, v_wide, top, total = refs
    start_row = pl.multiple_of(first * CHUNK, CHUNK)
    part_rows = QUERY_ROWS // ROW_PARTS

    def queries(part):
        return slice(part * part_rows, (part + 1) * part_rows)

    def keys(part):
        return pl.ds(start_row, (part + 1) * part_rows if diagonal else CHUNK)

    def start(unit):
        head, part = unit
        return nt(q_head[head, queries(part), :], k_turned[keys(part), :])

    def finish(unit, scores):
        head, part = unit
        held = (head, queries(part))
        value_block = v_wide[keys(part), :]
        if diagonal:
            place = lax.broadcasted_iota(jnp.int32, scores.shape, 0) + part * part_rows
            other = lax.broadcasted_iota(jnp.int32, scores.shape, 1)
            scores = jnp.where(other <= place, scores, MASKED)
        highest = jnp.max(scores, axis=1, keepdims=True)
        if diagonal:
            weights = jnp.exp2((scores - highest).astype(jnp.bfloat16))
            total[held] = nn(weights, value_block)
            top[held] = jnp.broadcast_to(highest, (part_rows, LANES))
        else:
            before = top[held]
            after = jnp.maximum(before, highest)
            weights = jnp.exp2((scores - after[:, :1]).astype(jnp.bfloat16))
            shrink = jnp.exp2(before - after)
            shrink = jnp.concatenate([shrink, shrink], axis=1)
            total[held] = total[held] * shrink + nn(weights, value_block)
            top[held] = after

    scores = start(UNITS[0])
    for index, unit in enumerate(UNITS):
        following = start(UNITS[index + 1]) if index + 1 < len(UNITS) else None
        finish(unit, scores)
        scores = following


def mixed_of(total):
    return by_head([total[head, :, :LANES] / total[head, :, LANES:] for head in range(HEADS_HELD)])


def attend_own_kernel(
    prior, q_ref, keys, values, cosine, sine, out_ref, top_ref, sum_ref, *scratch
):
    k_turned, v_wide, q_head, top, total = scratch
    block = pl.program_id(0)

    @pl.when(block == 0)
    def _():
        rotate_keys(prior, HALO_CHUNKS, keys, cosine, sine, k_turned)
        v_wide[:, :LANES] = values[...]
        v_wide[:, LANES:] = jnp.ones((values.shape[0], LANES), jnp.bfloat16)

    turned = turned_queries(prior, block, q_ref[...], cosine, sine)
    for head in range(HEADS_HELD):
        q_head[head] = of_head(turned, head)
    held = (q_head, k_turned, v_wide, top, total)
    add_keys(held, block, True)

    def earlier_chunk(index, unused):
        add_keys(held, block - 1 - index, False)
        return unused

    lax.fori_loop(0, jnp.minimum(prior[HALO_CHUNKS + block], block), earlier_chunk, 0)
    out_ref[...] = mixed_of(total).astype(jnp.bfloat16)
    top_ref[...] = by_head([top[head] for head in range(HEADS_HELD)])
    sum_ref[...] = by_head([total[head, :, LANES:] for head in range(HEADS_HELD)])


def attend_own(prior, q_seg, keys, values, cosine, sine):
    seg_rows = q_seg.shape[0]
    query_spec = pl.BlockSpec((QUERY_ROWS, LANES), lambda i, prior: (i, 0))
    wide = jax.ShapeDtypeStruct((seg_rows, LANES), jnp.float32)
    return pl.pallas_call(
        attend_own_kernel,
        grid_spec=pltpu.PrefetchScalarGridSpec(
            num_scalar_prefetch=1,
            grid=(seg_rows // QUERY_ROWS,),
            in_specs=[query_spec, VMEM, VMEM, VMEM, VMEM],
            out_specs=(query_spec,) * 3,
            scratch_shapes=[
                pltpu.VMEM((seg_rows, LANES), jnp.bfloat16),
                pltpu.VMEM((seg_rows, 2 * LANES), jnp.bfloat16),
                pltpu.VMEM((HEADS_HELD, QUERY_ROWS, LANES), jnp.bfloat16),
                pltpu.VMEM((HEADS_HELD, QUERY_ROWS, LANES), jnp.float32),
                pltpu.VMEM((HEADS_HELD, QUERY_ROWS, 2 * LANES), jnp.float32),
            ],
        ),
        out_shape=(jax.ShapeDtypeStruct((seg_rows, LANES), jnp.bfloat16), wide, wide),
        compiler_params=pltpu.CompilerParams(vmem_limit_bytes=BIG_VMEM),
        cost_estimate=BRIEF,
        name="attend_own",
    )(prior, q_seg, keys, values, cosine, sine)


def copy_in(pairs, sems):
    copies = [
        pltpu.make_async_copy(source, target, sems.at[index])
        for index, (source, target) in enumerate(pairs)
    ]
    for copy in copies:
        copy.start()
    for copy in copies:
        copy.wait()


def attend_halo_kernel(
    own_chunks, prior, q_seg, keys, values, cos_hbm, sin_hbm, out_in, top_in, sum_in,
    out, top_out, sum_out, *scratch
):
    k_turned, v_wide, q_head, top, total, key_rows, value_rows, cosine, sine = scratch[:9]
    q_rows, out_rows, top_rows, sum_rows, sems = scratch[9:]

    def one_block(block, unused):
        count = prior[HALO_CHUNKS + block] - block
        rows = chunk_rows(block, QUERY_ROWS)

        @pl.when(count > 0)
        def _():
            turned = turned_queries(prior, block, q_rows[rows, :], cosine, sine)
            mixed, tops, sums = out_rows[rows, :], top_rows[rows, :], sum_rows[rows, :]
            for head in range(HEADS_HELD):
                lane = head * HEAD_DIM
                q_head[head] = of_head(turned, head)
                top[head] = jnp.broadcast_to(tops[:, lane : lane + 1], top.shape[1:])
                weight = jnp.broadcast_to(sums[:, lane : lane + 1], top.shape[1:])
                total[head, :, :LANES] = mixed.astype(jnp.float32) * weight
                total[head, :, LANES:] = weight

            def earlier_chunk(index, unused):
                held = (q_head, k_turned, v_wide, top, total)
                add_keys(held, HALO_CHUNKS - 1 - index, False)
                return unused

            lax.fori_loop(0, count, earlier_chunk, 0)
            out_rows[rows, :] = mixed_of(total).astype(jnp.bfloat16)
            top_rows[rows, :] = by_head([top[head] for head in range(HEADS_HELD)])
            sum_rows[rows, :] = by_head([total[head, :, LANES:] for head in range(HEADS_HELD)])

        return unused

    @pl.when(needs_halo(prior, own_chunks))
    def _():
        part = pl.ds(0, q_rows.shape[0])
        held = ((out, out_rows), (top_out, top_rows), (sum_out, sum_rows))
        copy_in(
            (
                (keys, key_rows), (values, value_rows), (cos_hbm, cosine), (sin_hbm, sine),
                (q_seg.at[part], q_rows), *((hbm.at[part], rows) for hbm, rows in held),
            ),
            sems,
        )
        rotate_keys(prior, 0, key_rows, cosine, sine, k_turned)
        v_wide[:, :LANES] = value_rows[...]
        v_wide[:, LANES:] = jnp.ones((value_rows.shape[0], LANES), jnp.bfloat16)
        lax.fori_loop(0, q_rows.shape[0] // QUERY_ROWS, one_block, 0)
        copy_in([(rows, hbm.at[part]) for hbm, rows in held], sems)


def attend_halo(prior, q_seg, keys, values, cosine, sine, earlier):
    part = (min(q_seg.shape[0], HALO), LANES)
    per_head = (HEADS_HELD, QUERY_ROWS, LANES)
    return pl.pallas_call(
        functools.partial(attend_halo_kernel, q_seg.shape[0] // CHUNK),
        in_specs=[SMEM] + [ANY] * 8,
        out_specs=(ANY,) * 3,
        out_shape=tuple(jax.ShapeDtypeStruct(one.shape, one.dtype) for one in earlier),
        scratch_shapes=[
            pltpu.VMEM((HALO, LANES), jnp.bfloat16),
            pltpu.VMEM((HALO, 2 * LANES), jnp.bfloat16),
            pltpu.VMEM(per_head, jnp.bfloat16),
            pltpu.VMEM(per_head, jnp.float32),
            pltpu.VMEM((HEADS_HELD, QUERY_ROWS, 2 * LANES), jnp.float32),
            pltpu.VMEM((HALO, LANES), jnp.bfloat16),
            pltpu.VMEM((HALO, LANES), jnp.bfloat16),
            pltpu.VMEM((LONGEST, LANES), jnp.float32),
            pltpu.VMEM((LONGEST, LANES), jnp.float32),
            pltpu.VMEM(part, jnp.bfloat16),
            pltpu.VMEM(part, jnp.bfloat16),
            pltpu.VMEM(part, jnp.float32),
            pltpu.VMEM(part, jnp.float32),
            pltpu.SemaphoreType.DMA((8,)),
        ],
        input_output_aliases={6: 0, 7: 1, 8: 2},
        compiler_params=pltpu.CompilerParams(vmem_limit_bytes=BIG_VMEM),
        cost_estimate=BRIEF,
        name="attend_halo",
    )(prior, q_seg, keys, values, cosine, sine, *earlier)


def prepare_back(refs, block, prior, queries, grads, mixed, tops, sums, cosine, sine):
    q_head, grad_head, row_stats = refs
    turned = turned_queries(prior, block, queries, cosine, sine)
    grads = grads.astype(jnp.float32) / sums
    dots = (grads * mixed.astype(jnp.float32)).T
    tops = tops.T
    grads = grads.astype(jnp.bfloat16)
    for head in range(HEADS_HELD):
        q_head[head] = of_head(turned, head)
        grad_head[head] = of_head(grads, head)
        lanes = slice(head * HEAD_DIM, (head + 1) * HEAD_DIM)
        row_stats[head, 0:1, :] = tops[head * HEAD_DIM : head * HEAD_DIM + 1, :]
        row_stats[head, 1:2, :] = jnp.sum(dots[lanes, :], axis=0, keepdims=True)


def add_keys_back(refs, first, diagonal):
    q_head, grad_head, row_stats, k_turned, values, dq_total, dk_total, dv_total = refs
    part_rows = QUERY_ROWS // ROW_PARTS

    def keys(part):
        start = pl.multiple_of(first * CHUNK + part * part_rows, part_rows)
        return pl.ds(start, part_rows)

    def queries(part):
        return slice(part * part_rows if diagonal else 0, QUERY_ROWS)

    def start(unit):
        head, part = unit
        rows, wanted = keys(part), queries(part)
        return (
            nt(k_turned[rows, :], q_head[head, wanted, :]),
            nt(values[rows, :], grad_head[head, wanted, :]),
        )

    def finish(unit, products_):
        head, part = unit
        rows, wanted = keys(part), queries(part)
        scores, grad_weights = products_
        weights = jnp.exp2((scores - row_stats[head, 0:1, wanted]).astype(jnp.bfloat16))
        if diagonal:
            other = lax.broadcasted_iota(jnp.int32, scores.shape, 0)
            place = lax.broadcasted_iota(jnp.int32, scores.shape, 1)
            weights = jnp.where(other <= place, weights, jnp.zeros_like(weights))
        grad_scores = weights * (grad_weights - row_stats[head, 1:2, wanted]).astype(jnp.bfloat16)
        dv_total[rows, :] += nn(weights, grad_head[head, wanted, :])
        dk_total[rows, :] += nn(grad_scores, q_head[head, wanted, :])
        dq_total[head, wanted, :] += tn(grad_scores, k_turned[rows, :])

    held = start(UNITS[0])
    for index, unit in enumerate(UNITS):
        following = start(UNITS[index + 1]) if index + 1 < len(UNITS) else None
        finish(unit, held)
        held = following


def turn_keys_back(prior, first_chunk, dk_total, dv_total, cosine, sine, dk_ref, dv_ref):
    def one(index, unused):
        table = chunk_rows(prior[first_chunk + index], CHUNK)
        rows = chunk_rows(index, CHUNK)
        turned = rotate(dk_total[rows, :], cosine[table, :], -sine[table, :]) * (1.0 / LOG2E)
        dk_ref[rows, :] = turned.astype(dk_ref.dtype)
        dv_ref[rows, :] = dv_total[rows, :].astype(dv_ref.dtype)
        return unused

    lax.fori_loop(0, dk_ref.shape[0] // CHUNK, one, 0)


def attend_back_own_kernel(
    prior, q_ref, grad_ref, out_ref, top_ref, sum_ref, keys, values, cosine, sine, dq_part,
    dq_ref, dk_ref, dv_ref, k_turned, q_head, grad_head, dq_total, dk_total, dv_total, row_stats
):
    block = pl.program_id(0)
    chunks_back = prior[HALO_CHUNKS + block]

    @pl.when(block == 0)
    def _():
        rotate_keys(prior, HALO_CHUNKS, keys, cosine, sine, k_turned)
        dk_total[...] = jnp.zeros_like(dk_total)
        dv_total[...] = jnp.zeros_like(dv_total)

    prepare_back(
        (q_head, grad_head, row_stats), block, prior, q_ref[...], grad_ref[...], out_ref[...],
        top_ref[...], sum_ref[...], cosine, sine,
    )
    from_halo = jnp.where(chunks_back > block, dq_part[...], jnp.zeros_like(dq_part))
    for head in range(HEADS_HELD):
        dq_total[head] = from_halo
    held = (q_head, grad_head, row_stats, k_turned, values, dq_total, dk_total, dv_total)
    add_keys_back(held, block, True)

    def whole(index, unused):
        add_keys_back(held, index, False)
        return unused

    lax.fori_loop(jnp.maximum(block - chunks_back, 0), block, whole, 0)
    cos_rows, sin_rows = query_tables(prior, block, cosine, sine)
    turned = rotate(by_head([dq_total[head] for head in range(HEADS_HELD)]), cos_rows, -sin_rows)
    dq_ref[...] = (turned * HEAD_DIM ** (-0.5)).astype(jnp.bfloat16)

    @pl.when(block == pl.num_programs(0) - 1)
    def _():
        turn_keys_back(prior, HALO_CHUNKS, dk_total, dv_total, cosine, sine, dk_ref, dv_ref)


def back_scratch(key_rows):
    per_head = (HEADS_HELD, QUERY_ROWS, LANES)
    return [
        pltpu.VMEM((key_rows, LANES), jnp.bfloat16),
        pltpu.VMEM(per_head, jnp.bfloat16),
        pltpu.VMEM(per_head, jnp.bfloat16),
        pltpu.VMEM(per_head, jnp.float32),
        pltpu.VMEM((key_rows, LANES), jnp.float32),
        pltpu.VMEM((key_rows, LANES), jnp.float32),
        pltpu.VMEM((HEADS_HELD, 8, QUERY_ROWS), jnp.float32),
    ]


def attend_back_own(prior, q_seg, grad_seg, seen, keys, values, cosine, sine, dq_part):
    seg_rows = q_seg.shape[0]
    query_spec = pl.BlockSpec((QUERY_ROWS, LANES), lambda i, prior: (i, 0))
    wide = jax.ShapeDtypeStruct((seg_rows, LANES), jnp.float32)
    return pl.pallas_call(
        attend_back_own_kernel,
        grid_spec=pltpu.PrefetchScalarGridSpec(
            num_scalar_prefetch=1,
            grid=(seg_rows // QUERY_ROWS,),
            in_specs=[query_spec] * 5 + [VMEM] * 4 + [query_spec],
            out_specs=(query_spec, VMEM, VMEM),
            scratch_shapes=back_scratch(seg_rows),
        ),
        out_shape=(jax.ShapeDtypeStruct((seg_rows, LANES), jnp.bfloat16), wide, wide),
        compiler_params=pltpu.CompilerParams(vmem_limit_bytes=BIG_VMEM),
        cost_estimate=BRIEF,
        name="attend_back_own",
    )(prior, q_seg, grad_seg, *seen, keys, values, cosine, sine, dq_part)


def attend_back_halo_kernel(
    own_chunks, prior, q_seg, grad_seg, mixed, tops, sums, keys, values, cos_hbm, sin_hbm,
    dq_out, halves_out, *scratch
):
    k_turned, q_head, grad_head, dq_total, dk_total, dv_total, row_stats = scratch[:7]
    key_rows, value_rows, cosine, sine, dk_half, dv_half = scratch[7:13]
    q_rows, grad_rows, out_rows, top_rows, sum_rows, dq_rows, sems = scratch[13:]
    needed = needs_halo(prior, own_chunks)
    part = pl.ds(0, q_rows.shape[0])

    def one_block(block, unused):
        chunks_back = prior[HALO_CHUNKS + block]
        rows = chunk_rows(block, QUERY_ROWS)

        @pl.when(chunks_back > block)
        def _():
            prepare_back(
                (q_head, grad_head, row_stats), block, prior, q_rows[rows, :], grad_rows[rows, :],
                out_rows[rows, :], top_rows[rows, :], sum_rows[rows, :], cosine, sine,
            )
            dq_total[...] = jnp.zeros_like(dq_total)

            def whole(index, unused):
                add_keys_back(
                    (
                        q_head, grad_head, row_stats, k_turned, value_rows, dq_total, dk_total,
                        dv_total,
                    ),
                    index,
                    False,
                )
                return unused

            lax.fori_loop(HALO_CHUNKS + block - chunks_back, HALO_CHUNKS, whole, 0)
            dq_rows[rows, :] = by_head([dq_total[head] for head in range(HEADS_HELD)])

        return unused

    @pl.when(needed)
    def _():
        copy_in(
            (
                (keys, key_rows), (values, value_rows), (cos_hbm, cosine), (sin_hbm, sine),
                (q_seg.at[part], q_rows), (grad_seg.at[part], grad_rows),
                (mixed.at[part], out_rows), (tops.at[part], top_rows), (sums.at[part], sum_rows),
            ),
            sems,
        )
        rotate_keys(prior, 0, key_rows, cosine, sine, k_turned)
        dk_total[...] = jnp.zeros_like(dk_total)
        dv_total[...] = jnp.zeros_like(dv_total)
        lax.fori_loop(0, q_rows.shape[0] // QUERY_ROWS, one_block, 0)
        turn_keys_back(prior, 0, dk_total, dv_total, cosine, sine, dk_half, dv_half)
        copy_in(((dq_rows, dq_out.at[part]),), sems)

    @pl.when(jnp.logical_not(needed))
    def _():
        dk_half[...] = jnp.zeros_like(dk_half)
        dv_half[...] = jnp.zeros_like(dv_half)

    copy_in(((dk_half, halves_out.at[0]), (dv_half, halves_out.at[1])), sems)


def attend_back_halo(prior, q_seg, grad_seg, seen, keys, values, cosine, sine):
    seg_rows = q_seg.shape[0]
    part = (min(seg_rows, HALO), LANES)
    return pl.pallas_call(
        functools.partial(attend_back_halo_kernel, seg_rows // CHUNK),
        in_specs=[SMEM] + [ANY] * 9,
        out_specs=(ANY,) * 2,
        out_shape=(
            jax.ShapeDtypeStruct((seg_rows, LANES), jnp.float32),
            jax.ShapeDtypeStruct((2, HALO, LANES), jnp.bfloat16),
        ),
        scratch_shapes=back_scratch(HALO)
        + [
            pltpu.VMEM((HALO, LANES), jnp.bfloat16),
            pltpu.VMEM((HALO, LANES), jnp.bfloat16),
            pltpu.VMEM((LONGEST, LANES), jnp.float32),
            pltpu.VMEM((LONGEST, LANES), jnp.float32),
            pltpu.VMEM((HALO, LANES), jnp.bfloat16),
            pltpu.VMEM((HALO, LANES), jnp.bfloat16),
            pltpu.VMEM(part, jnp.bfloat16),
            pltpu.VMEM(part, jnp.bfloat16),
            pltpu.VMEM(part, jnp.bfloat16),
            pltpu.VMEM(part, jnp.float32),
            pltpu.VMEM(part, jnp.float32),
            pltpu.VMEM(part, jnp.float32),
            pltpu.SemaphoreType.DMA((9,)),
        ],
        compiler_params=pltpu.CompilerParams(vmem_limit_bytes=BIG_VMEM),
        cost_estimate=BRIEF,
        name="attend_back_halo",
    )(prior, q_seg, grad_seg, *seen, keys, values, cosine, sine)


def attention(plan, tables, q_seg, k_seg, v_seg):
    k_halo, v_halo = halo_of(plan, k_seg), halo_of(plan, v_seg)
    earlier = attend_own(tables[0], q_seg, k_seg, v_seg, *tables[1:])
    seen = attend_halo(tables[0], q_seg, k_halo, v_halo, *tables[1:], earlier)
    return seen[0], (q_seg, k_seg, v_seg, k_halo, v_halo, seen)


def attention_back(plan, tables, kept, grad_seg, waiting, late, beside=()):
    q_seg, k_seg, v_seg, k_halo, v_halo, seen = kept
    queries = (tables[0], q_seg, grad_seg, seen)
    dq_part, halves = attend_back_halo(*queries, k_halo, v_halo, *tables[1:])
    halos = halo_back(plan, halves)
    dq_part, waiting = lax.optimization_barrier((dq_part, waiting))
    dq, dk_own, dv_own = attend_back_own(*queries, k_seg, v_seg, *tables[1:], dq_part)
    dq, *final = collect(plan, (dq,), (), beside)
    dq, *halos = lax.optimization_barrier((dq, *halos))
    dkv, late = lax.optimization_barrier((collect(plan, (dk_own, dv_own), halos), late))
    return (dq, *dkv), waiting, late, *final


def rotary_tables():
    half = HEAD_DIM // 2
    lane = jnp.arange(LANES)
    frequency = jnp.exp(
        (lane % half).astype(jnp.float32) * (-2.0 * math.log(10000.0) / HEAD_DIM)
    )
    sign = jnp.where(lane % HEAD_DIM < half, -1.0, 1.0).astype(jnp.float32)
    step = 64
    fine = jnp.arange(step).astype(jnp.float32)[:, None] * frequency[None, :]
    coarse = jnp.arange(0, LONGEST, step).astype(jnp.float32)[:, None] * frequency[None, :]
    cos_fine, sin_fine, cos_coarse, sin_coarse = lax.optimization_barrier(
        (jnp.cos(fine), jnp.sin(fine), jnp.cos(coarse), jnp.sin(coarse))
    )
    cosine = cos_coarse[:, None] * cos_fine[None] - sin_coarse[:, None] * sin_fine[None]
    sine = sin_coarse[:, None] * cos_fine[None] + cos_coarse[:, None] * sin_fine[None]
    return (
        cosine.reshape(LONGEST, LANES),
        (sine * sign).reshape(LONGEST, LANES),
    )


def chunks_before(plan, lengths):
    segment, unused = plan.here()
    count = (HALO + plan.seg_rows) // CHUNK
    places = segment * plan.seg_rows - HALO + CHUNK * jnp.arange(count)
    ends = jnp.cumsum(lengths)
    passed = ends[None, :] <= places[:, None]
    opening = jnp.max(jnp.where(passed, ends[None, :], 0), axis=1)
    return jnp.clip((places - opening) // CHUNK, 0, HALO_CHUNKS).astype(jnp.int32)


def tied(array, *others):
    return lax.optimization_barrier((array, *others))[0]


def attention_pack(weights):
    return jnp.stack([weights[1].T, weights[2].T, weights[3].T, weights[4]])


def feedforward_pack(weights):
    return jnp.stack([weights[6].T, weights[7].T, weights[8]])


def fetch_mp(packs):
    rows = [pack.reshape(-1, pack.shape[-1]) for pack in packs]
    whole = rows[0] if len(rows) == 1 else jnp.concatenate(rows, axis=0)
    return lax.all_gather(whole, "mp", axis=0, tiled=False)


def fetch_dp(whole, first, pack):
    count, rows, width = pack.shape
    members = whole.shape[0]
    part = whole[:, first : first + count * rows].reshape(members, count, rows, width)
    part = part.transpose(1, 0, 2, 3).reshape(count, members * rows, width)
    return lax.all_gather(part, "dp", axis=2, tiled=True)


def turn_kernel(members, sizes, *refs):
    parts, out = refs[:-1], refs[-1]
    index, start, row = 0, 0, 0
    for size in sizes:
        if start == parts[index].shape[1]:
            index, start = index + 1, 0
        turned = parts[index][:, start : start + size].T
        count = size // members
        for member in range(members):
            out[member, row : row + count, :] = turned[member * count : (member + 1) * count, :]
        start += size
        row += count


def mp_blocks(plan, parts, sizes):
    rows = sum(sizes) // plan.m
    if parts[0].shape[0] == LANES:
        return pl.pallas_call(
            functools.partial(turn_kernel, plan.m, sizes),
            in_specs=[VMEM] * len(parts),
            out_specs=VMEM,
            out_shape=jax.ShapeDtypeStruct((plan.m, rows, LANES), jnp.bfloat16),
            compiler_params=pltpu.CompilerParams(vmem_limit_bytes=BIG_VMEM),
            cost_estimate=BRIEF,
            name="turn",
        )(*parts)
    turned, start, pieces = jnp.concatenate(parts, axis=1).T, 0, []
    for size in sizes:
        piece = turned[start : start + size]
        pieces.append(piece.reshape(plan.m, size // plan.m, turned.shape[1]))
        start += size
    return jnp.concatenate(pieces, axis=1)


def reduce_mp(plan, blocks, sizes):
    part = lax.psum_scatter(blocks, "mp", scatter_dimension=0, tiled=False).astype(jnp.float32)
    start, pieces = 0, []
    for size in sizes:
        pieces.append(part[start : start + size // plan.m])
        start += size // plan.m
    return pieces


def reduce_mp_beside(plan, blocks, sizes):
    me = lax.axis_index("mp")

    def block(distance):
        return lax.dynamic_index_in_dim(blocks, (me + distance) % plan.m, 0, keepdims=False)

    total = block(0).astype(jnp.float32)
    for distance in range(1, plan.m):
        route = [(i, (i + distance) % plan.m) for i in range(plan.m)]
        total = total + lax.ppermute(block(distance), "mp", route).astype(jnp.float32)
    start, pieces = 0, []
    for size in sizes:
        pieces.append(total[start : start + size // plan.m])
        start += size // plan.m
    return pieces


def reduce_qkv(plan, gradient, extra):
    gradient = jnp.concatenate([gradient, extra.astype(jnp.bfloat16)], axis=1)
    part = lax.psum_scatter(gradient, "dp", scatter_dimension=0, tiled=True)
    width = D // plan.m
    blocks = part[:, : 3 * D].reshape(-1, 3, plan.m, width).transpose(2, 0, 1, 3)
    blocks = blocks.reshape(plan.m, -1, 3 * width)
    shared = jnp.broadcast_to(part[None, :, 3 * D :], (plan.m, part.shape[0], LANES))
    blocks = jnp.concatenate([blocks, shared], axis=2)
    return lax.psum_scatter(blocks, "mp", scatter_dimension=0, tiled=False).astype(jnp.float32)


def project(normed, attention, first_values):
    query, key, fresh = (nt(normed, attention[part]) for part in range(3))
    if first_values is not None:
        fresh = 0.5 * fresh + 0.5 * first_values.astype(jnp.float32)
    return tuple(array.astype(jnp.bfloat16) for array in (query, key, fresh))


def feed_forward(middle, gain, feedforward):
    normed_ff = norm_rows(middle, gain).astype(jnp.bfloat16)
    gate = nt(normed_ff, feedforward[0])
    upward = nt(normed_ff, feedforward[1])
    hidden = (jax.nn.silu(gate) * upward).astype(jnp.bfloat16)
    return normed_ff, gate, upward, hidden


def feed_forward_back(grad_final, middle, gain, weights, stored):
    attention, feedforward = weights
    normed_ff, gate, upward, hidden = stored
    grad_bar = grad_final.astype(jnp.bfloat16)
    grad_hidden = nt(grad_bar, feedforward[2])
    gate_sigmoid = jax.nn.sigmoid(gate)
    grad_gate = (
        grad_hidden * upward * gate_sigmoid * (1.0 + gate * (1.0 - gate_sigmoid))
    ).astype(jnp.bfloat16)
    grad_up = (grad_hidden * gate * gate_sigmoid).astype(jnp.bfloat16)
    grad_normed_ff = nn(grad_gate, feedforward[0]) + nn(grad_up, feedforward[1])
    grad_norm, grad_gain = norm_back(middle, gain, grad_normed_ff)
    grad_middle = grad_final + grad_norm
    middle_bar = grad_middle.astype(jnp.bfloat16)
    grad_mixed = nt(middle_bar, attention[3]).astype(jnp.bfloat16)
    return grad_middle, grad_gain, grad_mixed, (grad_bar, grad_gate, grad_up, middle_bar)


def project_back(grad_middle, stream, gain, attention, dqkv):
    grad_normed = sum(nn(array, attention[part]) for part, array in enumerate(dqkv))
    grad_norm, grad_gain = norm_back(stream, gain, grad_normed)
    return grad_middle + grad_norm, grad_gain


def square_sum(values):
    widened = values.astype(jnp.float32)
    return jnp.sum(widened * widened)


def shards(n, m, inputs, lengths, *rest):
    plan = Plan(n, m)
    first, second, cotangent = rest[:9], rest[9:18], rest[18]
    cosine, sine = rotary_tables()
    tables = (chunks_before(plan, lengths), cosine, sine)
    by_hand = (n, m) == (8, 4)
    gain_shard = jnp.stack([first[0], first[5], second[0], second[5]])
    attention_packs = attention_pack(first), attention_pack(second)
    feedforward_packs = feedforward_pack(first), feedforward_pack(second)
    whole = fetch_mp(feedforward_packs[:1])
    if by_hand:
        gain_shard = jnp.pad(gain_shard, ((0, 12), (0, 0)))
        attention_one, gains = weave(plan, attention_packs[0], gain_shard)
        whole, cosine, sine = lax.optimization_barrier((whole, cosine, sine))
        whole = tied(whole, gains)
        tables = (tables[0], cosine, sine)
    else:
        gains = lax.all_gather(gain_shard, "dp", axis=1, tiled=True)
        attention_one = fetch_dp(fetch_mp(attention_packs[:1]), 0, attention_packs[0])
    feedforward_one = fetch_dp(whole, 0, feedforward_packs[0])
    gains = gains[:4].astype(jnp.float32)
    heads, hidden_rows = first[4].shape[0] * m, first[8].shape[0] * m
    rest_sizes = (hidden_rows, hidden_rows, hidden_rows, heads)

    stream = inputs.astype(jnp.float32)
    normed_one = norm_rows(stream, gains[0]).astype(jnp.bfloat16)
    qkv = project(normed_one, attention_one, None)
    values_one = qkv[2]
    q_seg, k_seg, v_seg = spread(plan, *qkv)
    packs_two = (attention_packs[1], feedforward_packs[1])
    feedforward_one, q_seg, packs_two = lax.optimization_barrier(
        (feedforward_one, q_seg, packs_two)
    )
    whole_two = fetch_mp(packs_two)
    out_seg, seen_one = attention(plan, tables, q_seg, k_seg, v_seg)
    out_seg, whole_two = lax.optimization_barrier((out_seg, whole_two))
    mixed_one = to_rows(plan, out_seg)
    attention_two = fetch_dp(whole_two, 0, packs_two[0])
    feedforward_two = fetch_dp(whole_two, 4 * packs_two[0].shape[1], packs_two[1])
    middle_one = stream + nn(mixed_one, attention_one[3])
    ff_one = feed_forward(middle_one, gains[1], feedforward_one)
    between = middle_one + nn(ff_one[3], feedforward_one[2])

    normed_two = norm_rows(between, gains[2]).astype(jnp.bfloat16)
    qkv = project(normed_two, attention_two, values_one)
    values_two = qkv[2]
    q_seg, k_seg, v_seg = spread(plan, *qkv)
    out_seg, seen_two = attention(plan, tables, q_seg, k_seg, v_seg)
    mixed_two = to_rows(plan, out_seg)
    middle_two = between + nn(mixed_two, attention_two[3])
    ff_two = feed_forward(middle_two, gains[3], feedforward_two)

    grad_middle, gain_ff_two, grad_mixed, (bar, grad_gate, grad_up, middle_bar) = feed_forward_back(
        cotangent.astype(jnp.float32), middle_two, gains[3], (attention_two, feedforward_two), ff_two
    )
    grad_seg, rest = products(
        plan,
        grad_mixed,
        (bar, ff_two[0], middle_bar),
        (ff_two[3], grad_gate, grad_up, mixed_two),
        (0, 1, 1, 2),
    )
    rest_two = lax.psum_scatter(rest, "dp", scatter_dimension=0, tiled=True)
    dqkv, unused, unused, final = attention_back(
        plan, tables, seen_two, grad_seg, (), (), (ff_two[3], feedforward_two, middle_two)
    )
    value_extra = 0.5 * dqkv[2].astype(jnp.float32)
    dqkv_two = (dqkv[0], dqkv[1], value_extra.astype(jnp.bfloat16))
    grad_between, gain_two = project_back(
        grad_middle, between, gains[2], attention_two, dqkv_two
    )

    qkv_two = jnp.concatenate(
        [tn(normed_two, array).astype(jnp.bfloat16) for array in dqkv_two], axis=1
    )
    grad_between, qkv_two = lax.optimization_barrier((grad_between, qkv_two))
    qkv_two = lax.psum_scatter(qkv_two, "dp", scatter_dimension=0, tiled=True)
    grad_middle, gain_ff_one, grad_mixed, (bar, grad_gate, grad_up, middle_bar) = feed_forward_back(
        grad_between, middle_one, gains[1], (attention_one, feedforward_one), ff_one
    )
    grad_mixed, rest_two = lax.optimization_barrier((grad_mixed, rest_two))
    grad_seg, rest = products(
        plan,
        grad_mixed,
        (bar, ff_one[0], middle_bar),
        (ff_one[3], grad_gate, grad_up, mixed_one),
        (0, 1, 1, 2),
    )
    grad_seg, blocks, rest = lax.optimization_barrier(
        (grad_seg, mp_blocks(plan, (tied(rest_two, grad_seg),), rest_sizes), rest)
    )
    reduced_two = reduce_mp_beside(plan, blocks, rest_sizes)
    rest_one = lax.psum_scatter(rest, "dp", scatter_dimension=0, tiled=True)
    dqkv, qkv_two, reduced_two = attention_back(
        plan, tables, seen_one, grad_seg, qkv_two, reduced_two
    )
    grad_values = dqkv[2].astype(jnp.float32) + value_extra
    dqkv_one = (dqkv[0], dqkv[1], grad_values.astype(jnp.bfloat16))
    input_grad, gain_one = project_back(grad_middle, stream, gains[0], attention_one, dqkv_one)
    input_grad, rest_one = lax.optimization_barrier((input_grad, rest_one))
    sizes = rest_sizes + (heads,) * 3
    blocks, dqkv_one = lax.optimization_barrier(
        (mp_blocks(plan, (rest_one, qkv_two), sizes), dqkv_one)
    )
    down_one, gate_one, up_one, output_one, query_two, key_two, value_two = reduce_mp(
        plan, blocks, sizes
    )
    down_two, gate_two, up_two, output_two = reduced_two
    squares = [square_sum(values_one), square_sum(values_two)]
    width = D // n
    own_row = jnp.arange(D) == lax.axis_index("dp") * width
    squares = [jnp.where(own_row, square, 0.0) for square in squares]
    extra = jnp.stack([gain_one, gain_ff_one, gain_two, gain_ff_two, *squares], axis=1)
    extra = jnp.pad(extra, ((0, 0), (0, LANES - extra.shape[1])))
    if by_hand:
        part = shed(plan, normed_one, dqkv_one, extra)
    else:
        whole = [tn(normed_one, array).astype(jnp.bfloat16) for array in dqkv_one]
        part = reduce_qkv(plan, jnp.concatenate(whole, axis=1), extra)
    piece = D // m
    query_one, key_one, value_one = (part[:, i * piece : (i + 1) * piece] for i in range(3))
    shared = part[:, 3 * piece :]
    value_norms = jnp.sqrt(shared[:1, 4:6] / (TOK_DEV * D))
    return (
        between.astype(jnp.bfloat16),
        final,
        input_grad,
        shared[:, 0], query_one, key_one, value_one, output_one,
        shared[:, 1], gate_one.T, up_one.T, down_one,
        shared[:, 2], query_two.T, key_two.T, value_two.T, output_two,
        shared[:, 3], gate_two.T, up_two.T, down_two,
        value_norms,
    )


def solution(mesh):
    tokens, row_split, column_split = P(("dp", "mp"), None), P("dp", "mp"), P("mp", "dp")
    layer = (
        P("dp"), row_split, row_split, row_split, column_split, P("dp"), row_split, row_split,
        column_split,
    )
    return jax.shard_map(
        functools.partial(shards, mesh.shape["dp"], mesh.shape["mp"]),
        mesh=mesh,
        in_specs=(tokens, P(), *layer, *layer, tokens),
        out_specs=(tokens, tokens, tokens, *layer, *layer, P("dp", None)),
        check_vma=False,
    )
```

```python
import functools
import math

import jax
import jax.numpy as jnp
from jax import lax
from jax.experimental import pallas as pl
from jax.experimental.pallas import tpu as pltpu
from jax.sharding import PartitionSpec as P

D = 1024
HEAD_DIM = 64
TOK_DEV = 2048
LONGEST = 4096

LANES = 128
HEADS_HELD = LANES // HEAD_DIM
CHUNK = 1024
HALO = LONGEST - CHUNK
QUERY_ROWS = 1024
TILE = 256
EPSILON = 1e-06
MASKED = -1e30
LOG2E = math.log2(math.e)
MESH = pl.DeviceIdType.MESH
ANY = pl.BlockSpec(memory_space=pl.ANY)
VMEM = pl.BlockSpec(memory_space=pltpu.VMEM)
SMEM = pl.BlockSpec(memory_space=pltpu.SMEM)
BIG_VMEM = 56 * 1024 * 1024
BRIEF = pl.CostEstimate(flops=0, bytes_accessed=1_000, transcendentals=0)


def nn(left_side, right_side):
    return jnp.dot(left_side, right_side, preferred_element_type=jnp.float32)


def tn(left_side, right_side):
    return lax.dot_general(
        left_side, right_side, (((0,), (0,)), ((), ())), preferred_element_type=jnp.float32
    )


def nt(left_side, right_side):
    return lax.dot_general(
        left_side, right_side, (((1,), (1,)), ((), ())), preferred_element_type=jnp.float32
    )


def norm_rows(values, gain_vector):
    scaling = lax.rsqrt(jnp.mean(values * values, axis=-1, keepdims=True) + EPSILON)
    return values * scaling * gain_vector


def norm_back(values, gain_vector, grad_output):
    unused, pullback = jax.vjp(norm_rows, values, gain_vector)
    return pullback(grad_output)


class Plan:
    def __init__(self, n, m):
        self.n, self.m = n, m
        self.group = D // LANES
        self.low = self.group // m
        self.segments = n // self.low
        self.rows = TOK_DEV // m
        self.seg_rows = self.rows * self.group
        self.spans = []
        left, distance = HALO, 1
        while left > 0:
            count = min(self.seg_rows, left)
            self.spans.append((distance, left - count, count))
            left -= count
            distance += 1

    def here(self):
        dp, mp = lax.axis_index("dp"), lax.axis_index("mp")
        return dp // self.low, (dp % self.low) * self.m + mp

    def device(self, segment, member):
        return (segment * self.low + member // self.m, member % self.m)


def greet(plan, segment, member):
    barrier = pltpu.get_barrier_semaphore()
    for offset in range(1, plan.group):
        peer = lax.rem(member + offset, plan.group)
        pl.semaphore_signal(
            barrier, inc=1, device_id=plan.device(segment, peer), device_id_type=MESH
        )
    pl.semaphore_wait(barrier, plan.group - 1)


def member_copies(plan, segment, member, source, target, send, recv, own):
    copies = [pltpu.make_async_copy(source(member), target, own)]
    for offset in range(1, plan.group):
        peer = lax.rem(member + offset, plan.group)
        copies.append(
            pltpu.make_async_remote_copy(
                src_ref=source(peer),
                dst_ref=target,
                send_sem=send.at[offset],
                recv_sem=recv.at[offset],
                device_id=plan.device(segment, peer),
                device_id_type=MESH,
            )
        )
    for copy in copies[1:] + copies[:1]:
        copy.start()
    return copies


def columns(index):
    return pl.ds(pl.multiple_of(index * LANES, LANES), LANES)


def spread_kernel(plan, query, key, value, q_seg, k_seg, v_seg, send, recv, own):
    segment, member = plan.here()
    rows = plan.rows
    greet(plan, segment, member)
    copies = []
    place = pl.ds(pl.multiple_of(member * rows, rows), rows)
    for part, (array, out) in enumerate(((key, k_seg), (value, v_seg), (query, q_seg))):

        def source(peer, array=array):
            return array.at[:, columns(peer)]

        copies += member_copies(
            plan, segment, member, source, out.at[place], send.at[part], recv.at[part], own.at[part]
        )
    for copy in copies:
        copy.wait()


def spread(plan, query, key, value):
    segment = jax.ShapeDtypeStruct((plan.seg_rows, LANES), jnp.bfloat16)
    return pl.pallas_call(
        functools.partial(spread_kernel, plan),
        out_shape=(segment,) * 3,
        in_specs=[ANY] * 3,
        out_specs=(ANY, ANY, ANY),
        scratch_shapes=[
            pltpu.SemaphoreType.DMA((3, plan.group)),
            pltpu.SemaphoreType.DMA((3, plan.group)),
            pltpu.SemaphoreType.DMA((3,)),
        ],
        compiler_params=pltpu.CompilerParams(collective_id=1, has_side_effects=True),
        cost_estimate=BRIEF,
        name="spread",
    )(query, key, value)


def halo_of(plan, seg):
    parts = []
    for distance, first, count in reversed(plan.spans):
        route = [(i, i + distance * plan.low) for i in range(plan.n - distance * plan.low)]
        parts.append(lax.ppermute(seg[plan.seg_rows - count :], "dp", route))
    return parts[0] if len(parts) == 1 else jnp.concatenate(parts, axis=0)


def halo_back(plan, halo):
    parts = []
    for distance, first, count in plan.spans:
        route = [(i, i - distance * plan.low) for i in range(distance * plan.low, plan.n)]
        parts.append(lax.ppermute(halo[:, first : first + count], "dp", route))
    return parts


def to_rows_kernel(plan, seg, rows_out, send, recv, own):
    segment, member = plan.here()
    rows = plan.rows
    greet(plan, segment, member)

    def source(peer):
        return seg.at[pl.ds(pl.multiple_of(peer * rows, rows), rows)]

    for copy in member_copies(
        plan, segment, member, source, rows_out.at[:, columns(member)], send, recv, own
    ):
        copy.wait()


def to_rows(plan, seg):
    return pl.pallas_call(
        functools.partial(to_rows_kernel, plan),
        out_shape=jax.ShapeDtypeStruct((plan.rows, D), jnp.bfloat16),
        in_specs=[ANY],
        out_specs=ANY,
        scratch_shapes=[
            pltpu.SemaphoreType.DMA((plan.group,)),
            pltpu.SemaphoreType.DMA((plan.group,)),
            pltpu.SemaphoreType.DMA,
        ],
        compiler_params=pltpu.CompilerParams(collective_id=2, has_side_effects=True),
        cost_estimate=BRIEF,
        name="to_rows",
    )(seg)


def dp_place():
    dp = lax.axis_index("dp")
    return dp, dp % 2, (dp // 2) % 2, dp // 4


def greet_all(plan, dp, mp):
    barrier = pltpu.get_barrier_semaphore()
    others = [(dp, lax.rem(mp + k, plan.m)) for k in range(1, plan.m)]
    others += [(lax.rem(dp + k, plan.n), mp) for k in range(1, plan.n)]
    for other in others:
        pl.semaphore_signal(barrier, inc=1, device_id=other, device_id_type=MESH)
    pl.semaphore_wait(barrier, len(others))


def remote(source, target, send, recv, device):
    copy = pltpu.make_async_remote_copy(
        src_ref=source,
        dst_ref=target,
        send_sem=send,
        recv_sem=recv,
        device_id=device,
        device_id_type=MESH,
    )
    copy.start()
    return copy


def weave_kernel(plan, shard, gain, out, gain_out, own, *sems):
    z_send, z_recv, x_send, x_recv, y_send, y_recv, c_send, c_recv, g_send, g_recv = sems
    (dp, core, x, y), mp = dp_place(), lax.axis_index("mp")
    types, rows = shard.shape[:2]
    half = types // 2
    greet_all(plan, dp, mp)
    beside = dp + 1 - 2 * core
    dp_x, dp_y = dp + 2 - 4 * x, dp + 4 - 8 * y
    dp_xy = dp_x + 4 - 8 * y

    def block(index, column, first=0, count=types):
        z = lax.rem(mp + plan.m - index, plan.m)
        place = pl.ds(pl.multiple_of(z * rows, rows), rows)
        return out.at[pl.ds(first, count), place, columns(column)]

    def pass_on(index, column, sems, slot, device, first=0, count=types):
        region = block(index, column, first, count)
        return remote(
            region, region, sems[0].at[index, slot], sems[1].at[index, slot], (device, mp)
        )

    locals_ = [
        pltpu.make_async_copy(shard, block(0, dp), own.at[0]),
        pltpu.make_async_copy(gain, gain_out.at[:, columns(dp)], own.at[1]),
    ]
    for copy in locals_:
        copy.start()
    z_copies = [None]
    for k in range(1, plan.m):
        z_copies.append(
            remote(shard, block(0, dp), z_send.at[k], z_recv.at[k], (dp, lax.rem(mp + k, plan.m)))
        )
    copies = [
        remote(
            gain,
            gain_out.at[:, columns(dp)],
            g_send.at[k],
            g_recv.at[k],
            (lax.rem(dp + k, plan.n), mp),
        )
        for k in range(1, plan.n)
    ]
    x_sems, y_sems, c_sems = (x_send, x_recv), (y_send, y_recv), (c_send, c_recv)
    x_own, y_own, x_far, y_far, c_all = [], [], [], [], []

    def first_stage(index):
        if index == 0:
            for copy in locals_:
                copy.wait()
        else:
            z_copies[index].wait_recv()
        x_own.append(pass_on(index, dp, x_sems, 0, dp_x))
        y_own.append(pass_on(index, dp, y_sems, 0, dp_y))
        c_all.append(pass_on(index, dp, c_sems, 0, beside))

    def second_stage(index):
        x_own[index].wait_recv()
        y_far.append(pass_on(index, dp_x, y_sems, 1, dp_y, 0, half))
        c_all.append(pass_on(index, dp_x, c_sems, 1, beside))
        y_own[index].wait_recv()
        x_far.append(pass_on(index, dp_y, x_sems, 1, dp_x, half, types - half))
        c_all.append(pass_on(index, dp_y, c_sems, 2, beside))

    def third_stage(index):
        y_far[index].wait_recv()
        c_all.append(pass_on(index, dp_xy, c_sems, 3, beside, 0, half))
        x_far[index].wait_recv()
        c_all.append(pass_on(index, dp_xy, c_sems, 4, beside, half, types - half))

    for step in range(plan.m + 2):
        if step < plan.m:
            first_stage(step)
        if 1 <= step < plan.m + 1:
            second_stage(step - 1)
        if step >= 2:
            third_stage(step - 2)
    for copy in copies + c_all:
        copy.wait()
    for copy in z_copies[1:] + x_own + y_own + x_far + y_far:
        copy.wait_send()


def weave(plan, shard, gain):
    types, rows = shard.shape[:2]
    dma = pltpu.SemaphoreType.DMA
    return pl.pallas_call(
        functools.partial(weave_kernel, plan),
        in_specs=[ANY, ANY],
        out_specs=(ANY, ANY),
        out_shape=(
            jax.ShapeDtypeStruct((types, plan.m * rows, D), jnp.bfloat16),
            jax.ShapeDtypeStruct((gain.shape[0], D), jnp.bfloat16),
        ),
        scratch_shapes=[dma((2,))]
        + [dma((plan.m,))] * 2
        + [dma((plan.m, 2))] * 4
        + [dma((plan.m, 5))] * 2
        + [dma((plan.n,))] * 2,
        compiler_params=pltpu.CompilerParams(collective_id=6, has_side_effects=True),
        cost_estimate=BRIEF,
        name="weave",
    )(shard, gain)


def shed_kernel(plan, normed, dq, dk, dv, extra, out, left, parts, from_core, sums, *rest):
    from_first, sums_first, from_second, blocks, from_z, c_sems, f_sems, s_sems, z_sems = rest
    (dp, core, x, y), mp = dp_place(), lax.axis_index("mp")
    width = D // plan.n
    wide = D // 2
    greet_all(plan, dp, mp)
    beside, dp_x, dp_y = dp + 1 - 2 * core, dp + 2 - 4 * x, dp + 4 - 8 * y

    def rows_of(index):
        return pl.ds(pl.multiple_of(index * width, width), width)

    def plus(one, other):
        return (one.astype(jnp.float32) + other.astype(jnp.float32)).astype(jnp.bfloat16)

    left[...] = normed[...].T
    c_copies, first, second = [], [], []
    for half in range(2):
        for kind, array in enumerate((dq, dk, dv)):
            place = slice(kind * wide, (kind + 1) * wide)
            source = slice(half * wide, (half + 1) * wide)
            parts[half, :, place] = nn(left[...], array[:, source]).astype(jnp.bfloat16)
        parts[half, :, 3 * wide :] = extra[...].astype(jnp.bfloat16)
        c_copies.append(
            [
                remote(
                    parts.at[half, rows_of(2 * j + 1 - core)],
                    from_core.at[half, j],
                    c_sems.at[0, half, j],
                    c_sems.at[1, half, j],
                    (beside, mp),
                )
                for j in range(4)
            ]
        )
    for half in range(2):
        for j in range(4):
            c_copies[half][j].wait_recv()
            sums[half, j] = plus(parts[half, rows_of(2 * j + core), :], from_core[half, j])
        for k in range(2):
            away = 2 * k + 1 - x if half == 0 else 2 * (1 - y) + k
            first.append(
                remote(
                    sums.at[half, away],
                    from_first.at[half, k],
                    f_sems.at[0, half, k],
                    f_sems.at[1, half, k],
                    (dp_x if half == 0 else dp_y, mp),
                )
            )
    for half in range(2):
        for k in range(2):
            first[2 * half + k].wait_recv()
            kept = 2 * k + x if half == 0 else 2 * y + k
            sums_first[half, k] = plus(sums[half, kept], from_first[half, k])
        second.append(
            remote(
                sums_first.at[half, 1 - y if half == 0 else 1 - x],
                from_second.at[half],
                s_sems.at[0, half],
                s_sems.at[1, half],
                (dp_y if half == 0 else dp_x, mp),
            )
        )
    piece = D // plan.m
    for half in range(2):
        second[half].wait_recv()
        total = plus(sums_first[half, y if half == 0 else x], from_second[half])
        for member in range(2):
            index = 2 * half + member
            for kind in range(3):
                start = kind * wide + member * piece
                blocks[index, :, kind * piece : (kind + 1) * piece] = total[:, start : start + piece]
            blocks[index, :, 3 * piece :] = total[:, 3 * wide :]
    z_copies = []
    for k in range(1, plan.m):
        peer = lax.rem(mp + k, plan.m)
        z_copies.append(
            remote(
                blocks.at[peer], from_z.at[k], z_sems.at[0, k], z_sems.at[1, k], (dp, peer)
            )
        )
    result = blocks[mp].astype(jnp.float32)
    for k in range(1, plan.m):
        z_copies[k - 1].wait_recv()
        result = result + from_z[k].astype(jnp.float32)
    out[...] = result
    for copy in c_copies[0] + c_copies[1] + first + second + z_copies:
        copy.wait_send()


def shed(plan, normed, dqkv, extra):
    dma = pltpu.SemaphoreType.DMA
    width, wide, kept = D // plan.n, 3 * (D // 2) + LANES, 3 * (D // plan.m) + LANES

    def held(*shape):
        return pltpu.VMEM(shape, jnp.bfloat16)

    return pl.pallas_call(
        functools.partial(shed_kernel, plan),
        in_specs=[VMEM] * 5,
        out_specs=VMEM,
        out_shape=jax.ShapeDtypeStruct((width, kept), jnp.float32),
        scratch_shapes=[
            held(D, normed.shape[0]),
            held(2, D, wide),
            held(2, 4, width, wide),
            held(2, 4, width, wide),
            held(2, 2, width, wide),
            held(2, 2, width, wide),
            held(2, width, wide),
            held(plan.m, width, kept),
            held(plan.m, width, kept),
            dma((2, 2, 4)),
            dma((2, 2, 2)),
            dma((2, 2)),
            dma((2, plan.m)),
        ],
        compiler_params=pltpu.CompilerParams(
            collective_id=7, has_side_effects=True, vmem_limit_bytes=BIG_VMEM
        ),
        cost_estimate=BRIEF,
        name="shed",
    )(normed, *dqkv, extra)


def products_kernel(plan, sides, *refs):
    rows_in, refs = refs[0], refs[1:]
    lefts, rights = refs[: len(set(sides))], refs[len(set(sides)) : len(set(sides)) + len(sides)]
    seg, out, left_sides, tiles, send, recv, own, sent = refs[len(lefts) + len(rights) :]
    segment, member = plan.here()
    rows = plan.rows
    greet(plan, segment, member)

    def source(peer):
        return rows_in.at[:, columns(peer)]

    place = seg.at[pl.ds(pl.multiple_of(member * rows, rows), rows)]
    copies = member_copies(plan, segment, member, source, place, send, recv, own)
    for index, array in enumerate(lefts):
        left_sides[index] = array[...].T
    start, pending = 0, [None, None]
    slot = 0
    for array, side in zip(rights, sides):
        size = array.shape[1]
        width = size // 2 if size % (2 * LANES) == 0 and size > D else D
        for first in range(0, size, width):
            if pending[slot] is not None:
                pending[slot].wait()
            tiles[slot, :, :width] = nn(
                left_sides[side], array[:, first : first + width]
            ).astype(jnp.bfloat16)
            pending[slot] = pltpu.make_async_copy(
                tiles.at[slot, :, :width], out.at[:, pl.ds(start, width)], sent.at[slot]
            )
            pending[slot].start()
            start += width
            slot = 1 - slot
    for copy in pending + copies:
        copy.wait()


def products(plan, rows_in, lefts, rights, sides):
    rows, widest = lefts[0].shape[0], max(array.shape[1] for array in rights) // 2
    total = sum(array.shape[1] for array in rights)
    return pl.pallas_call(
        functools.partial(products_kernel, plan, sides),
        in_specs=[ANY] + [VMEM] * (len(lefts) + len(rights)),
        out_specs=(ANY, ANY),
        out_shape=(
            jax.ShapeDtypeStruct((plan.seg_rows, LANES), jnp.bfloat16),
            jax.ShapeDtypeStruct((D, total), jnp.bfloat16),
        ),
        scratch_shapes=[
            pltpu.VMEM((len(lefts), D, rows), jnp.bfloat16),
            pltpu.VMEM((2, D, widest), jnp.bfloat16),
            pltpu.SemaphoreType.DMA((plan.group,)),
            pltpu.SemaphoreType.DMA((plan.group,)),
            pltpu.SemaphoreType.DMA,
            pltpu.SemaphoreType.DMA((2,)),
        ],
        compiler_params=pltpu.CompilerParams(
            collective_id=len(lefts), has_side_effects=True, vmem_limit_bytes=BIG_VMEM
        ),
        cost_estimate=BRIEF,
        name="products",
    )(rows_in, *lefts, *rights)


def collect_kernel(plan, spans, more, *refs):
    parts = 1 if spans == 0 else 2
    arrays, halos, refs = refs[:parts], refs[parts : parts + spans], refs[parts + spans :]
    beside, refs = refs[:more], refs[more:]
    outs, refs = refs[:parts], refs[parts:]
    total, send, recv, own = refs[-4:]
    segment, member = plan.here()
    rows = plan.rows
    greet(plan, segment, member)
    copies = []
    for part, array in enumerate(arrays):
        if spans:
            for piece in range(plan.seg_rows // CHUNK):
                start = piece * CHUNK
                value = array[pl.ds(start, CHUNK), :]
                for index, (distance, first, count) in enumerate(plan.spans):
                    offset = start - (plan.seg_rows - count)
                    if offset >= 0:
                        halo = halos[index][part, pl.ds(offset, CHUNK), :]
                        value = value + halo.astype(jnp.float32)
                total[part, pl.ds(start, CHUNK), :] = value.astype(jnp.bfloat16)
            array = total.at[part]

        def source(peer, array=array):
            return array.at[pl.ds(pl.multiple_of(peer * rows, rows), rows)]

        copies += member_copies(
            plan,
            segment,
            member,
            source,
            outs[part].at[:, columns(member)],
            send.at[part],
            recv.at[part],
            own.at[part],
        )
    if beside:
        (hidden, weights, middle), (final, down, loaded) = beside, refs[:3]
        load = pltpu.make_async_copy(weights.at[2], down, loaded)
        load.start()
        load.wait()
        for first in range(0, D, TILE):
            place = slice(first, first + TILE)
            final[:, place] = (middle[:, place] + nn(hidden[...], down[:, place])).astype(
                jnp.bfloat16
            )
    for copy in copies:
        copy.wait()


def collect(plan, arrays, halos, beside=()):
    parts, spans = len(arrays), len(plan.spans) if halos else 0
    return pl.pallas_call(
        functools.partial(collect_kernel, plan, spans, len(beside)),
        out_shape=(jax.ShapeDtypeStruct((plan.rows, D), jnp.bfloat16),) * (parts + bool(beside)),
        in_specs=[VMEM] * (parts + len(halos)) + [VMEM, ANY, VMEM][: len(beside)],
        out_specs=(ANY,) * parts + (VMEM,) * bool(beside),
        scratch_shapes=[pltpu.VMEM(one.shape[1:], one.dtype) for one in beside[1:2]]
        + [pltpu.SemaphoreType.DMA] * bool(beside)
        + [
            pltpu.VMEM((parts, plan.seg_rows if halos else 16, LANES), jnp.bfloat16),
            pltpu.SemaphoreType.DMA((parts, plan.group)),
            pltpu.SemaphoreType.DMA((parts, plan.group)),
            pltpu.SemaphoreType.DMA((parts,)),
        ],
        compiler_params=pltpu.CompilerParams(
            collective_id=5 if halos else 9 if beside else 8, has_side_effects=True, vmem_limit_bytes=BIG_VMEM
        ),
        cost_estimate=BRIEF,
        name="collect_kv" if halos else "collect_q",
    )(*arrays, *halos, *beside)


def swap_halves(values):
    lane = lax.broadcasted_iota(jnp.int32, values.shape, 1)
    half = HEAD_DIM // 2
    ahead = pltpu.roll(values, LANES - half, 1)
    behind = pltpu.roll(values, half, 1)
    return jnp.where(lax.rem(lane, HEAD_DIM) < half, ahead, behind)


def rotate(values, cosine, sine):
    return values * cosine + swap_halves(values) * sine


def of_head(values, head):
    lane = lax.broadcasted_iota(jnp.int32, values.shape, 1)
    return jnp.where(lane // HEAD_DIM == head, values, jnp.zeros_like(values))


def chunk_rows(index, size):
    return pl.ds(pl.multiple_of(index * size, size), size)


HALO_CHUNKS = HALO // CHUNK


def rotate_keys(prior, first, keys, cosine, sine, k_turned):
    def one(index, unused):
        table = chunk_rows(prior[first + index], CHUNK)
        rows = chunk_rows(index, CHUNK)
        k_turned[rows, :] = rotate(
            keys[rows, :].astype(jnp.float32), cosine[table, :], sine[table, :]
        ).astype(jnp.bfloat16)
        return unused

    lax.fori_loop(0, keys.shape[0] // CHUNK, one, 0)


def query_tables(prior, block, cosine, sine):
    rows = chunk_rows(prior[HALO_CHUNKS + block], QUERY_ROWS)
    return cosine[rows, :], sine[rows, :]


def turned_queries(prior, block, queries, cosine, sine):
    cos_rows, sin_rows = query_tables(prior, block, cosine, sine)
    turned = rotate(queries.astype(jnp.float32), cos_rows, sin_rows)
    return (turned * (LOG2E * HEAD_DIM ** (-0.5))).astype(jnp.bfloat16)


def by_head(parts):
    whole = parts[0]
    lane = lax.broadcasted_iota(jnp.int32, whole.shape, 1)
    for head in range(1, HEADS_HELD):
        whole = jnp.where(lane // HEAD_DIM == head, parts[head], whole)
    return whole


def needs_halo(prior, own_chunks):
    needed = prior[HALO_CHUNKS] > 0
    for chunk in range(1, min(own_chunks, HALO_CHUNKS)):
        needed = needed | (prior[HALO_CHUNKS + chunk] > chunk)
    return needed


ROW_PARTS = 4
UNITS = [(head, part) for part in range(ROW_PARTS) for head in range(HEADS_HELD)]


def add_keys(refs, first, diagonal):
    q_head, k_turned, v_wide, top, total = refs
    start_row = pl.multiple_of(first * CHUNK, CHUNK)
    part_rows = QUERY_ROWS // ROW_PARTS

    def queries(part):
        return slice(part * part_rows, (part + 1) * part_rows)

    def keys(part):
        return pl.ds(start_row, (part + 1) * part_rows if diagonal else CHUNK)

    def start(unit):
        head, part = unit
        return nt(q_head[head, queries(part), :], k_turned[keys(part), :])

    def finish(unit, scores):
        head, part = unit
        held = (head, queries(part))
        value_block = v_wide[keys(part), :]
        if diagonal:
            place = lax.broadcasted_iota(jnp.int32, scores.shape, 0) + part * part_rows
            other = lax.broadcasted_iota(jnp.int32, scores.shape, 1)
            scores = jnp.where(other <= place, scores, MASKED)
        highest = jnp.max(scores, axis=1, keepdims=True)
        if diagonal:
            weights = jnp.exp2((scores - highest).astype(jnp.bfloat16))
            total[held] = nn(weights, value_block)
            top[held] = jnp.broadcast_to(highest, (part_rows, LANES))
        else:
            before = top[held]
            after = jnp.maximum(before, highest)
            weights = jnp.exp2((scores - after[:, :1]).astype(jnp.bfloat16))
            shrink = jnp.exp2(before - after)
            shrink = jnp.concatenate([shrink, shrink], axis=1)
            total[held] = total[held] * shrink + nn(weights, value_block)
            top[held] = after

    scores = start(UNITS[0])
    for index, unit in enumerate(UNITS):
        following = start(UNITS[index + 1]) if index + 1 < len(UNITS) else None
        finish(unit, scores)
        scores = following


def mixed_of(total):
    return by_head([total[head, :, :LANES] / total[head, :, LANES:] for head in range(HEADS_HELD)])


def attend_own_kernel(
    prior, q_ref, keys, values, cosine, sine, out_ref, top_ref, sum_ref, *scratch
):
    k_turned, v_wide, q_head, top, total = scratch
    block = pl.program_id(0)

    @pl.when(block == 0)
    def _():
        rotate_keys(prior, HALO_CHUNKS, keys, cosine, sine, k_turned)
        v_wide[:, :LANES] = values[...]
        v_wide[:, LANES:] = jnp.ones((values.shape[0], LANES), jnp.bfloat16)

    turned = turned_queries(prior, block, q_ref[...], cosine, sine)
    for head in range(HEADS_HELD):
        q_head[head] = of_head(turned, head)
    held = (q_head, k_turned, v_wide, top, total)
    add_keys(held, block, True)

    def earlier_chunk(index, unused):
        add_keys(held, block - 1 - index, False)
        return unused

    lax.fori_loop(0, jnp.minimum(prior[HALO_CHUNKS + block], block), earlier_chunk, 0)
    out_ref[...] = mixed_of(total).astype(jnp.bfloat16)
    top_ref[...] = by_head([top[head] for head in range(HEADS_HELD)])
    sum_ref[...] = by_head([total[head, :, LANES:] for head in range(HEADS_HELD)])


def attend_own(prior, q_seg, keys, values, cosine, sine):
    seg_rows = q_seg.shape[0]
    query_spec = pl.BlockSpec((QUERY_ROWS, LANES), lambda i, prior: (i, 0))
    wide = jax.ShapeDtypeStruct((seg_rows, LANES), jnp.float32)
    return pl.pallas_call(
        attend_own_kernel,
        grid_spec=pltpu.PrefetchScalarGridSpec(
            num_scalar_prefetch=1,
            grid=(seg_rows // QUERY_ROWS,),
            in_specs=[query_spec, VMEM, VMEM, VMEM, VMEM],
            out_specs=(query_spec,) * 3,
            scratch_shapes=[
                pltpu.VMEM((seg_rows, LANES), jnp.bfloat16),
                pltpu.VMEM((seg_rows, 2 * LANES), jnp.bfloat16),
                pltpu.VMEM((HEADS_HELD, QUERY_ROWS, LANES), jnp.bfloat16),
                pltpu.VMEM((HEADS_HELD, QUERY_ROWS, LANES), jnp.float32),
                pltpu.VMEM((HEADS_HELD, QUERY_ROWS, 2 * LANES), jnp.float32),
            ],
        ),
        out_shape=(jax.ShapeDtypeStruct((seg_rows, LANES), jnp.bfloat16), wide, wide),
        compiler_params=pltpu.CompilerParams(vmem_limit_bytes=BIG_VMEM),
        cost_estimate=BRIEF,
        name="attend_own",
    )(prior, q_seg, keys, values, cosine, sine)


def copy_in(pairs, sems):
    copies = [
        pltpu.make_async_copy(source, target, sems.at[index])
        for index, (source, target) in enumerate(pairs)
    ]
    for copy in copies:
        copy.start()
    for copy in copies:
        copy.wait()


def attend_halo_kernel(
    own_chunks, prior, q_seg, keys, values, cos_hbm, sin_hbm, out_in, top_in, sum_in,
    out, top_out, sum_out, *scratch
):
    k_turned, v_wide, q_head, top, total, key_rows, value_rows, cosine, sine = scratch[:9]
    q_rows, out_rows, top_rows, sum_rows, sems = scratch[9:]

    def one_block(block, unused):
        count = prior[HALO_CHUNKS + block] - block
        rows = chunk_rows(block, QUERY_ROWS)

        @pl.when(count > 0)
        def _():
            turned = turned_queries(prior, block, q_rows[rows, :], cosine, sine)
            mixed, tops, sums = out_rows[rows, :], top_rows[rows, :], sum_rows[rows, :]
            for head in range(HEADS_HELD):
                lane = head * HEAD_DIM
                q_head[head] = of_head(turned, head)
                top[head] = jnp.broadcast_to(tops[:, lane : lane + 1], top.shape[1:])
                weight = jnp.broadcast_to(sums[:, lane : lane + 1], top.shape[1:])
                total[head, :, :LANES] = mixed.astype(jnp.float32) * weight
                total[head, :, LANES:] = weight

            def earlier_chunk(index, unused):
                held = (q_head, k_turned, v_wide, top, total)
                add_keys(held, HALO_CHUNKS - 1 - index, False)
                return unused

            lax.fori_loop(0, count, earlier_chunk, 0)
            out_rows[rows, :] = mixed_of(total).astype(jnp.bfloat16)
            top_rows[rows, :] = by_head([top[head] for head in range(HEADS_HELD)])
            sum_rows[rows, :] = by_head([total[head, :, LANES:] for head in range(HEADS_HELD)])

        return unused

    @pl.when(needs_halo(prior, own_chunks))
    def _():
        part = pl.ds(0, q_rows.shape[0])
        held = ((out, out_rows), (top_out, top_rows), (sum_out, sum_rows))
        copy_in(
            (
                (keys, key_rows), (values, value_rows), (cos_hbm, cosine), (sin_hbm, sine),
                (q_seg.at[part], q_rows), *((hbm.at[part], rows) for hbm, rows in held),
            ),
            sems,
        )
        rotate_keys(prior, 0, key_rows, cosine, sine, k_turned)
        v_wide[:, :LANES] = value_rows[...]
        v_wide[:, LANES:] = jnp.ones((value_rows.shape[0], LANES), jnp.bfloat16)
        lax.fori_loop(0, q_rows.shape[0] // QUERY_ROWS, one_block, 0)
        copy_in([(rows, hbm.at[part]) for hbm, rows in held], sems)


def attend_halo(prior, q_seg, keys, values, cosine, sine, earlier):
    part = (min(q_seg.shape[0], HALO), LANES)
    per_head = (HEADS_HELD, QUERY_ROWS, LANES)
    return pl.pallas_call(
        functools.partial(attend_halo_kernel, q_seg.shape[0] // CHUNK),
        in_specs=[SMEM] + [ANY] * 8,
        out_specs=(ANY,) * 3,
        out_shape=tuple(jax.ShapeDtypeStruct(one.shape, one.dtype) for one in earlier),
        scratch_shapes=[
            pltpu.VMEM((HALO, LANES), jnp.bfloat16),
            pltpu.VMEM((HALO, 2 * LANES), jnp.bfloat16),
            pltpu.VMEM(per_head, jnp.bfloat16),
            pltpu.VMEM(per_head, jnp.float32),
            pltpu.VMEM((HEADS_HELD, QUERY_ROWS, 2 * LANES), jnp.float32),
            pltpu.VMEM((HALO, LANES), jnp.bfloat16),
            pltpu.VMEM((HALO, LANES), jnp.bfloat16),
            pltpu.VMEM((LONGEST, LANES), jnp.float32),
            pltpu.VMEM((LONGEST, LANES), jnp.float32),
            pltpu.VMEM(part, jnp.bfloat16),
            pltpu.VMEM(part, jnp.bfloat16),
            pltpu.VMEM(part, jnp.float32),
            pltpu.VMEM(part, jnp.float32),
            pltpu.SemaphoreType.DMA((8,)),
        ],
        input_output_aliases={6: 0, 7: 1, 8: 2},
        compiler_params=pltpu.CompilerParams(vmem_limit_bytes=BIG_VMEM),
        cost_estimate=BRIEF,
        name="attend_halo",
    )(prior, q_seg, keys, values, cosine, sine, *earlier)


def prepare_back(refs, block, prior, queries, grads, mixed, tops, sums, cosine, sine):
    q_head, grad_head, row_stats = refs
    turned = turned_queries(prior, block, queries, cosine, sine)
    grads = grads.astype(jnp.float32) / sums
    dots = (grads * mixed.astype(jnp.float32)).T
    tops = tops.T
    grads = grads.astype(jnp.bfloat16)
    for head in range(HEADS_HELD):
        q_head[head] = of_head(turned, head)
        grad_head[head] = of_head(grads, head)
        lanes = slice(head * HEAD_DIM, (head + 1) * HEAD_DIM)
        row_stats[head, 0:1, :] = tops[head * HEAD_DIM : head * HEAD_DIM + 1, :]
        row_stats[head, 1:2, :] = jnp.sum(dots[lanes, :], axis=0, keepdims=True)


def add_keys_back(refs, first, diagonal):
    q_head, grad_head, row_stats, k_turned, values, dq_total, dk_total, dv_total = refs
    part_rows = QUERY_ROWS // ROW_PARTS

    def keys(part):
        start = pl.multiple_of(first * CHUNK + part * part_rows, part_rows)
        return pl.ds(start, part_rows)

    def queries(part):
        return slice(part * part_rows if diagonal else 0, QUERY_ROWS)

    def start(unit):
        head, part = unit
        rows, wanted = keys(part), queries(part)
        return (
            nt(k_turned[rows, :], q_head[head, wanted, :]),
            nt(values[rows, :], grad_head[head, wanted, :]),
        )

    def finish(unit, products_):
        head, part = unit
        rows, wanted = keys(part), queries(part)
        scores, grad_weights = products_
        weights = jnp.exp2((scores - row_stats[head, 0:1, wanted]).astype(jnp.bfloat16))
        if diagonal:
            other = lax.broadcasted_iota(jnp.int32, scores.shape, 0)
            place = lax.broadcasted_iota(jnp.int32, scores.shape, 1)
            weights = jnp.where(other <= place, weights, jnp.zeros_like(weights))
        grad_scores = weights * (grad_weights - row_stats[head, 1:2, wanted]).astype(jnp.bfloat16)
        dv_total[rows, :] += nn(weights, grad_head[head, wanted, :])
        dk_total[rows, :] += nn(grad_scores, q_head[head, wanted, :])
        dq_total[head, wanted, :] += tn(grad_scores, k_turned[rows, :])

    held = start(UNITS[0])
    for index, unit in enumerate(UNITS):
        following = start(UNITS[index + 1]) if index + 1 < len(UNITS) else None
        finish(unit, held)
        held = following


def turn_keys_back(prior, first_chunk, dk_total, dv_total, cosine, sine, dk_ref, dv_ref):
    def one(index, unused):
        table = chunk_rows(prior[first_chunk + index], CHUNK)
        rows = chunk_rows(index, CHUNK)
        turned = rotate(dk_total[rows, :], cosine[table, :], -sine[table, :]) * (1.0 / LOG2E)
        dk_ref[rows, :] = turned.astype(dk_ref.dtype)
        dv_ref[rows, :] = dv_total[rows, :].astype(dv_ref.dtype)
        return unused

    lax.fori_loop(0, dk_ref.shape[0] // CHUNK, one, 0)


def attend_back_own_kernel(
    prior, q_ref, grad_ref, out_ref, top_ref, sum_ref, keys, values, cosine, sine, dq_part,
    dq_ref, dk_ref, dv_ref, k_turned, q_head, grad_head, dq_total, dk_total, dv_total, row_stats
):
    block = pl.program_id(0)
    chunks_back = prior[HALO_CHUNKS + block]

    @pl.when(block == 0)
    def _():
        rotate_keys(prior, HALO_CHUNKS, keys, cosine, sine, k_turned)
        dk_total[...] = jnp.zeros_like(dk_total)
        dv_total[...] = jnp.zeros_like(dv_total)

    prepare_back(
        (q_head, grad_head, row_stats), block, prior, q_ref[...], grad_ref[...], out_ref[...],
        top_ref[...], sum_ref[...], cosine, sine,
    )
    from_halo = jnp.where(chunks_back > block, dq_part[...], jnp.zeros_like(dq_part))
    for head in range(HEADS_HELD):
        dq_total[head] = from_halo
    held = (q_head, grad_head, row_stats, k_turned, values, dq_total, dk_total, dv_total)
    add_keys_back(held, block, True)

    def whole(index, unused):
        add_keys_back(held, index, False)
        return unused

    lax.fori_loop(jnp.maximum(block - chunks_back, 0), block, whole, 0)
    cos_rows, sin_rows = query_tables(prior, block, cosine, sine)
    turned = rotate(by_head([dq_total[head] for head in range(HEADS_HELD)]), cos_rows, -sin_rows)
    dq_ref[...] = (turned * HEAD_DIM ** (-0.5)).astype(jnp.bfloat16)

    @pl.when(block == pl.num_programs(0) - 1)
    def _():
        turn_keys_back(prior, HALO_CHUNKS, dk_total, dv_total, cosine, sine, dk_ref, dv_ref)


def back_scratch(key_rows):
    per_head = (HEADS_HELD, QUERY_ROWS, LANES)
    return [
        pltpu.VMEM((key_rows, LANES), jnp.bfloat16),
        pltpu.VMEM(per_head, jnp.bfloat16),
        pltpu.VMEM(per_head, jnp.bfloat16),
        pltpu.VMEM(per_head, jnp.float32),
        pltpu.VMEM((key_rows, LANES), jnp.float32),
        pltpu.VMEM((key_rows, LANES), jnp.float32),
        pltpu.VMEM((HEADS_HELD, 8, QUERY_ROWS), jnp.float32),
    ]


def attend_back_own(prior, q_seg, grad_seg, seen, keys, values, cosine, sine, dq_part):
    seg_rows = q_seg.shape[0]
    query_spec = pl.BlockSpec((QUERY_ROWS, LANES), lambda i, prior: (i, 0))
    wide = jax.ShapeDtypeStruct((seg_rows, LANES), jnp.float32)
    return pl.pallas_call(
        attend_back_own_kernel,
        grid_spec=pltpu.PrefetchScalarGridSpec(
            num_scalar_prefetch=1,
            grid=(seg_rows // QUERY_ROWS,),
            in_specs=[query_spec] * 5 + [VMEM] * 4 + [query_spec],
            out_specs=(query_spec, VMEM, VMEM),
            scratch_shapes=back_scratch(seg_rows),
        ),
        out_shape=(jax.ShapeDtypeStruct((seg_rows, LANES), jnp.bfloat16), wide, wide),
        compiler_params=pltpu.CompilerParams(vmem_limit_bytes=BIG_VMEM),
        cost_estimate=BRIEF,
        name="attend_back_own",
    )(prior, q_seg, grad_seg, *seen, keys, values, cosine, sine, dq_part)


def attend_back_halo_kernel(
    own_chunks, prior, q_seg, grad_seg, mixed, tops, sums, keys, values, cos_hbm, sin_hbm,
    dq_out, halves_out, *scratch
):
    k_turned, q_head, grad_head, dq_total, dk_total, dv_total, row_stats = scratch[:7]
    key_rows, value_rows, cosine, sine, dk_half, dv_half = scratch[7:13]
    q_rows, grad_rows, out_rows, top_rows, sum_rows, dq_rows, sems = scratch[13:]
    needed = needs_halo(prior, own_chunks)
    part = pl.ds(0, q_rows.shape[0])

    def one_block(block, unused):
        chunks_back = prior[HALO_CHUNKS + block]
        rows = chunk_rows(block, QUERY_ROWS)

        @pl.when(chunks_back > block)
        def _():
            prepare_back(
                (q_head, grad_head, row_stats), block, prior, q_rows[rows, :], grad_rows[rows, :],
                out_rows[rows, :], top_rows[rows, :], sum_rows[rows, :], cosine, sine,
            )
            dq_total[...] = jnp.zeros_like(dq_total)

            def whole(index, unused):
                add_keys_back(
                    (
                        q_head, grad_head, row_stats, k_turned, value_rows, dq_total, dk_total,
                        dv_total,
                    ),
                    index,
                    False,
                )
                return unused

            lax.fori_loop(HALO_CHUNKS + block - chunks_back, HALO_CHUNKS, whole, 0)
            dq_rows[rows, :] = by_head([dq_total[head] for head in range(HEADS_HELD)])

        return unused

    @pl.when(needed)
    def _():
        copy_in(
            (
                (keys, key_rows), (values, value_rows), (cos_hbm, cosine), (sin_hbm, sine),
                (q_seg.at[part], q_rows), (grad_seg.at[part], grad_rows),
                (mixed.at[part], out_rows), (tops.at[part], top_rows), (sums.at[part], sum_rows),
            ),
            sems,
        )
        rotate_keys(prior, 0, key_rows, cosine, sine, k_turned)
        dk_total[...] = jnp.zeros_like(dk_total)
        dv_total[...] = jnp.zeros_like(dv_total)
        lax.fori_loop(0, q_rows.shape[0] // QUERY_ROWS, one_block, 0)
        turn_keys_back(prior, 0, dk_total, dv_total, cosine, sine, dk_half, dv_half)
        copy_in(((dq_rows, dq_out.at[part]),), sems)

    @pl.when(jnp.logical_not(needed))
    def _():
        dk_half[...] = jnp.zeros_like(dk_half)
        dv_half[...] = jnp.zeros_like(dv_half)

    copy_in(((dk_half, halves_out.at[0]), (dv_half, halves_out.at[1])), sems)


def attend_back_halo(prior, q_seg, grad_seg, seen, keys, values, cosine, sine):
    seg_rows = q_seg.shape[0]
    part = (min(seg_rows, HALO), LANES)
    return pl.pallas_call(
        functools.partial(attend_back_halo_kernel, seg_rows // CHUNK),
        in_specs=[SMEM] + [ANY] * 9,
        out_specs=(ANY,) * 2,
        out_shape=(
            jax.ShapeDtypeStruct((seg_rows, LANES), jnp.float32),
            jax.ShapeDtypeStruct((2, HALO, LANES), jnp.bfloat16),
        ),
        scratch_shapes=back_scratch(HALO)
        + [
            pltpu.VMEM((HALO, LANES), jnp.bfloat16),
            pltpu.VMEM((HALO, LANES), jnp.bfloat16),
            pltpu.VMEM((LONGEST, LANES), jnp.float32),
            pltpu.VMEM((LONGEST, LANES), jnp.float32),
            pltpu.VMEM((HALO, LANES), jnp.bfloat16),
            pltpu.VMEM((HALO, LANES), jnp.bfloat16),
            pltpu.VMEM(part, jnp.bfloat16),
            pltpu.VMEM(part, jnp.bfloat16),
            pltpu.VMEM(part, jnp.bfloat16),
            pltpu.VMEM(part, jnp.float32),
            pltpu.VMEM(part, jnp.float32),
            pltpu.VMEM(part, jnp.float32),
            pltpu.SemaphoreType.DMA((9,)),
        ],
        compiler_params=pltpu.CompilerParams(vmem_limit_bytes=BIG_VMEM),
        cost_estimate=BRIEF,
        name="attend_back_halo",
    )(prior, q_seg, grad_seg, *seen, keys, values, cosine, sine)


def attention(plan, tables, q_seg, k_seg, v_seg):
    k_halo, v_halo = halo_of(plan, k_seg), halo_of(plan, v_seg)
    earlier = attend_own(tables[0], q_seg, k_seg, v_seg, *tables[1:])
    seen = attend_halo(tables[0], q_seg, k_halo, v_halo, *tables[1:], earlier)
    return seen[0], (q_seg, k_seg, v_seg, k_halo, v_halo, seen)


def attention_back(plan, tables, kept, grad_seg, waiting, late, beside=()):
    q_seg, k_seg, v_seg, k_halo, v_halo, seen = kept
    queries = (tables[0], q_seg, grad_seg, seen)
    dq_part, halves = attend_back_halo(*queries, k_halo, v_halo, *tables[1:])
    halos = halo_back(plan, halves)
    dq, dk_own, dv_own = attend_back_own(*queries, k_seg, v_seg, *tables[1:], dq_part)
    dq, waiting = lax.optimization_barrier((dq, waiting))
    dq, *final = collect(plan, (dq,), (), beside)
    dq, *halos = lax.optimization_barrier((dq, *halos))
    dkv, late = lax.optimization_barrier((collect(plan, (dk_own, dv_own), halos), late))
    return (dq, *dkv), waiting, late, *final


def rotary_tables():
    half = HEAD_DIM // 2
    lane = jnp.arange(LANES)
    frequency = jnp.exp(
        (lane % half).astype(jnp.float32) * (-2.0 * math.log(10000.0) / HEAD_DIM)
    )
    sign = jnp.where(lane % HEAD_DIM < half, -1.0, 1.0).astype(jnp.float32)
    step = 64
    fine = jnp.arange(step).astype(jnp.float32)[:, None] * frequency[None, :]
    coarse = jnp.arange(0, LONGEST, step).astype(jnp.float32)[:, None] * frequency[None, :]
    cos_fine, sin_fine, cos_coarse, sin_coarse = lax.optimization_barrier(
        (jnp.cos(fine), jnp.sin(fine), jnp.cos(coarse), jnp.sin(coarse))
    )
    cosine = cos_coarse[:, None] * cos_fine[None] - sin_coarse[:, None] * sin_fine[None]
    sine = sin_coarse[:, None] * cos_fine[None] + cos_coarse[:, None] * sin_fine[None]
    return (
        cosine.reshape(LONGEST, LANES),
        (sine * sign).reshape(LONGEST, LANES),
    )


def chunks_before(plan, lengths):
    segment, unused = plan.here()
    count = (HALO + plan.seg_rows) // CHUNK
    places = segment * plan.seg_rows - HALO + CHUNK * jnp.arange(count)
    ends = jnp.cumsum(lengths)
    passed = ends[None, :] <= places[:, None]
    opening = jnp.max(jnp.where(passed, ends[None, :], 0), axis=1)
    return jnp.clip((places - opening) // CHUNK, 0, HALO_CHUNKS).astype(jnp.int32)


def tied(array, *others):
    return lax.optimization_barrier((array, *others))[0]


def attention_pack(weights):
    return jnp.stack([weights[1].T, weights[2].T, weights[3].T, weights[4]])


def feedforward_pack(weights):
    return jnp.stack([weights[6].T, weights[7].T, weights[8]])


def fetch_mp(packs):
    rows = [pack.reshape(-1, pack.shape[-1]) for pack in packs]
    whole = rows[0] if len(rows) == 1 else jnp.concatenate(rows, axis=0)
    return lax.all_gather(whole, "mp", axis=0, tiled=False)


def fetch_dp(whole, first, pack):
    count, rows, width = pack.shape
    members = whole.shape[0]
    part = whole[:, first : first + count * rows].reshape(members, count, rows, width)
    part = part.transpose(1, 0, 2, 3).reshape(count, members * rows, width)
    return lax.all_gather(part, "dp", axis=2, tiled=True)


def turn_kernel(members, sizes, *refs):
    parts, out = refs[:-1], refs[-1]
    index, start, row = 0, 0, 0
    for size in sizes:
        if start == parts[index].shape[1]:
            index, start = index + 1, 0
        turned = parts[index][:, start : start + size].T
        count = size // members
        for member in range(members):
            out[member, row : row + count, :] = turned[member * count : (member + 1) * count, :]
        start += size
        row += count


def mp_blocks(plan, parts, sizes):
    rows = sum(sizes) // plan.m
    if parts[0].shape[0] == LANES:
        return pl.pallas_call(
            functools.partial(turn_kernel, plan.m, sizes),
            in_specs=[VMEM] * len(parts),
            out_specs=VMEM,
            out_shape=jax.ShapeDtypeStruct((plan.m, rows, LANES), jnp.bfloat16),
            compiler_params=pltpu.CompilerParams(vmem_limit_bytes=BIG_VMEM),
            cost_estimate=BRIEF,
            name="turn",
        )(*parts)
    turned, start, pieces = jnp.concatenate(parts, axis=1).T, 0, []
    for size in sizes:
        piece = turned[start : start + size]
        pieces.append(piece.reshape(plan.m, size // plan.m, turned.shape[1]))
        start += size
    return jnp.concatenate(pieces, axis=1)


def reduce_mp(plan, blocks, sizes):
    part = lax.psum_scatter(blocks, "mp", scatter_dimension=0, tiled=False).astype(jnp.float32)
    start, pieces = 0, []
    for size in sizes:
        pieces.append(part[start : start + size // plan.m])
        start += size // plan.m
    return pieces


def reduce_mp_beside(plan, blocks, sizes):
    me = lax.axis_index("mp")

    def block(distance):
        return lax.dynamic_index_in_dim(blocks, (me + distance) % plan.m, 0, keepdims=False)

    total = block(0).astype(jnp.float32)
    for distance in range(1, plan.m):
        route = [(i, (i + distance) % plan.m) for i in range(plan.m)]
        total = total + lax.ppermute(block(distance), "mp", route).astype(jnp.float32)
    start, pieces = 0, []
    for size in sizes:
        pieces.append(total[start : start + size // plan.m])
        start += size // plan.m
    return pieces


def reduce_qkv(plan, gradient, extra):
    gradient = jnp.concatenate([gradient, extra.astype(jnp.bfloat16)], axis=1)
    part = lax.psum_scatter(gradient, "dp", scatter_dimension=0, tiled=True)
    width = D // plan.m
    blocks = part[:, : 3 * D].reshape(-1, 3, plan.m, width).transpose(2, 0, 1, 3)
    blocks = blocks.reshape(plan.m, -1, 3 * width)
    shared = jnp.broadcast_to(part[None, :, 3 * D :], (plan.m, part.shape[0], LANES))
    blocks = jnp.concatenate([blocks, shared], axis=2)
    return lax.psum_scatter(blocks, "mp", scatter_dimension=0, tiled=False).astype(jnp.float32)


def project(normed, attention, first_values):
    query, key, fresh = (nt(normed, attention[part]) for part in range(3))
    if first_values is not None:
        fresh = 0.5 * fresh + 0.5 * first_values.astype(jnp.float32)
    return tuple(array.astype(jnp.bfloat16) for array in (query, key, fresh))


def feed_forward(middle, gain, feedforward):
    normed_ff = norm_rows(middle, gain).astype(jnp.bfloat16)
    gate = nt(normed_ff, feedforward[0])
    upward = nt(normed_ff, feedforward[1])
    hidden = (jax.nn.silu(gate) * upward).astype(jnp.bfloat16)
    return normed_ff, gate, upward, hidden


def feed_forward_back(grad_final, middle, gain, weights, stored):
    attention, feedforward = weights
    normed_ff, gate, upward, hidden = stored
    grad_bar = grad_final.astype(jnp.bfloat16)
    grad_hidden = nt(grad_bar, feedforward[2])
    gate_sigmoid = jax.nn.sigmoid(gate)
    grad_gate = (
        grad_hidden * upward * gate_sigmoid * (1.0 + gate * (1.0 - gate_sigmoid))
    ).astype(jnp.bfloat16)
    grad_up = (grad_hidden * gate * gate_sigmoid).astype(jnp.bfloat16)
    grad_normed_ff = nn(grad_gate, feedforward[0]) + nn(grad_up, feedforward[1])
    grad_norm, grad_gain = norm_back(middle, gain, grad_normed_ff)
    grad_middle = grad_final + grad_norm
    middle_bar = grad_middle.astype(jnp.bfloat16)
    grad_mixed = nt(middle_bar, attention[3]).astype(jnp.bfloat16)
    return grad_middle, grad_gain, grad_mixed, (grad_bar, grad_gate, grad_up, middle_bar)


def project_back(grad_middle, stream, gain, attention, dqkv):
    grad_normed = sum(nn(array, attention[part]) for part, array in enumerate(dqkv))
    grad_norm, grad_gain = norm_back(stream, gain, grad_normed)
    return grad_middle + grad_norm, grad_gain


def square_sum(values):
    widened = values.astype(jnp.float32)
    return jnp.sum(widened * widened)


def shards(n, m, inputs, lengths, *rest):
    plan = Plan(n, m)
    first, second, cotangent = rest[:9], rest[9:18], rest[18]
    cosine, sine = rotary_tables()
    tables = (chunks_before(plan, lengths), cosine, sine)
    by_hand = (n, m) == (8, 4)
    gain_shard = jnp.stack([first[0], first[5], second[0], second[5]])
    attention_packs = attention_pack(first), attention_pack(second)
    feedforward_packs = feedforward_pack(first), feedforward_pack(second)
    whole = fetch_mp(feedforward_packs[:1])
    if by_hand:
        gain_shard = jnp.pad(gain_shard, ((0, 12), (0, 0)))
        attention_one, gains = weave(plan, attention_packs[0], gain_shard)
        whole, cosine, sine = lax.optimization_barrier((whole, cosine, sine))
        whole = tied(whole, gains)
        tables = (tables[0], cosine, sine)
    else:
        gains = lax.all_gather(gain_shard, "dp", axis=1, tiled=True)
        attention_one = fetch_dp(fetch_mp(attention_packs[:1]), 0, attention_packs[0])
    feedforward_one = fetch_dp(whole, 0, feedforward_packs[0])
    gains = gains[:4].astype(jnp.float32)
    heads, hidden_rows = first[4].shape[0] * m, first[8].shape[0] * m
    rest_sizes = (hidden_rows, hidden_rows, hidden_rows, heads)

    stream = inputs.astype(jnp.float32)
    normed_one = norm_rows(stream, gains[0]).astype(jnp.bfloat16)
    qkv = project(normed_one, attention_one, None)
    values_one = qkv[2]
    q_seg, k_seg, v_seg = spread(plan, *qkv)
    packs_two = (attention_packs[1], feedforward_packs[1])
    feedforward_one, q_seg, packs_two = lax.optimization_barrier(
        (feedforward_one, q_seg, packs_two)
    )
    whole_two = fetch_mp(packs_two)
    out_seg, seen_one = attention(plan, tables, q_seg, k_seg, v_seg)
    out_seg, whole_two = lax.optimization_barrier((out_seg, whole_two))
    mixed_one = to_rows(plan, out_seg)
    attention_two = fetch_dp(whole_two, 0, packs_two[0])
    feedforward_two = fetch_dp(whole_two, 4 * packs_two[0].shape[1], packs_two[1])
    middle_one = stream + nn(mixed_one, attention_one[3])
    ff_one = feed_forward(middle_one, gains[1], feedforward_one)
    between = middle_one + nn(ff_one[3], feedforward_one[2])

    normed_two = norm_rows(between, gains[2]).astype(jnp.bfloat16)
    qkv = project(normed_two, attention_two, values_one)
    values_two = qkv[2]
    q_seg, k_seg, v_seg = spread(plan, *qkv)
    out_seg, seen_two = attention(plan, tables, q_seg, k_seg, v_seg)
    mixed_two = to_rows(plan, out_seg)
    middle_two = between + nn(mixed_two, attention_two[3])
    ff_two = feed_forward(middle_two, gains[3], feedforward_two)

    grad_middle, gain_ff_two, grad_mixed, (bar, grad_gate, grad_up, middle_bar) = feed_forward_back(
        cotangent.astype(jnp.float32), middle_two, gains[3], (attention_two, feedforward_two), ff_two
    )
    grad_seg, rest = products(
        plan,
        grad_mixed,
        (bar, ff_two[0], middle_bar),
        (ff_two[3], grad_gate, grad_up, mixed_two),
        (0, 1, 1, 2),
    )
    rest_two = lax.psum_scatter(rest, "dp", scatter_dimension=0, tiled=True)
    dqkv, unused, unused, final = attention_back(
        plan, tables, seen_two, grad_seg, (), (), (ff_two[3], feedforward_two, middle_two)
    )
    value_extra = 0.5 * dqkv[2].astype(jnp.float32)
    dqkv_two = (dqkv[0], dqkv[1], value_extra.astype(jnp.bfloat16))
    grad_between, gain_two = project_back(
        grad_middle, between, gains[2], attention_two, dqkv_two
    )

    qkv_two = tn(normed_two, jnp.concatenate(dqkv_two, axis=1)).astype(jnp.bfloat16)
    grad_between, qkv_two = lax.optimization_barrier((grad_between, qkv_two))
    qkv_two = lax.psum_scatter(qkv_two, "dp", scatter_dimension=0, tiled=True)
    grad_middle, gain_ff_one, grad_mixed, (bar, grad_gate, grad_up, middle_bar) = feed_forward_back(
        grad_between, middle_one, gains[1], (attention_one, feedforward_one), ff_one
    )
    grad_mixed, rest_two = lax.optimization_barrier((grad_mixed, rest_two))
    grad_seg, rest = products(
        plan,
        grad_mixed,
        (bar, ff_one[0], middle_bar),
        (ff_one[3], grad_gate, grad_up, mixed_one),
        (0, 1, 1, 2),
    )
    grad_seg, blocks, rest = lax.optimization_barrier(
        (grad_seg, mp_blocks(plan, (tied(rest_two, grad_seg),), rest_sizes), rest)
    )
    reduced_two = reduce_mp_beside(plan, blocks, rest_sizes)
    rest_one = lax.psum_scatter(rest, "dp", scatter_dimension=0, tiled=True)
    dqkv, qkv_two, reduced_two = attention_back(
        plan, tables, seen_one, grad_seg, qkv_two, reduced_two
    )
    grad_values = dqkv[2].astype(jnp.float32) + value_extra
    dqkv_one = (dqkv[0], dqkv[1], grad_values.astype(jnp.bfloat16))
    input_grad, gain_one = project_back(grad_middle, stream, gains[0], attention_one, dqkv_one)
    input_grad, rest_one = lax.optimization_barrier((input_grad, rest_one))
    sizes = rest_sizes + (heads,) * 3
    blocks, dqkv_one = lax.optimization_barrier(
        (mp_blocks(plan, (rest_one, qkv_two), sizes), dqkv_one)
    )
    down_one, gate_one, up_one, output_one, query_two, key_two, value_two = reduce_mp(
        plan, blocks, sizes
    )
    down_two, gate_two, up_two, output_two = reduced_two
    squares = [square_sum(values_one), square_sum(values_two)]
    width = D // n
    own_row = jnp.arange(D) == lax.axis_index("dp") * width
    squares = [jnp.where(own_row, square, 0.0) for square in squares]
    extra = jnp.stack([gain_one, gain_ff_one, gain_two, gain_ff_two, *squares], axis=1)
    extra = jnp.pad(extra, ((0, 0), (0, LANES - extra.shape[1])))
    if by_hand:
        part = shed(plan, normed_one, dqkv_one, extra)
    else:
        whole = [tn(normed_one, array).astype(jnp.bfloat16) for array in dqkv_one]
        part = reduce_qkv(plan, jnp.concatenate(whole, axis=1), extra)
    piece = D // m
    query_one, key_one, value_one = (part[:, i * piece : (i + 1) * piece] for i in range(3))
    shared = part[:, 3 * piece :]
    value_norms = jnp.sqrt(shared[:1, 4:6] / (TOK_DEV * D))
    return (
        between.astype(jnp.bfloat16),
        final,
        input_grad,
        shared[:, 0], query_one, key_one, value_one, output_one,
        shared[:, 1], gate_one.T, up_one.T, down_one,
        shared[:, 2], query_two.T, key_two.T, value_two.T, output_two,
        shared[:, 3], gate_two.T, up_two.T, down_two,
        value_norms,
    )


def solution(mesh):
    tokens, row_split, column_split = P(("dp", "mp"), None), P("dp", "mp"), P("mp", "dp")
    layer = (
        P("dp"), row_split, row_split, row_split, column_split, P("dp"), row_split, row_split,
        column_split,
    )
    return jax.shard_map(
        functools.partial(shards, mesh.shape["dp"], mesh.shape["mp"]),
        mesh=mesh,
        in_specs=(tokens, P(), *layer, *layer, tokens),
        out_specs=(tokens, tokens, tokens, *layer, *layer, P("dp", None)),
        check_vma=False,
    )
```

```python
import functools
import math

import jax
import jax.numpy as jnp
from jax import lax
from jax.experimental import pallas as pl
from jax.experimental.pallas import tpu as pltpu
from jax.sharding import PartitionSpec as P

D = 1024
HEAD_DIM = 64
TOK_DEV = 2048
LONGEST = 4096

LANES = 128
HEADS_HELD = LANES // HEAD_DIM
CHUNK = 1024
HALO = LONGEST - CHUNK
QUERY_ROWS = 1024
TILE = 256
EPSILON = 1e-06
MASKED = -1e30
LOG2E = math.log2(math.e)
MESH = pl.DeviceIdType.MESH
ANY = pl.BlockSpec(memory_space=pl.ANY)
VMEM = pl.BlockSpec(memory_space=pltpu.VMEM)
SMEM = pl.BlockSpec(memory_space=pltpu.SMEM)
BIG_VMEM = 56 * 1024 * 1024
BRIEF = pl.CostEstimate(flops=0, bytes_accessed=1_000, transcendentals=0)


def nn(left_side, right_side):
    return jnp.dot(left_side, right_side, preferred_element_type=jnp.float32)


def tn(left_side, right_side):
    return lax.dot_general(
        left_side, right_side, (((0,), (0,)), ((), ())), preferred_element_type=jnp.float32
    )


def nt(left_side, right_side):
    return lax.dot_general(
        left_side, right_side, (((1,), (1,)), ((), ())), preferred_element_type=jnp.float32
    )


def norm_rows(values, gain_vector):
    scaling = lax.rsqrt(jnp.mean(values * values, axis=-1, keepdims=True) + EPSILON)
    return values * scaling * gain_vector


def norm_back(values, gain_vector, grad_output):
    unused, pullback = jax.vjp(norm_rows, values, gain_vector)
    return pullback(grad_output)


class Plan:
    def __init__(self, n, m):
        self.n, self.m = n, m
        self.group = D // LANES
        self.low = self.group // m
        self.segments = n // self.low
        self.rows = TOK_DEV // m
        self.seg_rows = self.rows * self.group
        self.spans = []
        left, distance = HALO, 1
        while left > 0:
            count = min(self.seg_rows, left)
            self.spans.append((distance, left - count, count))
            left -= count
            distance += 1

    def here(self):
        dp, mp = lax.axis_index("dp"), lax.axis_index("mp")
        return dp // self.low, (dp % self.low) * self.m + mp

    def device(self, segment, member):
        return (segment * self.low + member // self.m, member % self.m)


def greet(plan, segment, member):
    barrier = pltpu.get_barrier_semaphore()
    for offset in range(1, plan.group):
        peer = lax.rem(member + offset, plan.group)
        pl.semaphore_signal(
            barrier, inc=1, device_id=plan.device(segment, peer), device_id_type=MESH
        )
    pl.semaphore_wait(barrier, plan.group - 1)


def member_copies(plan, segment, member, source, target, send, recv, own):
    copies = [pltpu.make_async_copy(source(member), target, own)]
    for offset in range(1, plan.group):
        peer = lax.rem(member + offset, plan.group)
        copies.append(
            pltpu.make_async_remote_copy(
                src_ref=source(peer),
                dst_ref=target,
                send_sem=send.at[offset],
                recv_sem=recv.at[offset],
                device_id=plan.device(segment, peer),
                device_id_type=MESH,
            )
        )
    for copy in copies[1:] + copies[:1]:
        copy.start()
    return copies


def columns(index):
    return pl.ds(pl.multiple_of(index * LANES, LANES), LANES)


def spread_kernel(plan, query, key, value, q_seg, k_seg, v_seg, send, recv, own):
    segment, member = plan.here()
    rows = plan.rows
    greet(plan, segment, member)
    copies = []
    place = pl.ds(pl.multiple_of(member * rows, rows), rows)
    for part, (array, out) in enumerate(((key, k_seg), (value, v_seg), (query, q_seg))):

        def source(peer, array=array):
            return array.at[:, columns(peer)]

        copies += member_copies(
            plan, segment, member, source, out.at[place], send.at[part], recv.at[part], own.at[part]
        )
    for copy in copies:
        copy.wait()


def spread(plan, query, key, value):
    segment = jax.ShapeDtypeStruct((plan.seg_rows, LANES), jnp.bfloat16)
    return pl.pallas_call(
        functools.partial(spread_kernel, plan),
        out_shape=(segment,) * 3,
        in_specs=[ANY] * 3,
        out_specs=(ANY, ANY, ANY),
        scratch_shapes=[
            pltpu.SemaphoreType.DMA((3, plan.group)),
            pltpu.SemaphoreType.DMA((3, plan.group)),
            pltpu.SemaphoreType.DMA((3,)),
        ],
        compiler_params=pltpu.CompilerParams(collective_id=1, has_side_effects=True),
        cost_estimate=BRIEF,
        name="spread",
    )(query, key, value)


def halo_of(plan, seg):
    parts = []
    for distance, first, count in reversed(plan.spans):
        route = [(i, i + distance * plan.low) for i in range(plan.n - distance * plan.low)]
        parts.append(lax.ppermute(seg[plan.seg_rows - count :], "dp", route))
    return parts[0] if len(parts) == 1 else jnp.concatenate(parts, axis=0)


def halo_back(plan, halo):
    parts = []
    for distance, first, count in plan.spans:
        route = [(i, i - distance * plan.low) for i in range(distance * plan.low, plan.n)]
        parts.append(lax.ppermute(halo[:, first : first + count], "dp", route))
    return parts


def to_rows_kernel(plan, seg, rows_out, send, recv, own):
    segment, member = plan.here()
    rows = plan.rows
    greet(plan, segment, member)

    def source(peer):
        return seg.at[pl.ds(pl.multiple_of(peer * rows, rows), rows)]

    for copy in member_copies(
        plan, segment, member, source, rows_out.at[:, columns(member)], send, recv, own
    ):
        copy.wait()


def to_rows(plan, seg):
    return pl.pallas_call(
        functools.partial(to_rows_kernel, plan),
        out_shape=jax.ShapeDtypeStruct((plan.rows, D), jnp.bfloat16),
        in_specs=[ANY],
        out_specs=ANY,
        scratch_shapes=[
            pltpu.SemaphoreType.DMA((plan.group,)),
            pltpu.SemaphoreType.DMA((plan.group,)),
            pltpu.SemaphoreType.DMA,
        ],
        compiler_params=pltpu.CompilerParams(collective_id=2, has_side_effects=True),
        cost_estimate=BRIEF,
        name="to_rows",
    )(seg)


def dp_place():
    dp = lax.axis_index("dp")
    return dp, dp % 2, (dp // 2) % 2, dp // 4


def greet_all(plan, dp, mp):
    barrier = pltpu.get_barrier_semaphore()
    others = [(dp, lax.rem(mp + k, plan.m)) for k in range(1, plan.m)]
    others += [(lax.rem(dp + k, plan.n), mp) for k in range(1, plan.n)]
    for other in others:
        pl.semaphore_signal(barrier, inc=1, device_id=other, device_id_type=MESH)
    pl.semaphore_wait(barrier, len(others))


def remote(source, target, send, recv, device):
    copy = pltpu.make_async_remote_copy(
        src_ref=source,
        dst_ref=target,
        send_sem=send,
        recv_sem=recv,
        device_id=device,
        device_id_type=MESH,
    )
    copy.start()
    return copy


def weave_kernel(plan, shard, gain, out, gain_out, own, *sems):
    z_send, z_recv, x_send, x_recv, y_send, y_recv, c_send, c_recv, g_send, g_recv = sems
    (dp, core, x, y), mp = dp_place(), lax.axis_index("mp")
    types, rows = shard.shape[:2]
    half = types // 2
    greet_all(plan, dp, mp)
    beside = dp + 1 - 2 * core
    dp_x, dp_y = dp + 2 - 4 * x, dp + 4 - 8 * y
    dp_xy = dp_x + 4 - 8 * y

    def block(index, column, first=0, count=types):
        z = lax.rem(mp + plan.m - index, plan.m)
        place = pl.ds(pl.multiple_of(z * rows, rows), rows)
        return out.at[pl.ds(first, count), place, columns(column)]

    def pass_on(index, column, sems, slot, device, first=0, count=types):
        region = block(index, column, first, count)
        return remote(
            region, region, sems[0].at[index, slot], sems[1].at[index, slot], (device, mp)
        )

    locals_ = [
        pltpu.make_async_copy(shard, block(0, dp), own.at[0]),
        pltpu.make_async_copy(gain, gain_out.at[:, columns(dp)], own.at[1]),
    ]
    for copy in locals_:
        copy.start()
    z_copies = [None]
    for k in range(1, plan.m):
        z_copies.append(
            remote(shard, block(0, dp), z_send.at[k], z_recv.at[k], (dp, lax.rem(mp + k, plan.m)))
        )
    copies = [
        remote(
            gain,
            gain_out.at[:, columns(dp)],
            g_send.at[k],
            g_recv.at[k],
            (lax.rem(dp + k, plan.n), mp),
        )
        for k in range(1, plan.n)
    ]
    x_sems, y_sems, c_sems = (x_send, x_recv), (y_send, y_recv), (c_send, c_recv)
    x_own, y_own, x_far, y_far, c_all = [], [], [], [], []

    def first_stage(index):
        if index == 0:
            for copy in locals_:
                copy.wait()
        else:
            z_copies[index].wait_recv()
        x_own.append(pass_on(index, dp, x_sems, 0, dp_x))
        y_own.append(pass_on(index, dp, y_sems, 0, dp_y))
        c_all.append(pass_on(index, dp, c_sems, 0, beside))

    def second_stage(index):
        x_own[index].wait_recv()
        y_far.append(pass_on(index, dp_x, y_sems, 1, dp_y, 0, half))
        c_all.append(pass_on(index, dp_x, c_sems, 1, beside))
        y_own[index].wait_recv()
        x_far.append(pass_on(index, dp_y, x_sems, 1, dp_x, half, types - half))
        c_all.append(pass_on(index, dp_y, c_sems, 2, beside))

    def third_stage(index):
        y_far[index].wait_recv()
        c_all.append(pass_on(index, dp_xy, c_sems, 3, beside, 0, half))
        x_far[index].wait_recv()
        c_all.append(pass_on(index, dp_xy, c_sems, 4, beside, half, types - half))

    for step in range(plan.m + 2):
        if step < plan.m:
            first_stage(step)
        if 1 <= step < plan.m + 1:
            second_stage(step - 1)
        if step >= 2:
            third_stage(step - 2)
    for copy in copies + c_all:
        copy.wait()
    for copy in z_copies[1:] + x_own + y_own + x_far + y_far:
        copy.wait_send()


def weave(plan, shard, gain):
    types, rows = shard.shape[:2]
    dma = pltpu.SemaphoreType.DMA
    return pl.pallas_call(
        functools.partial(weave_kernel, plan),
        in_specs=[ANY, ANY],
        out_specs=(ANY, ANY),
        out_shape=(
            jax.ShapeDtypeStruct((types, plan.m * rows, D), jnp.bfloat16),
            jax.ShapeDtypeStruct((gain.shape[0], D), jnp.bfloat16),
        ),
        scratch_shapes=[dma((2,))]
        + [dma((plan.m,))] * 2
        + [dma((plan.m, 2))] * 4
        + [dma((plan.m, 5))] * 2
        + [dma((plan.n,))] * 2,
        compiler_params=pltpu.CompilerParams(collective_id=6, has_side_effects=True),
        cost_estimate=BRIEF,
        name="weave",
    )(shard, gain)


def shed_kernel(plan, normed, dq, dk, dv, extra, out, left, parts, from_core, sums, *rest):
    from_first, sums_first, from_second, blocks, from_z, c_sems, f_sems, s_sems, z_sems = rest
    (dp, core, x, y), mp = dp_place(), lax.axis_index("mp")
    width = D // plan.n
    wide = D // 2
    greet_all(plan, dp, mp)
    beside, dp_x, dp_y = dp + 1 - 2 * core, dp + 2 - 4 * x, dp + 4 - 8 * y

    def rows_of(index):
        return pl.ds(pl.multiple_of(index * width, width), width)

    def plus(one, other):
        return (one.astype(jnp.float32) + other.astype(jnp.float32)).astype(jnp.bfloat16)

    left[...] = normed[...].T
    c_copies, first, second = [], [], []
    for half in range(2):
        for kind, array in enumerate((dq, dk, dv)):
            place = slice(kind * wide, (kind + 1) * wide)
            source = slice(half * wide, (half + 1) * wide)
            parts[half, :, place] = nn(left[...], array[:, source]).astype(jnp.bfloat16)
        parts[half, :, 3 * wide :] = extra[...].astype(jnp.bfloat16)
        c_copies.append(
            [
                remote(
                    parts.at[half, rows_of(2 * j + 1 - core)],
                    from_core.at[half, j],
                    c_sems.at[0, half, j],
                    c_sems.at[1, half, j],
                    (beside, mp),
                )
                for j in range(4)
            ]
        )
    for half in range(2):
        for j in range(4):
            c_copies[half][j].wait_recv()
            sums[half, j] = plus(parts[half, rows_of(2 * j + core), :], from_core[half, j])
        for k in range(2):
            away = 2 * k + 1 - x if half == 0 else 2 * (1 - y) + k
            first.append(
                remote(
                    sums.at[half, away],
                    from_first.at[half, k],
                    f_sems.at[0, half, k],
                    f_sems.at[1, half, k],
                    (dp_x if half == 0 else dp_y, mp),
                )
            )
    for half in range(2):
        for k in range(2):
            first[2 * half + k].wait_recv()
            kept = 2 * k + x if half == 0 else 2 * y + k
            sums_first[half, k] = plus(sums[half, kept], from_first[half, k])
        second.append(
            remote(
                sums_first.at[half, 1 - y if half == 0 else 1 - x],
                from_second.at[half],
                s_sems.at[0, half],
                s_sems.at[1, half],
                (dp_y if half == 0 else dp_x, mp),
            )
        )
    piece = D // plan.m
    for half in range(2):
        second[half].wait_recv()
        total = plus(sums_first[half, y if half == 0 else x], from_second[half])
        for member in range(2):
            index = 2 * half + member
            for kind in range(3):
                start = kind * wide + member * piece
                blocks[index, :, kind * piece : (kind + 1) * piece] = total[:, start : start + piece]
            blocks[index, :, 3 * piece :] = total[:, 3 * wide :]
    z_copies = []
    for k in range(1, plan.m):
        peer = lax.rem(mp + k, plan.m)
        z_copies.append(
            remote(
                blocks.at[peer], from_z.at[k], z_sems.at[0, k], z_sems.at[1, k], (dp, peer)
            )
        )
    result = blocks[mp].astype(jnp.float32)
    for k in range(1, plan.m):
        z_copies[k - 1].wait_recv()
        result = result + from_z[k].astype(jnp.float32)
    out[...] = result
    for copy in c_copies[0] + c_copies[1] + first + second + z_copies:
        copy.wait_send()


def shed(plan, normed, dqkv, extra):
    dma = pltpu.SemaphoreType.DMA
    width, wide, kept = D // plan.n, 3 * (D // 2) + LANES, 3 * (D // plan.m) + LANES

    def held(*shape):
        return pltpu.VMEM(shape, jnp.bfloat16)

    return pl.pallas_call(
        functools.partial(shed_kernel, plan),
        in_specs=[VMEM] * 5,
        out_specs=VMEM,
        out_shape=jax.ShapeDtypeStruct((width, kept), jnp.float32),
        scratch_shapes=[
            held(D, normed.shape[0]),
            held(2, D, wide),
            held(2, 4, width, wide),
            held(2, 4, width, wide),
            held(2, 2, width, wide),
            held(2, 2, width, wide),
            held(2, width, wide),
            held(plan.m, width, kept),
            held(plan.m, width, kept),
            dma((2, 2, 4)),
            dma((2, 2, 2)),
            dma((2, 2)),
            dma((2, plan.m)),
        ],
        compiler_params=pltpu.CompilerParams(
            collective_id=7, has_side_effects=True, vmem_limit_bytes=BIG_VMEM
        ),
        cost_estimate=BRIEF,
        name="shed",
    )(normed, *dqkv, extra)


def products_kernel(plan, sides, *refs):
    rows_in, refs = refs[0], refs[1:]
    lefts, rights = refs[: len(set(sides))], refs[len(set(sides)) : len(set(sides)) + len(sides)]
    seg, out, left_sides, tiles, send, recv, own, sent = refs[len(lefts) + len(rights) :]
    segment, member = plan.here()
    rows = plan.rows
    greet(plan, segment, member)

    def source(peer):
        return rows_in.at[:, columns(peer)]

    place = seg.at[pl.ds(pl.multiple_of(member * rows, rows), rows)]
    copies = member_copies(plan, segment, member, source, place, send, recv, own)
    for index, array in enumerate(lefts):
        left_sides[index] = array[...].T
    start, pending = 0, [None, None]
    slot = 0
    for array, side in zip(rights, sides):
        size = array.shape[1]
        width = size // 2 if size % (2 * LANES) == 0 and size > D else D
        for first in range(0, size, width):
            if pending[slot] is not None:
                pending[slot].wait()
            tiles[slot, :, :width] = nn(
                left_sides[side], array[:, first : first + width]
            ).astype(jnp.bfloat16)
            pending[slot] = pltpu.make_async_copy(
                tiles.at[slot, :, :width], out.at[:, pl.ds(start, width)], sent.at[slot]
            )
            pending[slot].start()
            start += width
            slot = 1 - slot
    for copy in pending + copies:
        copy.wait()


def products(plan, rows_in, lefts, rights, sides):
    rows, widest = lefts[0].shape[0], max(array.shape[1] for array in rights) // 2
    total = sum(array.shape[1] for array in rights)
    return pl.pallas_call(
        functools.partial(products_kernel, plan, sides),
        in_specs=[ANY] + [VMEM] * (len(lefts) + len(rights)),
        out_specs=(ANY, ANY),
        out_shape=(
            jax.ShapeDtypeStruct((plan.seg_rows, LANES), jnp.bfloat16),
            jax.ShapeDtypeStruct((D, total), jnp.bfloat16),
        ),
        scratch_shapes=[
            pltpu.VMEM((len(lefts), D, rows), jnp.bfloat16),
            pltpu.VMEM((2, D, widest), jnp.bfloat16),
            pltpu.SemaphoreType.DMA((plan.group,)),
            pltpu.SemaphoreType.DMA((plan.group,)),
            pltpu.SemaphoreType.DMA,
            pltpu.SemaphoreType.DMA((2,)),
        ],
        compiler_params=pltpu.CompilerParams(
            collective_id=len(lefts), has_side_effects=True, vmem_limit_bytes=BIG_VMEM
        ),
        cost_estimate=BRIEF,
        name="products",
    )(rows_in, *lefts, *rights)


def collect_kernel(plan, spans, more, *refs):
    parts = 1 if spans == 0 else 2
    arrays, halos, refs = refs[:parts], refs[parts : parts + spans], refs[parts + spans :]
    beside, refs = refs[:more], refs[more:]
    outs, refs = refs[:parts], refs[parts:]
    total, send, recv, own = refs[-4:]
    segment, member = plan.here()
    rows = plan.rows
    greet(plan, segment, member)
    copies = []
    for part, array in enumerate(arrays):
        if spans:
            for piece in range(plan.seg_rows // CHUNK):
                start = piece * CHUNK
                value = array[pl.ds(start, CHUNK), :]
                for index, (distance, first, count) in enumerate(plan.spans):
                    offset = start - (plan.seg_rows - count)
                    if offset >= 0:
                        halo = halos[index][part, pl.ds(offset, CHUNK), :]
                        value = value + halo.astype(jnp.float32)
                total[part, pl.ds(start, CHUNK), :] = value.astype(jnp.bfloat16)
            array = total.at[part]

        def source(peer, array=array):
            return array.at[pl.ds(pl.multiple_of(peer * rows, rows), rows)]

        copies += member_copies(
            plan,
            segment,
            member,
            source,
            outs[part].at[:, columns(member)],
            send.at[part],
            recv.at[part],
            own.at[part],
        )
    if beside:
        (hidden, weights, middle), (final, down, loaded) = beside, refs[:3]
        load = pltpu.make_async_copy(weights.at[2], down, loaded)
        load.start()
        load.wait()
        for first in range(0, D, TILE):
            place = slice(first, first + TILE)
            final[:, place] = (middle[:, place] + nn(hidden[...], down[:, place])).astype(
                jnp.bfloat16
            )
    for copy in copies:
        copy.wait()


def collect(plan, arrays, halos, beside=()):
    parts, spans = len(arrays), len(plan.spans) if halos else 0
    return pl.pallas_call(
        functools.partial(collect_kernel, plan, spans, len(beside)),
        out_shape=(jax.ShapeDtypeStruct((plan.rows, D), jnp.bfloat16),) * (parts + bool(beside)),
        in_specs=[VMEM] * (parts + len(halos)) + [VMEM, ANY, VMEM][: len(beside)],
        out_specs=(ANY,) * parts + (VMEM,) * bool(beside),
        scratch_shapes=[pltpu.VMEM(one.shape[1:], one.dtype) for one in beside[1:2]]
        + [pltpu.SemaphoreType.DMA] * bool(beside)
        + [
            pltpu.VMEM((parts, plan.seg_rows if halos else 16, LANES), jnp.bfloat16),
            pltpu.SemaphoreType.DMA((parts, plan.group)),
            pltpu.SemaphoreType.DMA((parts, plan.group)),
            pltpu.SemaphoreType.DMA((parts,)),
        ],
        compiler_params=pltpu.CompilerParams(
            collective_id=5 if halos else 9 if beside else 8, has_side_effects=True, vmem_limit_bytes=BIG_VMEM
        ),
        cost_estimate=BRIEF,
        name="collect_kv" if halos else "collect_q",
    )(*arrays, *halos, *beside)


def swap_halves(values):
    lane = lax.broadcasted_iota(jnp.int32, values.shape, 1)
    half = HEAD_DIM // 2
    ahead = pltpu.roll(values, LANES - half, 1)
    behind = pltpu.roll(values, half, 1)
    return jnp.where(lax.rem(lane, HEAD_DIM) < half, ahead, behind)


def rotate(values, cosine, sine):
    return values * cosine + swap_halves(values) * sine


def of_head(values, head):
    lane = lax.broadcasted_iota(jnp.int32, values.shape, 1)
    return jnp.where(lane // HEAD_DIM == head, values, jnp.zeros_like(values))


def chunk_rows(index, size):
    return pl.ds(pl.multiple_of(index * size, size), size)


HALO_CHUNKS = HALO // CHUNK


def rotate_keys(prior, first, keys, cosine, sine, k_turned):
    def one(index, unused):
        table = chunk_rows(prior[first + index], CHUNK)
        rows = chunk_rows(index, CHUNK)
        k_turned[rows, :] = rotate(
            keys[rows, :].astype(jnp.float32), cosine[table, :], sine[table, :]
        ).astype(jnp.bfloat16)
        return unused

    lax.fori_loop(0, keys.shape[0] // CHUNK, one, 0)


def query_tables(prior, block, cosine, sine):
    rows = chunk_rows(prior[HALO_CHUNKS + block], QUERY_ROWS)
    return cosine[rows, :], sine[rows, :]


def turned_queries(prior, block, queries, cosine, sine):
    cos_rows, sin_rows = query_tables(prior, block, cosine, sine)
    turned = rotate(queries.astype(jnp.float32), cos_rows, sin_rows)
    return (turned * (LOG2E * HEAD_DIM ** (-0.5))).astype(jnp.bfloat16)


def by_head(parts):
    whole = parts[0]
    lane = lax.broadcasted_iota(jnp.int32, whole.shape, 1)
    for head in range(1, HEADS_HELD):
        whole = jnp.where(lane // HEAD_DIM == head, parts[head], whole)
    return whole


def needs_halo(prior, own_chunks):
    needed = prior[HALO_CHUNKS] > 0
    for chunk in range(1, min(own_chunks, HALO_CHUNKS)):
        needed = needed | (prior[HALO_CHUNKS + chunk] > chunk)
    return needed


ROW_PARTS = 4


def units_of(diagonal):
    parts = ROW_PARTS if diagonal else ROW_PARTS // 2
    units = [(head, part) for part in range(parts) for head in range(HEADS_HELD)]
    return units, QUERY_ROWS // parts


def add_keys(refs, first, diagonal):
    q_head, k_turned, v_wide, top, total = refs
    start_row = pl.multiple_of(first * CHUNK, CHUNK)
    units, part_rows = units_of(diagonal)

    def queries(part):
        return slice(part * part_rows, (part + 1) * part_rows)

    def keys(part):
        return pl.ds(start_row, (part + 1) * part_rows if diagonal else CHUNK)

    def start(unit):
        head, part = unit
        return nt(q_head[head, queries(part), :], k_turned[keys(part), :])

    def finish(unit, scores):
        head, part = unit
        held = (head, queries(part))
        value_block = v_wide[keys(part), :]
        if diagonal:
            place = lax.broadcasted_iota(jnp.int32, scores.shape, 0) + part * part_rows
            other = lax.broadcasted_iota(jnp.int32, scores.shape, 1)
            scores = jnp.where(other <= place, scores, MASKED)
        highest = jnp.max(scores, axis=1, keepdims=True)
        if diagonal:
            weights = jnp.exp2((scores - highest).astype(jnp.bfloat16))
            total[held] = nn(weights, value_block)
            top[held] = jnp.broadcast_to(highest, (part_rows, LANES))
        else:
            before = top[held]
            after = jnp.maximum(before, highest)
            weights = jnp.exp2((scores - after[:, :1]).astype(jnp.bfloat16))
            shrink = jnp.exp2(before - after)
            shrink = jnp.concatenate([shrink, shrink], axis=1)
            total[held] = total[held] * shrink + nn(weights, value_block)
            top[held] = after

    scores = start(units[0])
    for index, unit in enumerate(units):
        following = start(units[index + 1]) if index + 1 < len(units) else None
        finish(unit, scores)
        scores = following


def mixed_of(total):
    return by_head([total[head, :, :LANES] / total[head, :, LANES:] for head in range(HEADS_HELD)])


def attend_own_kernel(
    prior, q_ref, keys, values, cosine, sine, out_ref, top_ref, sum_ref, *scratch
):
    k_turned, v_wide, q_head, top, total = scratch
    block = pl.program_id(0)

    @pl.when(block == 0)
    def _():
        rotate_keys(prior, HALO_CHUNKS, keys, cosine, sine, k_turned)
        v_wide[:, :LANES] = values[...]
        v_wide[:, LANES:] = jnp.ones((values.shape[0], LANES), jnp.bfloat16)

    turned = turned_queries(prior, block, q_ref[...], cosine, sine)
    for head in range(HEADS_HELD):
        q_head[head] = of_head(turned, head)
    held = (q_head, k_turned, v_wide, top, total)
    add_keys(held, block, True)

    def earlier_chunk(index, unused):
        add_keys(held, block - 1 - index, False)
        return unused

    lax.fori_loop(0, jnp.minimum(prior[HALO_CHUNKS + block], block), earlier_chunk, 0)
    out_ref[...] = mixed_of(total).astype(jnp.bfloat16)
    top_ref[...] = by_head([top[head] for head in range(HEADS_HELD)])
    sum_ref[...] = by_head([total[head, :, LANES:] for head in range(HEADS_HELD)])


def attend_own(prior, q_seg, keys, values, cosine, sine):
    seg_rows = q_seg.shape[0]
    query_spec = pl.BlockSpec((QUERY_ROWS, LANES), lambda i, prior: (i, 0))
    wide = jax.ShapeDtypeStruct((seg_rows, LANES), jnp.float32)
    return pl.pallas_call(
        attend_own_kernel,
        grid_spec=pltpu.PrefetchScalarGridSpec(
            num_scalar_prefetch=1,
            grid=(seg_rows // QUERY_ROWS,),
            in_specs=[query_spec, VMEM, VMEM, VMEM, VMEM],
            out_specs=(query_spec,) * 3,
            scratch_shapes=[
                pltpu.VMEM((seg_rows, LANES), jnp.bfloat16),
                pltpu.VMEM((seg_rows, 2 * LANES), jnp.bfloat16),
                pltpu.VMEM((HEADS_HELD, QUERY_ROWS, LANES), jnp.bfloat16),
                pltpu.VMEM((HEADS_HELD, QUERY_ROWS, LANES), jnp.float32),
                pltpu.VMEM((HEADS_HELD, QUERY_ROWS, 2 * LANES), jnp.float32),
            ],
        ),
        out_shape=(jax.ShapeDtypeStruct((seg_rows, LANES), jnp.bfloat16), wide, wide),
        compiler_params=pltpu.CompilerParams(vmem_limit_bytes=BIG_VMEM),
        cost_estimate=BRIEF,
        name="attend_own",
    )(prior, q_seg, keys, values, cosine, sine)


def copy_in(pairs, sems):
    copies = [
        pltpu.make_async_copy(source, target, sems.at[index])
        for index, (source, target) in enumerate(pairs)
    ]
    for copy in copies:
        copy.start()
    for copy in copies:
        copy.wait()


def attend_halo_kernel(
    own_chunks, prior, q_seg, keys, values, cos_hbm, sin_hbm, out_in, top_in, sum_in,
    out, top_out, sum_out, *scratch
):
    k_turned, v_wide, q_head, top, total, key_rows, value_rows, cosine, sine = scratch[:9]
    q_rows, out_rows, top_rows, sum_rows, sems = scratch[9:]

    def one_block(block, unused):
        count = prior[HALO_CHUNKS + block] - block
        rows = chunk_rows(block, QUERY_ROWS)

        @pl.when(count > 0)
        def _():
            turned = turned_queries(prior, block, q_rows[rows, :], cosine, sine)
            mixed, tops, sums = out_rows[rows, :], top_rows[rows, :], sum_rows[rows, :]
            for head in range(HEADS_HELD):
                lane = head * HEAD_DIM
                q_head[head] = of_head(turned, head)
                top[head] = jnp.broadcast_to(tops[:, lane : lane + 1], top.shape[1:])
                weight = jnp.broadcast_to(sums[:, lane : lane + 1], top.shape[1:])
                total[head, :, :LANES] = mixed.astype(jnp.float32) * weight
                total[head, :, LANES:] = weight

            def earlier_chunk(index, unused):
                held = (q_head, k_turned, v_wide, top, total)
                add_keys(held, HALO_CHUNKS - 1 - index, False)
                return unused

            lax.fori_loop(0, count, earlier_chunk, 0)
            out_rows[rows, :] = mixed_of(total).astype(jnp.bfloat16)
            top_rows[rows, :] = by_head([top[head] for head in range(HEADS_HELD)])
            sum_rows[rows, :] = by_head([total[head, :, LANES:] for head in range(HEADS_HELD)])

        return unused

    @pl.when(needs_halo(prior, own_chunks))
    def _():
        part = pl.ds(0, q_rows.shape[0])
        held = ((out, out_rows), (top_out, top_rows), (sum_out, sum_rows))
        copy_in(
            (
                (keys, key_rows), (values, value_rows), (cos_hbm, cosine), (sin_hbm, sine),
                (q_seg.at[part], q_rows), *((hbm.at[part], rows) for hbm, rows in held),
            ),
            sems,
        )
        rotate_keys(prior, 0, key_rows, cosine, sine, k_turned)
        v_wide[:, :LANES] = value_rows[...]
        v_wide[:, LANES:] = jnp.ones((value_rows.shape[0], LANES), jnp.bfloat16)
        lax.fori_loop(0, q_rows.shape[0] // QUERY_ROWS, one_block, 0)
        copy_in([(rows, hbm.at[part]) for hbm, rows in held], sems)


def attend_halo(prior, q_seg, keys, values, cosine, sine, earlier):
    part = (min(q_seg.shape[0], HALO), LANES)
    per_head = (HEADS_HELD, QUERY_ROWS, LANES)
    return pl.pallas_call(
        functools.partial(attend_halo_kernel, q_seg.shape[0] // CHUNK),
        in_specs=[SMEM] + [ANY] * 8,
        out_specs=(ANY,) * 3,
        out_shape=tuple(jax.ShapeDtypeStruct(one.shape, one.dtype) for one in earlier),
        scratch_shapes=[
            pltpu.VMEM((HALO, LANES), jnp.bfloat16),
            pltpu.VMEM((HALO, 2 * LANES), jnp.bfloat16),
            pltpu.VMEM(per_head, jnp.bfloat16),
            pltpu.VMEM(per_head, jnp.float32),
            pltpu.VMEM((HEADS_HELD, QUERY_ROWS, 2 * LANES), jnp.float32),
            pltpu.VMEM((HALO, LANES), jnp.bfloat16),
            pltpu.VMEM((HALO, LANES), jnp.bfloat16),
            pltpu.VMEM((LONGEST, LANES), jnp.float32),
            pltpu.VMEM((LONGEST, LANES), jnp.float32),
            pltpu.VMEM(part, jnp.bfloat16),
            pltpu.VMEM(part, jnp.bfloat16),
            pltpu.VMEM(part, jnp.float32),
            pltpu.VMEM(part, jnp.float32),
            pltpu.SemaphoreType.DMA((8,)),
        ],
        input_output_aliases={6: 0, 7: 1, 8: 2},
        compiler_params=pltpu.CompilerParams(vmem_limit_bytes=BIG_VMEM),
        cost_estimate=BRIEF,
        name="attend_halo",
    )(prior, q_seg, keys, values, cosine, sine, *earlier)


def prepare_back(refs, block, prior, queries, grads, mixed, tops, sums, cosine, sine):
    q_head, grad_head, row_stats = refs
    turned = turned_queries(prior, block, queries, cosine, sine)
    grads = grads.astype(jnp.float32) / sums
    dots = (grads * mixed.astype(jnp.float32)).T
    tops = tops.T
    grads = grads.astype(jnp.bfloat16)
    for head in range(HEADS_HELD):
        q_head[head] = of_head(turned, head)
        grad_head[head] = of_head(grads, head)
        lanes = slice(head * HEAD_DIM, (head + 1) * HEAD_DIM)
        row_stats[head, 0:1, :] = tops[head * HEAD_DIM : head * HEAD_DIM + 1, :]
        row_stats[head, 1:2, :] = jnp.sum(dots[lanes, :], axis=0, keepdims=True)


def add_keys_back(refs, first, diagonal):
    q_head, grad_head, row_stats, k_turned, values, dq_total, dk_total, dv_total = refs
    units, part_rows = units_of(diagonal)

    def keys(part):
        start = pl.multiple_of(first * CHUNK + part * part_rows, part_rows)
        return pl.ds(start, part_rows)

    def queries(part):
        return slice(part * part_rows if diagonal else 0, QUERY_ROWS)

    def start(unit):
        head, part = unit
        rows, wanted = keys(part), queries(part)
        return (
            nt(k_turned[rows, :], q_head[head, wanted, :]),
            nt(values[rows, :], grad_head[head, wanted, :]),
        )

    def finish(unit, products_):
        head, part = unit
        rows, wanted = keys(part), queries(part)
        scores, grad_weights = products_
        weights = jnp.exp2((scores - row_stats[head, 0:1, wanted]).astype(jnp.bfloat16))
        if diagonal:
            other = lax.broadcasted_iota(jnp.int32, scores.shape, 0)
            place = lax.broadcasted_iota(jnp.int32, scores.shape, 1)
            weights = jnp.where(other <= place, weights, jnp.zeros_like(weights))
        grad_scores = weights * (grad_weights - row_stats[head, 1:2, wanted]).astype(jnp.bfloat16)
        dv_total[rows, :] += nn(weights, grad_head[head, wanted, :])
        dk_total[rows, :] += nn(grad_scores, q_head[head, wanted, :])
        dq_total[head, wanted, :] += tn(grad_scores, k_turned[rows, :])

    held = start(units[0])
    for index, unit in enumerate(units):
        following = start(units[index + 1]) if index + 1 < len(units) else None
        finish(unit, held)
        held = following


def turn_keys_back(prior, first_chunk, dk_total, dv_total, cosine, sine, dk_ref, dv_ref):
    def one(index, unused):
        table = chunk_rows(prior[first_chunk + index], CHUNK)
        rows = chunk_rows(index, CHUNK)
        turned = rotate(dk_total[rows, :], cosine[table, :], -sine[table, :]) * (1.0 / LOG2E)
        dk_ref[rows, :] = turned.astype(dk_ref.dtype)
        dv_ref[rows, :] = dv_total[rows, :].astype(dv_ref.dtype)
        return unused

    lax.fori_loop(0, dk_ref.shape[0] // CHUNK, one, 0)


def attend_back_own_kernel(
    prior, q_ref, grad_ref, out_ref, top_ref, sum_ref, keys, values, cosine, sine, dq_part,
    dq_ref, dk_ref, dv_ref, k_turned, q_head, grad_head, dq_total, dk_total, dv_total, row_stats
):
    block = pl.program_id(0)
    chunks_back = prior[HALO_CHUNKS + block]

    @pl.when(block == 0)
    def _():
        rotate_keys(prior, HALO_CHUNKS, keys, cosine, sine, k_turned)
        dk_total[...] = jnp.zeros_like(dk_total)
        dv_total[...] = jnp.zeros_like(dv_total)

    prepare_back(
        (q_head, grad_head, row_stats), block, prior, q_ref[...], grad_ref[...], out_ref[...],
        top_ref[...], sum_ref[...], cosine, sine,
    )
    from_halo = jnp.where(chunks_back > block, dq_part[...], jnp.zeros_like(dq_part))
    for head in range(HEADS_HELD):
        dq_total[head] = from_halo
    held = (q_head, grad_head, row_stats, k_turned, values, dq_total, dk_total, dv_total)
    add_keys_back(held, block, True)

    def whole(index, unused):
        add_keys_back(held, index, False)
        return unused

    lax.fori_loop(jnp.maximum(block - chunks_back, 0), block, whole, 0)
    cos_rows, sin_rows = query_tables(prior, block, cosine, sine)
    turned = rotate(by_head([dq_total[head] for head in range(HEADS_HELD)]), cos_rows, -sin_rows)
    dq_ref[...] = (turned * HEAD_DIM ** (-0.5)).astype(jnp.bfloat16)

    @pl.when(block == pl.num_programs(0) - 1)
    def _():
        turn_keys_back(prior, HALO_CHUNKS, dk_total, dv_total, cosine, sine, dk_ref, dv_ref)


def back_scratch(key_rows):
    per_head = (HEADS_HELD, QUERY_ROWS, LANES)
    return [
        pltpu.VMEM((key_rows, LANES), jnp.bfloat16),
        pltpu.VMEM(per_head, jnp.bfloat16),
        pltpu.VMEM(per_head, jnp.bfloat16),
        pltpu.VMEM(per_head, jnp.float32),
        pltpu.VMEM((key_rows, LANES), jnp.float32),
        pltpu.VMEM((key_rows, LANES), jnp.float32),
        pltpu.VMEM((HEADS_HELD, 8, QUERY_ROWS), jnp.float32),
    ]


def attend_back_own(prior, q_seg, grad_seg, seen, keys, values, cosine, sine, dq_part):
    seg_rows = q_seg.shape[0]
    query_spec = pl.BlockSpec((QUERY_ROWS, LANES), lambda i, prior: (i, 0))
    wide = jax.ShapeDtypeStruct((seg_rows, LANES), jnp.float32)
    return pl.pallas_call(
        attend_back_own_kernel,
        grid_spec=pltpu.PrefetchScalarGridSpec(
            num_scalar_prefetch=1,
            grid=(seg_rows // QUERY_ROWS,),
            in_specs=[query_spec] * 5 + [VMEM] * 4 + [query_spec],
            out_specs=(query_spec, VMEM, VMEM),
            scratch_shapes=back_scratch(seg_rows),
        ),
        out_shape=(jax.ShapeDtypeStruct((seg_rows, LANES), jnp.bfloat16), wide, wide),
        compiler_params=pltpu.CompilerParams(vmem_limit_bytes=BIG_VMEM),
        cost_estimate=BRIEF,
        name="attend_back_own",
    )(prior, q_seg, grad_seg, *seen, keys, values, cosine, sine, dq_part)


def attend_back_halo_kernel(
    own_chunks, prior, q_seg, grad_seg, mixed, tops, sums, keys, values, cos_hbm, sin_hbm,
    dq_out, halves_out, *scratch
):
    k_turned, q_head, grad_head, dq_total, dk_total, dv_total, row_stats = scratch[:7]
    key_rows, value_rows, cosine, sine, dk_half, dv_half = scratch[7:13]
    q_rows, grad_rows, out_rows, top_rows, sum_rows, dq_rows, sems = scratch[13:]
    needed = needs_halo(prior, own_chunks)
    part = pl.ds(0, q_rows.shape[0])

    def one_block(block, unused):
        chunks_back = prior[HALO_CHUNKS + block]
        rows = chunk_rows(block, QUERY_ROWS)

        @pl.when(chunks_back > block)
        def _():
            prepare_back(
                (q_head, grad_head, row_stats), block, prior, q_rows[rows, :], grad_rows[rows, :],
                out_rows[rows, :], top_rows[rows, :], sum_rows[rows, :], cosine, sine,
            )
            dq_total[...] = jnp.zeros_like(dq_total)

            def whole(index, unused):
                add_keys_back(
                    (
                        q_head, grad_head, row_stats, k_turned, value_rows, dq_total, dk_total,
                        dv_total,
                    ),
                    index,
                    False,
                )
                return unused

            lax.fori_loop(HALO_CHUNKS + block - chunks_back, HALO_CHUNKS, whole, 0)
            dq_rows[rows, :] = by_head([dq_total[head] for head in range(HEADS_HELD)])

        return unused

    @pl.when(needed)
    def _():
        copy_in(
            (
                (keys, key_rows), (values, value_rows), (cos_hbm, cosine), (sin_hbm, sine),
                (q_seg.at[part], q_rows), (grad_seg.at[part], grad_rows),
                (mixed.at[part], out_rows), (tops.at[part], top_rows), (sums.at[part], sum_rows),
            ),
            sems,
        )
        rotate_keys(prior, 0, key_rows, cosine, sine, k_turned)
        dk_total[...] = jnp.zeros_like(dk_total)
        dv_total[...] = jnp.zeros_like(dv_total)
        lax.fori_loop(0, q_rows.shape[0] // QUERY_ROWS, one_block, 0)
        turn_keys_back(prior, 0, dk_total, dv_total, cosine, sine, dk_half, dv_half)
        copy_in(((dq_rows, dq_out.at[part]),), sems)

    @pl.when(jnp.logical_not(needed))
    def _():
        dk_half[...] = jnp.zeros_like(dk_half)
        dv_half[...] = jnp.zeros_like(dv_half)

    copy_in(((dk_half, halves_out.at[0]), (dv_half, halves_out.at[1])), sems)


def attend_back_halo(prior, q_seg, grad_seg, seen, keys, values, cosine, sine):
    seg_rows = q_seg.shape[0]
    part = (min(seg_rows, HALO), LANES)
    return pl.pallas_call(
        functools.partial(attend_back_halo_kernel, seg_rows // CHUNK),
        in_specs=[SMEM] + [ANY] * 9,
        out_specs=(ANY,) * 2,
        out_shape=(
            jax.ShapeDtypeStruct((seg_rows, LANES), jnp.float32),
            jax.ShapeDtypeStruct((2, HALO, LANES), jnp.bfloat16),
        ),
        scratch_shapes=back_scratch(HALO)
        + [
            pltpu.VMEM((HALO, LANES), jnp.bfloat16),
            pltpu.VMEM((HALO, LANES), jnp.bfloat16),
            pltpu.VMEM((LONGEST, LANES), jnp.float32),
            pltpu.VMEM((LONGEST, LANES), jnp.float32),
            pltpu.VMEM((HALO, LANES), jnp.bfloat16),
            pltpu.VMEM((HALO, LANES), jnp.bfloat16),
            pltpu.VMEM(part, jnp.bfloat16),
            pltpu.VMEM(part, jnp.bfloat16),
            pltpu.VMEM(part, jnp.bfloat16),
            pltpu.VMEM(part, jnp.float32),
            pltpu.VMEM(part, jnp.float32),
            pltpu.VMEM(part, jnp.float32),
            pltpu.SemaphoreType.DMA((9,)),
        ],
        compiler_params=pltpu.CompilerParams(vmem_limit_bytes=BIG_VMEM),
        cost_estimate=BRIEF,
        name="attend_back_halo",
    )(prior, q_seg, grad_seg, *seen, keys, values, cosine, sine)


def attention(plan, tables, q_seg, k_seg, v_seg):
    k_halo, v_halo = halo_of(plan, k_seg), halo_of(plan, v_seg)
    earlier = attend_own(tables[0], q_seg, k_seg, v_seg, *tables[1:])
    seen = attend_halo(tables[0], q_seg, k_halo, v_halo, *tables[1:], earlier)
    return seen[0], (q_seg, k_seg, v_seg, k_halo, v_halo, seen)


def attention_back(plan, tables, kept, grad_seg, waiting, late, beside=()):
    q_seg, k_seg, v_seg, k_halo, v_halo, seen = kept
    queries = (tables[0], q_seg, grad_seg, seen)
    dq_part, halves = attend_back_halo(*queries, k_halo, v_halo, *tables[1:])
    halos = halo_back(plan, halves)
    dq, dk_own, dv_own = attend_back_own(*queries, k_seg, v_seg, *tables[1:], dq_part)
    dq, waiting = lax.optimization_barrier((dq, waiting))
    dq, *final = collect(plan, (dq,), (), beside)
    dq, *halos = lax.optimization_barrier((dq, *halos))
    dkv, late = lax.optimization_barrier((collect(plan, (dk_own, dv_own), halos), late))
    return (dq, *dkv), waiting, late, *final


def rotary_tables():
    half = HEAD_DIM // 2
    lane = jnp.arange(LANES)
    frequency = jnp.exp(
        (lane % half).astype(jnp.float32) * (-2.0 * math.log(10000.0) / HEAD_DIM)
    )
    sign = jnp.where(lane % HEAD_DIM < half, -1.0, 1.0).astype(jnp.float32)
    step = 64
    fine = jnp.arange(step).astype(jnp.float32)[:, None] * frequency[None, :]
    coarse = jnp.arange(0, LONGEST, step).astype(jnp.float32)[:, None] * frequency[None, :]
    cos_fine, sin_fine, cos_coarse, sin_coarse = lax.optimization_barrier(
        (jnp.cos(fine), jnp.sin(fine), jnp.cos(coarse), jnp.sin(coarse))
    )
    cosine = cos_coarse[:, None] * cos_fine[None] - sin_coarse[:, None] * sin_fine[None]
    sine = sin_coarse[:, None] * cos_fine[None] + cos_coarse[:, None] * sin_fine[None]
    return (
        cosine.reshape(LONGEST, LANES),
        (sine * sign).reshape(LONGEST, LANES),
    )


def chunks_before(plan, lengths):
    segment, unused = plan.here()
    count = (HALO + plan.seg_rows) // CHUNK
    places = segment * plan.seg_rows - HALO + CHUNK * jnp.arange(count)
    ends = jnp.cumsum(lengths)
    passed = ends[None, :] <= places[:, None]
    opening = jnp.max(jnp.where(passed, ends[None, :], 0), axis=1)
    return jnp.clip((places - opening) // CHUNK, 0, HALO_CHUNKS).astype(jnp.int32)


def tied(array, *others):
    return lax.optimization_barrier((array, *others))[0]


def attention_pack(weights):
    return jnp.stack([weights[1].T, weights[2].T, weights[3].T, weights[4]])


def feedforward_pack(weights):
    return jnp.stack([weights[6].T, weights[7].T, weights[8]])


def fetch_mp(packs):
    rows = [pack.reshape(-1, pack.shape[-1]) for pack in packs]
    whole = rows[0] if len(rows) == 1 else jnp.concatenate(rows, axis=0)
    return lax.all_gather(whole, "mp", axis=0, tiled=False)


def fetch_dp(whole, first, pack):
    count, rows, width = pack.shape
    members = whole.shape[0]
    part = whole[:, first : first + count * rows].reshape(members, count, rows, width)
    part = part.transpose(1, 0, 2, 3).reshape(count, members * rows, width)
    return lax.all_gather(part, "dp", axis=2, tiled=True)


def turn_kernel(members, sizes, *refs):
    parts, out = refs[:-1], refs[-1]
    index, start, row = 0, 0, 0
    for size in sizes:
        if start == parts[index].shape[1]:
            index, start = index + 1, 0
        turned = parts[index][:, start : start + size].T
        count = size // members
        for member in range(members):
            out[member, row : row + count, :] = turned[member * count : (member + 1) * count, :]
        start += size
        row += count


def mp_blocks(plan, parts, sizes):
    rows = sum(sizes) // plan.m
    if parts[0].shape[0] == LANES:
        return pl.pallas_call(
            functools.partial(turn_kernel, plan.m, sizes),
            in_specs=[VMEM] * len(parts),
            out_specs=VMEM,
            out_shape=jax.ShapeDtypeStruct((plan.m, rows, LANES), jnp.bfloat16),
            compiler_params=pltpu.CompilerParams(vmem_limit_bytes=BIG_VMEM),
            cost_estimate=BRIEF,
            name="turn",
        )(*parts)
    turned, start, pieces = jnp.concatenate(parts, axis=1).T, 0, []
    for size in sizes:
        piece = turned[start : start + size]
        pieces.append(piece.reshape(plan.m, size // plan.m, turned.shape[1]))
        start += size
    return jnp.concatenate(pieces, axis=1)


def reduce_mp(plan, blocks, sizes):
    part = lax.psum_scatter(blocks, "mp", scatter_dimension=0, tiled=False).astype(jnp.float32)
    start, pieces = 0, []
    for size in sizes:
        pieces.append(part[start : start + size // plan.m])
        start += size // plan.m
    return pieces


def reduce_mp_beside(plan, blocks, sizes):
    me = lax.axis_index("mp")

    def block(distance):
        return lax.dynamic_index_in_dim(blocks, (me + distance) % plan.m, 0, keepdims=False)

    total = block(0).astype(jnp.float32)
    for distance in range(1, plan.m):
        route = [(i, (i + distance) % plan.m) for i in range(plan.m)]
        total = total + lax.ppermute(block(distance), "mp", route).astype(jnp.float32)
    start, pieces = 0, []
    for size in sizes:
        pieces.append(total[start : start + size // plan.m])
        start += size // plan.m
    return pieces


def reduce_qkv(plan, gradient, extra):
    gradient = jnp.concatenate([gradient, extra.astype(jnp.bfloat16)], axis=1)
    part = lax.psum_scatter(gradient, "dp", scatter_dimension=0, tiled=True)
    width = D // plan.m
    blocks = part[:, : 3 * D].reshape(-1, 3, plan.m, width).transpose(2, 0, 1, 3)
    blocks = blocks.reshape(plan.m, -1, 3 * width)
    shared = jnp.broadcast_to(part[None, :, 3 * D :], (plan.m, part.shape[0], LANES))
    blocks = jnp.concatenate([blocks, shared], axis=2)
    return lax.psum_scatter(blocks, "mp", scatter_dimension=0, tiled=False).astype(jnp.float32)


def project(normed, attention, first_values):
    query, key, fresh = (nt(normed, attention[part]) for part in range(3))
    if first_values is not None:
        fresh = 0.5 * fresh + 0.5 * first_values.astype(jnp.float32)
    return tuple(array.astype(jnp.bfloat16) for array in (query, key, fresh))


def feed_forward(middle, gain, feedforward):
    normed_ff = norm_rows(middle, gain).astype(jnp.bfloat16)
    gate = nt(normed_ff, feedforward[0])
    upward = nt(normed_ff, feedforward[1])
    hidden = (jax.nn.silu(gate) * upward).astype(jnp.bfloat16)
    return normed_ff, gate, upward, hidden


def feed_forward_back(grad_final, middle, gain, weights, stored):
    attention, feedforward = weights
    normed_ff, gate, upward, hidden = stored
    grad_bar = grad_final.astype(jnp.bfloat16)
    grad_hidden = nt(grad_bar, feedforward[2])
    gate_sigmoid = jax.nn.sigmoid(gate)
    grad_gate = (
        grad_hidden * upward * gate_sigmoid * (1.0 + gate * (1.0 - gate_sigmoid))
    ).astype(jnp.bfloat16)
    grad_up = (grad_hidden * gate * gate_sigmoid).astype(jnp.bfloat16)
    grad_normed_ff = nn(grad_gate, feedforward[0]) + nn(grad_up, feedforward[1])
    grad_norm, grad_gain = norm_back(middle, gain, grad_normed_ff)
    grad_middle = grad_final + grad_norm
    middle_bar = grad_middle.astype(jnp.bfloat16)
    grad_mixed = nt(middle_bar, attention[3]).astype(jnp.bfloat16)
    return grad_middle, grad_gain, grad_mixed, (grad_bar, grad_gate, grad_up, middle_bar)


def project_back(grad_middle, stream, gain, attention, dqkv):
    grad_normed = sum(nn(array, attention[part]) for part, array in enumerate(dqkv))
    grad_norm, grad_gain = norm_back(stream, gain, grad_normed)
    return grad_middle + grad_norm, grad_gain


def square_sum(values):
    widened = values.astype(jnp.float32)
    return jnp.sum(widened * widened)


def shards(n, m, inputs, lengths, *rest):
    plan = Plan(n, m)
    first, second, cotangent = rest[:9], rest[9:18], rest[18]
    cosine, sine = rotary_tables()
    tables = (chunks_before(plan, lengths), cosine, sine)
    by_hand = (n, m) == (8, 4)
    gain_shard = jnp.stack([first[0], first[5], second[0], second[5]])
    attention_packs = attention_pack(first), attention_pack(second)
    feedforward_packs = feedforward_pack(first), feedforward_pack(second)
    whole = fetch_mp(feedforward_packs[:1])
    if by_hand:
        gain_shard = jnp.pad(gain_shard, ((0, 12), (0, 0)))
        attention_one, gains = weave(plan, attention_packs[0], gain_shard)
        whole, cosine, sine = lax.optimization_barrier((whole, cosine, sine))
        whole = tied(whole, gains)
        tables = (tables[0], cosine, sine)
    else:
        gains = lax.all_gather(gain_shard, "dp", axis=1, tiled=True)
        attention_one = fetch_dp(fetch_mp(attention_packs[:1]), 0, attention_packs[0])
    feedforward_one = fetch_dp(whole, 0, feedforward_packs[0])
    gains = gains[:4].astype(jnp.float32)
    heads, hidden_rows = first[4].shape[0] * m, first[8].shape[0] * m
    rest_sizes = (hidden_rows, hidden_rows, hidden_rows, heads)

    stream = inputs.astype(jnp.float32)
    normed_one = norm_rows(stream, gains[0]).astype(jnp.bfloat16)
    qkv = project(normed_one, attention_one, None)
    values_one = qkv[2]
    q_seg, k_seg, v_seg = spread(plan, *qkv)
    packs_two = (attention_packs[1], feedforward_packs[1])
    feedforward_one, q_seg, packs_two = lax.optimization_barrier(
        (feedforward_one, q_seg, packs_two)
    )
    whole_two = fetch_mp(packs_two)
    out_seg, seen_one = attention(plan, tables, q_seg, k_seg, v_seg)
    out_seg, whole_two = lax.optimization_barrier((out_seg, whole_two))
    mixed_one = to_rows(plan, out_seg)
    attention_two = fetch_dp(whole_two, 0, packs_two[0])
    feedforward_two = fetch_dp(whole_two, 4 * packs_two[0].shape[1], packs_two[1])
    middle_one = stream + nn(mixed_one, attention_one[3])
    ff_one = feed_forward(middle_one, gains[1], feedforward_one)
    between = middle_one + nn(ff_one[3], feedforward_one[2])

    normed_two = norm_rows(between, gains[2]).astype(jnp.bfloat16)
    qkv = project(normed_two, attention_two, values_one)
    values_two = qkv[2]
    q_seg, k_seg, v_seg = spread(plan, *qkv)
    out_seg, seen_two = attention(plan, tables, q_seg, k_seg, v_seg)
    mixed_two = to_rows(plan, out_seg)
    middle_two = between + nn(mixed_two, attention_two[3])
    ff_two = feed_forward(middle_two, gains[3], feedforward_two)

    grad_middle, gain_ff_two, grad_mixed, (bar, grad_gate, grad_up, middle_bar) = feed_forward_back(
        cotangent.astype(jnp.float32), middle_two, gains[3], (attention_two, feedforward_two), ff_two
    )
    grad_seg, rest = products(
        plan,
        grad_mixed,
        (bar, ff_two[0], middle_bar),
        (ff_two[3], grad_gate, grad_up, mixed_two),
        (0, 1, 1, 2),
    )
    rest_two = lax.psum_scatter(rest, "dp", scatter_dimension=0, tiled=True)
    dqkv, unused, unused, final = attention_back(
        plan, tables, seen_two, grad_seg, (), (), (ff_two[3], feedforward_two, middle_two)
    )
    value_extra = 0.5 * dqkv[2].astype(jnp.float32)
    dqkv_two = (dqkv[0], dqkv[1], value_extra.astype(jnp.bfloat16))
    grad_between, gain_two = project_back(
        grad_middle, between, gains[2], attention_two, dqkv_two
    )

    qkv_two = tn(normed_two, jnp.concatenate(dqkv_two, axis=1)).astype(jnp.bfloat16)
    grad_between, qkv_two = lax.optimization_barrier((grad_between, qkv_two))
    qkv_two = lax.psum_scatter(qkv_two, "dp", scatter_dimension=0, tiled=True)
    grad_middle, gain_ff_one, grad_mixed, (bar, grad_gate, grad_up, middle_bar) = feed_forward_back(
        grad_between, middle_one, gains[1], (attention_one, feedforward_one), ff_one
    )
    grad_mixed, rest_two = lax.optimization_barrier((grad_mixed, rest_two))
    grad_seg, rest = products(
        plan,
        grad_mixed,
        (bar, ff_one[0], middle_bar),
        (ff_one[3], grad_gate, grad_up, mixed_one),
        (0, 1, 1, 2),
    )
    grad_seg, blocks, rest = lax.optimization_barrier(
        (grad_seg, mp_blocks(plan, (tied(rest_two, grad_seg),), rest_sizes), rest)
    )
    reduced_two = reduce_mp_beside(plan, blocks, rest_sizes)
    rest_one = lax.psum_scatter(rest, "dp", scatter_dimension=0, tiled=True)
    dqkv, qkv_two, reduced_two = attention_back(
        plan, tables, seen_one, grad_seg, qkv_two, reduced_two
    )
    grad_values = dqkv[2].astype(jnp.float32) + value_extra
    dqkv_one = (dqkv[0], dqkv[1], grad_values.astype(jnp.bfloat16))
    input_grad, gain_one = project_back(grad_middle, stream, gains[0], attention_one, dqkv_one)
    input_grad, rest_one = lax.optimization_barrier((input_grad, rest_one))
    sizes = rest_sizes + (heads,) * 3
    blocks, dqkv_one = lax.optimization_barrier(
        (mp_blocks(plan, (rest_one, qkv_two), sizes), dqkv_one)
    )
    down_one, gate_one, up_one, output_one, query_two, key_two, value_two = reduce_mp(
        plan, blocks, sizes
    )
    down_two, gate_two, up_two, output_two = reduced_two
    squares = [square_sum(values_one), square_sum(values_two)]
    width = D // n
    own_row = jnp.arange(D) == lax.axis_index("dp") * width
    squares = [jnp.where(own_row, square, 0.0) for square in squares]
    extra = jnp.stack([gain_one, gain_ff_one, gain_two, gain_ff_two, *squares], axis=1)
    extra = jnp.pad(extra, ((0, 0), (0, LANES - extra.shape[1])))
    if by_hand:
        part = shed(plan, normed_one, dqkv_one, extra)
    else:
        whole = [tn(normed_one, array).astype(jnp.bfloat16) for array in dqkv_one]
        part = reduce_qkv(plan, jnp.concatenate(whole, axis=1), extra)
    piece = D // m
    query_one, key_one, value_one = (part[:, i * piece : (i + 1) * piece] for i in range(3))
    shared = part[:, 3 * piece :]
    value_norms = jnp.sqrt(shared[:1, 4:6] / (TOK_DEV * D))
    return (
        between.astype(jnp.bfloat16),
        final,
        input_grad,
        shared[:, 0], query_one, key_one, value_one, output_one,
        shared[:, 1], gate_one.T, up_one.T, down_one,
        shared[:, 2], query_two.T, key_two.T, value_two.T, output_two,
        shared[:, 3], gate_two.T, up_two.T, down_two,
        value_norms,
    )


def solution(mesh):
    tokens, row_split, column_split = P(("dp", "mp"), None), P("dp", "mp"), P("mp", "dp")
    layer = (
        P("dp"), row_split, row_split, row_split, column_split, P("dp"), row_split, row_split,
        column_split,
    )
    return jax.shard_map(
        functools.partial(shards, mesh.shape["dp"], mesh.shape["mp"]),
        mesh=mesh,
        in_specs=(tokens, P(), *layer, *layer, tokens),
        out_specs=(tokens, tokens, tokens, *layer, *layer, P("dp", None)),
        check_vma=False,
    )
```
